256 devices in a mesh: own: 8 (over z), col: 8 (over x, core), mlp: 4 (over y).
Axes of the slice: x: 4, y: 4, z: 8, core: 2. Of those that a mesh axis runs over, the one named last changes fastest.
Arguments:
- features: bfloat16 [262144, 512], P(('own', 'col')), may hold values from -6 to 6
- nbr_page: int32 [8192, 32], P(('own', 'col')), may hold values from 0 to 262143, as said below
- nbr_weight: bfloat16 [8192, 32], P(('own', 'col')), may hold values from 0.0049743652 to 0.29882812
- labels: int32 [8192], P(('own', 'col')), may hold values from 0 to 255
- w_one: bfloat16 [512, 2048], P(None, 'mlp'), may hold values from -0.25 to 0.25
- w_two: bfloat16 [2048, 256], P('mlp'), may hold values from -0.125 to 0.125
Outputs:
- grad_one: float32 [512, 2048], P(None, 'mlp')
- grad_two: float32 [2048, 256], P('mlp')
The draws below stay inside these ranges and needn't reach their ends.
Inputs may be any that keep to these rules, and one draw needn't show every extreme that they name: `nbr_page`: page p is held by owner p // 4096 (owners numbered along own then col) at its row p % 4096. The 32 neighbours of a target are distinct pages listed in non-decreasing order of owner. Of the 4096 neighbour entries of the targets of one index of own and col, at most 128 fall on one owner; one owner receives exactly 128 entries from every index, and some owners receive none from some indices.
All inputs are finite; a program needn't handle non-finite values.
Results may differ from the reference program's by a relative error of at most 0.011.
Values may be sent and summed in bfloat16 or wider, within the bound.
No kernel may reach another device: no remote copies, remote signals or barrier semaphores. Data moves between devices by JAX's collectives and lax.ppermute only.
A program may use at most 128 MiB of HBM per device.

```python
import math
import jax
import jax.numpy as jnp
from jax import lax

F = 512
H = 2048
C = 256
K = 32
TGT_DEV = 128
ROWS_DEV = 4096
OWNERS = 64
PAGES = 262144
TARGETS = 8192
MEAN_LOAD = 64


STRIDES = (10007, 10009, 10037, 10039, 10061, 10067, 10069, 10079)


def draw_nbr_page(key, part):
    entries = TGT_DEV * K
    hot_key, order_key, offset_key, stride_key, mixing_key = jax.random.split(key, 5)
    hottest = jax.random.randint(hot_key, (), 0, OWNERS).astype(jnp.int32)

    def one_block(block_id):
        others = jax.random.permutation(jax.random.fold_in(order_key, block_id), OWNERS - 1).astype(jnp.int32)
        others = others + (others >= hottest).astype(jnp.int32)
        sequence = jnp.concatenate([hottest[None], others])
        rank_load = jnp.full((OWNERS,), MEAN_LOAD, jnp.int32)
        rank_load = rank_load.at[0].set(2 * MEAN_LOAD).at[1].set(0)
        rank_load = rank_load.at[2].set(MEAN_LOAD + MEAN_LOAD // 2).at[3].set(MEAN_LOAD // 2)
        owner_load = jnp.zeros((OWNERS,), jnp.int32).at[sequence].set(rank_load)
        load_end = jnp.cumsum(owner_load).astype(jnp.int32)
        starts = load_end - owner_load
        entry_ids = jnp.arange(entries, dtype=jnp.int32)
        owner_ids = jnp.searchsorted(load_end, entry_ids, side='right').astype(jnp.int32)
        within = entry_ids - starts[owner_ids]
        offset = jax.random.randint(jax.random.fold_in(offset_key, block_id), (OWNERS,), 0, ROWS_DEV).astype(jnp.int32)
        chosen = jax.random.randint(jax.random.fold_in(stride_key, block_id), (OWNERS,), 0, 8)
        stride = jnp.asarray(STRIDES, jnp.int32)[chosen]
        local_row = (offset[owner_ids] + within * stride[owner_ids]) % ROWS_DEV
        flat_pages = (owner_ids * ROWS_DEV + local_row).astype(jnp.int32)
        mixing = jax.random.permutation(jax.random.fold_in(mixing_key, block_id), entries).astype(jnp.int32)
        mixed = flat_pages[mixing].reshape(TGT_DEV, K)
        return jnp.sort(mixed, axis=1).astype(jnp.int32)
    page_ids = lax.map(one_block, jnp.arange(OWNERS, dtype=jnp.int32))
    return page_ids.reshape(TARGETS, K).astype(jnp.int32)


def with_ends(drawn, stream_key, low, top_value):
    longest = drawn.shape.index(max(drawn.shape))
    spots = []
    for shift in (0, 1):
        where = [jax.random.randint(jax.random.fold_in(stream_key, axis), (), 0, length) for axis, length in enumerate(drawn.shape)]
        where[longest] = (where[longest] + shift) % drawn.shape[longest]
        spots.append(tuple(where))
    return drawn.at[spots[0]].set(low).at[spots[1]].set(top_value)


def block_levels(key, shape, cuts, low, high):
    loudness = 1.0
    for axis_at, shards_of in cuts:
        draws = jax.random.uniform(jax.random.fold_in(jax.random.fold_in(key, 6), axis_at), (shards_of,), jnp.float32, low / len(cuts), high / len(cuts))
        loudness = loudness * jnp.repeat(jnp.exp(draws), shape[axis_at] // shards_of).reshape((-1,) + (1,) * (len(shape) - 1 - axis_at))
    return loudness


def gaussian(own_key, shape, scale, bound, cuts=(), kind=jnp.bfloat16):
    loudness = block_levels(own_key, shape, cuts, -0.22, 0.18) if cuts else 1.0
    array = jax.random.normal(own_key, shape, jnp.float32) * scale * loudness
    return jnp.minimum(jnp.maximum(array, -bound), bound).astype(kind)


def setup_inputs(seed: int = 0) -> dict:
    key_list = jax.random.split(jax.random.key(seed), 7)
    return {
        "features": gaussian(key_list[0], (PAGES, F), 1.0, 6.0, ((0, 64),)),
        "nbr_page": draw_nbr_page(jax.random.fold_in(key_list[6], 71), 0),
        "nbr_weight": jnp.clip(jnp.exp(math.log(0.29882812) - 4.095571 * jax.random.uniform(key_list[2], (TARGETS, K), jnp.float32) ** block_levels(key_list[2], (TARGETS, K), ((0, 64),), -0.2, 0.2)), 0.0049743652, 0.29882812).astype(jnp.bfloat16),
        "labels": with_ends(jax.random.randint(key_list[3], (TARGETS,), 0, C), jax.random.fold_in(key_list[3], 1), 0, C - 1).astype(jnp.int32),
        "w_one": gaussian(key_list[4], (F, H), F ** -0.5, 0.25, ((1, 4),)),
        "w_two": gaussian(key_list[5], (H, C), H ** -0.5, 0.125, ((0, 4),)),
    }


def reference(features, nbr_page, nbr_weight, labels, w_one, w_two):
    pages_in = nbr_page.reshape(OWNERS, TGT_DEV, K)
    weights_in = nbr_weight.reshape(OWNERS, TGT_DEV, K)
    labels_in = labels.reshape(OWNERS, TGT_DEV)

    def one_block(totals, block_in):
        page_ids, weight_in, label_ids = block_in
        row_feats = features[page_ids.reshape(-1)]
        pre_act = jnp.dot(row_feats, w_one, preferred_element_type=jnp.float32)
        active = jnp.maximum(pre_act, 0.0).astype(jnp.bfloat16)
        hidden = jnp.einsum("tk,tkh->th", weight_in.astype(jnp.float32),
                            active.reshape(TGT_DEV, K, H).astype(jnp.float32)).astype(jnp.bfloat16)
        logits = jnp.dot(hidden, w_two, preferred_element_type=jnp.float32)
        exponent = jnp.exp(logits)
        probability = exponent / jnp.sum(exponent, axis=1, keepdims=True)
        onehot_label = (label_ids[:, None] == jnp.arange(C, dtype=jnp.int32)[None, :]).astype(jnp.float32)
        d_logits = (probability - onehot_label).astype(jnp.bfloat16)
        grad_two = jnp.dot(hidden.T, d_logits, preferred_element_type=jnp.float32)
        d_hidden = jnp.dot(d_logits, w_two.T, preferred_element_type=jnp.float32).astype(jnp.bfloat16)
        scaled = weight_in.astype(jnp.float32)[:, :, None] * d_hidden.astype(jnp.float32)[:, None, :]
        positive = (pre_act > 0).astype(jnp.float32)
        d_pre = (scaled.reshape(TGT_DEV * K, H) * positive).astype(jnp.bfloat16)
        grad_one = jnp.dot(row_feats.T, d_pre, preferred_element_type=jnp.float32)
        return (totals[0] + grad_one, totals[1] + grad_two), None

    start = (jnp.zeros((F, H), jnp.float32), jnp.zeros((H, C), jnp.float32))
    totals, unused = lax.scan(one_block, start, (pages_in, weights_in, labels_in))
    return (totals[0], totals[1])
```

```python
import jax
import jax.numpy as jnp
from jax import lax
from jax.sharding import PartitionSpec as P

BF = jnp.bfloat16
F32 = jnp.float32


def dot(a, b, ca=1, cb=0):
    return lax.dot_general(a, b, (((ca,), (cb,)), ((), ())), preferred_element_type=F32)


def exchange(x, axes, groups=None):
    return lax.all_to_all(
        x, axes, split_axis=0, concat_axis=0, tiled=True, axis_index_groups=groups
    )


def body(features, nbr_page, nbr_weight, labels, w_one, w_two):
    rows_dev, width_f = features.shape
    targets, width_k = nbr_page.shape
    own_n, col_n, mlp_n = (lax.axis_size(a) for a in ("own", "col", "mlp"))
    owners = own_n * col_n
    entries = targets * width_k
    capacity = 2 * entries // owners
    share = capacity // mlp_n
    quarter = targets // mlp_n
    units, classes = w_two.shape
    me = lax.axis_index("mlp")
    core = lax.axis_index("col") % 2

    w_one_all = lax.all_gather(w_one, "mlp")
    w_two_all = lax.all_gather(w_two, "mlp", tiled=True)

    owner_range = jnp.arange(owners, dtype=jnp.int32)
    owner_ids = nbr_page // rows_dev
    local_row = nbr_page % rows_dev
    matches = owner_ids[:, :, None] == owner_range[None, None, :]
    row_count = jnp.sum(matches.astype(F32), axis=1)
    t_range = jnp.arange(targets)
    earlier = dot((t_range[:, None] > t_range[None, :]).astype(BF), row_count.astype(BF))
    before = dot(row_count.astype(BF), (owner_range[:, None] < owner_range[None, :]).astype(BF))
    first_slot = earlier - before
    slot_ids = (
        jnp.sum(matches.astype(F32) * first_slot[:, None, :], axis=2).astype(jnp.int32)
        + jnp.arange(width_k, dtype=jnp.int32)[None, :]
    )
    by_owner = matches.astype(BF).reshape(entries, owners)
    in_slot = slot_ids[:, :, None] == jnp.arange(capacity, dtype=jnp.int32)[None, None, :]

    def place(values):
        spread_out = jnp.where(in_slot, values.astype(BF)[:, :, None], jnp.zeros((), BF))
        return dot(by_owner, spread_out.reshape(entries, capacity), 0, 0)

    requests = (place(local_row // 64) * 64.0 + place(local_row % 64)).astype(jnp.int32)
    slot_weight = place(nbr_weight)
    slot_target = place(jnp.broadcast_to(t_range[:, None], (targets, width_k)))

    asked = exchange(requests, ("own", "col"))
    asked = lax.dynamic_slice_in_dim(asked, me * share, share, 1)
    fetched = features[asked]
    received = exchange(fetched, ("own", "col")).reshape(owners * share, width_f)

    my_weight = lax.dynamic_slice_in_dim(slot_weight, me * share, share, 1).reshape(1, -1)
    my_target = lax.dynamic_slice_in_dim(slot_target, me * share, share, 1).reshape(1, -1)
    spread = jnp.where(
        my_target.astype(jnp.int32) == t_range[:, None].astype(jnp.int32), my_weight, 0.0
    ).astype(BF)

    active = [
        jnp.maximum(dot(received, w_one_all[j]), 0.0).astype(BF) for j in range(mlp_n)
    ]
    partial_hidden = jnp.concatenate([dot(spread, a).astype(BF) for a in active], axis=1)
    parts = exchange(partial_hidden.reshape(mlp_n, quarter, mlp_n * units), "mlp")
    hidden = jnp.sum(parts.astype(F32), axis=0).astype(BF)
    logits = dot(hidden, w_two_all)
    exponent = jnp.exp(logits)
    probability = exponent / jnp.sum(exponent, axis=1, keepdims=True)
    my_labels = lax.dynamic_slice_in_dim(labels, me * quarter, quarter, 0)
    onehot = (my_labels[:, None] == jnp.arange(classes, dtype=jnp.int32)[None, :]).astype(F32)
    d_logits = (probability - onehot).astype(BF)
    send = jnp.stack(
        [
            jnp.concatenate([hidden[:, j * units : (j + 1) * units], d_logits], axis=1)
            for j in range(mlp_n)
        ]
    )
    got = exchange(send, "mlp").reshape(targets, units + classes)
    hidden_all = got[:, :units]
    d_logits_all = got[:, units:]

    grad_two = dot(hidden_all, d_logits_all, 0, 0)
    d_hidden = dot(d_logits_all, w_two_all, 1, 1).astype(BF)
    grads = []
    for j in range(mlp_n):
        scattered = dot(spread, d_hidden[:, j * units : (j + 1) * units], 0, 0)
        d_pre = jnp.where(active[j] > 0, scattered, 0.0).astype(BF)
        grads.append(dot(received, d_pre, 0, 0))
    grad_one = jnp.stack(grads)

    half = width_f // 2
    pairs = [(i, i ^ 1) for i in range(col_n)]

    def halves(x, axis):
        size = x.shape[axis] // 2
        mine = lax.dynamic_slice_in_dim(x, core * size, size, axis)
        other = lax.dynamic_slice_in_dim(x, (1 - core) * size, size, axis).astype(BF)
        return mine + lax.ppermute(other, "col", pairs).astype(F32)

    grad_one = halves(grad_one, 1).astype(BF)
    grad_two = halves(grad_two, 0)
    grad_one = jnp.sum(exchange(grad_one, "mlp").reshape(mlp_n, half, units).astype(F32), axis=0)
    both = jnp.concatenate([grad_one, grad_two], axis=1).astype(BF)
    chips = owners // 2
    groups = [[2 * i + c for i in range(chips)] for c in (0, 1)]
    width = units + classes
    both = exchange(both.reshape(chips, half // chips, width), ("own", "col"), groups)
    both = jnp.sum(both.astype(F32), axis=0).astype(BF)
    both = jnp.broadcast_to(both[None], (chips, half // chips, width))
    both = exchange(both, ("own", "col"), groups).reshape(half, width)
    other = lax.ppermute(both, "col", pairs)
    low = jnp.where(core == 0, both, other)
    high = jnp.where(core == 0, other, both)
    both = jnp.concatenate([low, high], axis=0).astype(F32)
    return both[:, :units], both[:, units:]


def solution(mesh):
    placed = (
        P(("own", "col"), None),
        P(("own", "col"), None),
        P(("own", "col"), None),
        P(("own", "col")),
        P(None, "mlp"),
        P("mlp", None),
    )
    return jax.shard_map(
        body,
        mesh=mesh,
        in_specs=placed,
        out_specs=(P(None, "mlp"), P("mlp", None)),
        check_vma=False,
    )
```

```python
import jax
import jax.numpy as jnp
from jax import lax
from jax.sharding import PartitionSpec as P

BF = jnp.bfloat16
F32 = jnp.float32


def dot(a, b, ca=1, cb=0):
    return lax.dot_general(a, b, (((ca,), (cb,)), ((), ())), preferred_element_type=F32)


def exchange(x, axes, groups=None):
    return lax.all_to_all(
        x, axes, split_axis=0, concat_axis=0, tiled=True, axis_index_groups=groups
    )


def body(features, nbr_page, nbr_weight, labels, w_one, w_two):
    rows_dev, width_f = features.shape
    targets, width_k = nbr_page.shape
    own_n, col_n, mlp_n = (lax.axis_size(a) for a in ("own", "col", "mlp"))
    owners = own_n * col_n
    entries = targets * width_k
    capacity = 2 * entries // owners
    share = capacity // mlp_n
    units, classes = w_two.shape
    me = lax.axis_index("mlp")
    core = lax.axis_index("col") % 2

    def to_mlp(x, step):
        return lax.ppermute(x, "mlp", [(j, (j + step) % mlp_n) for j in range(mlp_n)])

    steps = (2, 1, 3, 0)
    w_both = jnp.concatenate([w_one, w_two], axis=1)
    w_ones, w_twos = {0: w_one}, {0: w_two}
    for step in steps[:-1]:
        w_got = to_mlp(w_both, -step)
        w_ones[step], w_twos[step] = w_got[:, :units], w_got[:, units:]

    owner_range = jnp.arange(owners, dtype=jnp.int32)
    owner_ids = nbr_page // rows_dev
    local_row = nbr_page % rows_dev
    matches = owner_ids[:, :, None] == owner_range[None, None, :]
    row_count = jnp.sum(matches.astype(F32), axis=1)
    t_range = jnp.arange(targets)
    earlier = dot((t_range[:, None] > t_range[None, :]).astype(BF), row_count.astype(BF))
    before = dot(row_count.astype(BF), (owner_range[:, None] < owner_range[None, :]).astype(BF))
    first_slot = earlier - before
    slot_ids = (
        jnp.sum(matches.astype(F32) * first_slot[:, None, :], axis=2).astype(jnp.int32)
        + jnp.arange(width_k, dtype=jnp.int32)[None, :]
    )
    by_owner = matches.astype(BF).reshape(entries, owners)
    in_slot = slot_ids[:, :, None] == jnp.arange(capacity, dtype=jnp.int32)[None, None, :]

    def place(values):
        spread_out = jnp.where(in_slot, values.astype(BF)[:, :, None], jnp.zeros((), BF))
        return dot(by_owner, spread_out.reshape(entries, capacity), 0, 0)

    requests = (place(local_row // 64) * 64.0 + place(local_row % 64)).astype(jnp.int32)
    slot_weight = place(nbr_weight)
    slot_target = place(jnp.broadcast_to(t_range[:, None], (targets, width_k)))

    asked = exchange(requests, ("own", "col"))
    asked = lax.dynamic_slice_in_dim(asked, me * share, share, 1)
    fetched = features[asked]
    received = exchange(fetched, ("own", "col")).reshape(owners * share, width_f)

    my_weight = lax.dynamic_slice_in_dim(slot_weight, me * share, share, 1).reshape(1, -1)
    my_target = lax.dynamic_slice_in_dim(slot_target, me * share, share, 1).reshape(1, -1)
    spread = jnp.where(
        my_target.astype(jnp.int32) == t_range[:, None].astype(jnp.int32), my_weight, 0.0
    ).astype(BF)
    spread, spread_t = lax.optimization_barrier((spread, spread.T))

    active, hidden = {}, 0.0
    for step in steps:
        active[step] = lax.optimization_barrier(
            jnp.maximum(dot(received, w_ones[step]), 0.0).astype(BF)
        )
        part = dot(spread, active[step])
        hidden += to_mlp(part.astype(BF), step).astype(F32) if step else part
    hidden = hidden.astype(BF)
    half = width_f // 2
    own_half = jnp.where(core == 0, received[:, :half], received[:, half:])
    other_half = jnp.where(core == 0, received[:, half:], received[:, :half])
    own_half, other_half = lax.optimization_barrier((own_half.T, other_half.T))

    part = dot(hidden, w_two)
    logits = part
    for step in steps[:-1]:
        logits += to_mlp(part, step)
    exponent = jnp.exp(logits)
    probability = exponent / jnp.sum(exponent, axis=1, keepdims=True)
    onehot = (labels[:, None] == jnp.arange(classes, dtype=jnp.int32)[None, :]).astype(F32)
    d_logits = (probability - onehot).astype(BF)

    pairs = [(i, i ^ 1) for i in range(col_n)]

    def partner(x):
        return lax.ppermute(x, "col", pairs)

    grad_two = dot(hidden, d_logits, 0, 0)
    mine = lax.dynamic_slice_in_dim(grad_two, core * (units // 2), units // 2, 0)
    other = lax.dynamic_slice_in_dim(grad_two, (1 - core) * (units // 2), units // 2, 0)
    grad_two = mine + partner(other.astype(BF)).astype(F32)
    grad_one = 0.0
    for step in steps:
        d_hidden = dot(d_logits, w_twos[step], 1, 1).astype(BF)
        d_pre = jnp.where(active[step] > 0, dot(spread_t, d_hidden), 0.0).astype(BF)
        d_pre = lax.optimization_barrier(d_pre)
        other = partner(dot(other_half, d_pre).astype(BF))
        mine = dot(own_half, d_pre) + other.astype(F32)
        grad_one += to_mlp(mine.astype(BF), step).astype(F32) if step else mine
    both = jnp.concatenate([grad_one, grad_two], axis=1).astype(BF)
    chips = owners // 2
    groups = [[2 * i + c for i in range(chips)] for c in (0, 1)]
    width = units + classes
    both = exchange(both.reshape(chips, half // chips, width), ("own", "col"), groups)
    both = jnp.sum(both.astype(F32), axis=0).astype(BF)
    both = jnp.broadcast_to(both[None], (chips, half // chips, width))
    both = exchange(both, ("own", "col"), groups).reshape(half, width)
    other = partner(both)
    low = jnp.where(core == 0, both, other)
    high = jnp.where(core == 0, other, both)
    both = jnp.concatenate([low, high], axis=0).astype(F32)
    return both[:, :units], both[:, units:]


def solution(mesh):
    placed = (
        P(("own", "col"), None),
        P(("own", "col"), None),
        P(("own", "col"), None),
        P(("own", "col")),
        P(None, "mlp"),
        P("mlp", None),
    )
    return jax.shard_map(
        body,
        mesh=mesh,
        in_specs=placed,
        out_specs=(P(None, "mlp"), P("mlp", None)),
        check_vma=False,
    )
```

```python
import jax
import jax.numpy as jnp
from jax import lax
from jax.experimental import pallas as pl
from jax.experimental.pallas import tpu as pltpu
from jax.sharding import PartitionSpec as P

BF = jnp.bfloat16
F32 = jnp.float32


def dot(a, b, ca=1, cb=0):
    return lax.dot_general(a, b, (((ca,), (cb,)), ((), ())), preferred_element_type=F32)


def exchange(x, axes, groups=None):
    return lax.all_to_all(
        x, axes, split_axis=0, concat_axis=0, tiled=True, axis_index_groups=groups
    )


def middle(parts, labels, hidden, w_twos, core):
    count = len(parts)
    targets, classes = parts[0].shape
    units = hidden.shape[1]
    half = units // 2

    def kernel(core_ref, *refs):
        part_refs, refs = refs[:count], refs[count:]
        labels_ref, hidden_ref = refs[:2]
        w_refs, refs = refs[2 : 2 + count], refs[2 + count :]
        own_ref, other_ref = refs[:2]
        d_hidden_refs = refs[2:]
        logits = part_refs[0][...]
        for part in part_refs[1:]:
            logits += part[...]
        exponent = jnp.exp(logits)
        probability = exponent / jnp.sum(exponent, axis=1, keepdims=True)
        ids = lax.broadcasted_iota(jnp.int32, (targets, classes), 1)
        onehot = (labels_ref[...] == ids).astype(F32)
        d_logits = (probability - onehot).astype(BF)
        for w_ref, out in zip(w_refs, d_hidden_refs):
            out[...] = dot(d_logits, w_ref[...], 1, 1).astype(BF)
        both = dot(hidden_ref[...], d_logits, 0, 0)
        swap = core_ref[0] != 0
        low, high = both[:half], both[half:]
        own_ref[...] = jnp.where(swap, high, low)
        other_ref[...] = jnp.where(swap, low, high).astype(BF)

    vmem = pl.BlockSpec(memory_space=pltpu.VMEM)
    return pl.pallas_call(
        kernel,
        out_shape=[
            jax.ShapeDtypeStruct((half, classes), F32),
            jax.ShapeDtypeStruct((half, classes), BF),
        ]
        + [jax.ShapeDtypeStruct((targets, units), BF)] * count,
        in_specs=[pl.BlockSpec(memory_space=pltpu.SMEM)] + [vmem] * (2 * count + 2),
        out_specs=[vmem] * (2 + count),
        compiler_params=pltpu.CompilerParams(vmem_limit_bytes=24 * 2**20),
        cost_estimate=pl.CostEstimate(
            flops=2 * targets * classes * units * (count + 1),
            bytes_accessed=4 * 2**20,
            transcendentals=targets * classes,
        ),
    )(core, *parts, labels, hidden, *w_twos)


def backward(spread_t, d_hidden, active, rows_t):
    slots, targets = spread_t.shape
    units = d_hidden.shape[1]
    width_f = rows_t.shape[0]
    half = width_f // 2
    block = 512
    steps = slots // block

    def kernel(spread_ref, d_hidden_ref, active_ref, rows_ref, own_ref, other_ref, total):
        step = pl.program_id(0)
        scattered = dot(spread_ref[...], d_hidden_ref[...]).astype(BF)
        d_pre = jnp.where(active_ref[...] > 0, scattered, jnp.zeros_like(scattered))
        term = dot(rows_ref[...], d_pre)

        @pl.when(step == 0)
        def _():
            total[...] = term

        @pl.when(step > 0)
        def _():
            total[...] += term

        @pl.when(step == steps - 1)
        def _():
            own_ref[...] = total[:half]
            other_ref[...] = total[half:].astype(BF)

    return pl.pallas_call(
        kernel,
        out_shape=[
            jax.ShapeDtypeStruct((half, units), F32),
            jax.ShapeDtypeStruct((half, units), BF),
        ],
        grid=(steps,),
        in_specs=[
            pl.BlockSpec((block, targets), lambda i: (i, 0)),
            pl.BlockSpec((targets, units), lambda i: (0, 0)),
            pl.BlockSpec((block, units), lambda i: (i, 0)),
            pl.BlockSpec((width_f, block), lambda i: (0, i)),
        ],
        out_specs=[
            pl.BlockSpec((half, units), lambda i: (0, 0)),
            pl.BlockSpec((half, units), lambda i: (0, 0)),
        ],
        scratch_shapes=[pltpu.VMEM((width_f, units), F32)],
        compiler_params=pltpu.CompilerParams(vmem_limit_bytes=24 * 2**20),
        cost_estimate=pl.CostEstimate(
            flops=2 * slots * units * (width_f + 2 * targets),
            bytes_accessed=2 * slots * (width_f + units + targets),
            transcendentals=0,
        ),
    )(spread_t, d_hidden, active, rows_t)


def body(features, nbr_page, nbr_weight, labels, w_one, w_two):
    rows_dev, width_f = features.shape
    targets, width_k = nbr_page.shape
    own_n, col_n, mlp_n = (lax.axis_size(a) for a in ("own", "col", "mlp"))
    owners = own_n * col_n
    entries = targets * width_k
    capacity = 2 * entries // owners
    share = capacity // mlp_n
    units, classes = w_two.shape
    me = lax.axis_index("mlp")
    core = lax.axis_index("col") % 2

    def to_mlp(x, step):
        return lax.ppermute(x, "mlp", [(j, (j + step) % mlp_n) for j in range(mlp_n)])

    steps = (2, 1, 3, 0)
    w_both = jnp.concatenate([w_one, w_two], axis=1)
    w_ones, w_twos = {0: w_one}, {0: w_two}
    for step in steps[:-1]:
        w_got = to_mlp(w_both, -step)
        w_ones[step], w_twos[step] = w_got[:, :units], w_got[:, units:]

    owner_range = jnp.arange(owners, dtype=jnp.int32)
    owner_ids = nbr_page // rows_dev
    local_row = nbr_page % rows_dev
    matches = owner_ids[:, :, None] == owner_range[None, None, :]
    row_count = jnp.sum(matches.astype(F32), axis=1)
    t_range = jnp.arange(targets)
    earlier = dot((t_range[:, None] > t_range[None, :]).astype(BF), row_count.astype(BF))
    before = dot(row_count.astype(BF), (owner_range[:, None] < owner_range[None, :]).astype(BF))
    first_slot = earlier - before
    slot_ids = (
        jnp.sum(matches.astype(F32) * first_slot[:, None, :], axis=2).astype(jnp.int32)
        + jnp.arange(width_k, dtype=jnp.int32)[None, :]
    )
    by_owner = matches.astype(BF).reshape(entries, owners)
    in_slot = slot_ids[:, :, None] == jnp.arange(capacity, dtype=jnp.int32)[None, None, :]

    def place(values):
        spread_out = jnp.where(in_slot, values.astype(BF)[:, :, None], jnp.zeros((), BF))
        return dot(by_owner, spread_out.reshape(entries, capacity), 0, 0)

    requests = (place(local_row // 64) * 64.0 + place(local_row % 64)).astype(jnp.int32)
    slot_weight = place(nbr_weight)
    slot_target = place(jnp.broadcast_to(t_range[:, None], (targets, width_k)))

    asked = exchange(requests, ("own", "col"))
    asked = lax.dynamic_slice_in_dim(asked, me * share, share, 1)
    fetched = features[asked]
    received = exchange(fetched, ("own", "col")).reshape(owners * share, width_f)

    my_weight = lax.dynamic_slice_in_dim(slot_weight, me * share, share, 1).reshape(1, -1)
    my_target = lax.dynamic_slice_in_dim(slot_target, me * share, share, 1).reshape(1, -1)
    spread = jnp.where(
        my_target.astype(jnp.int32) == t_range[:, None].astype(jnp.int32), my_weight, 0.0
    ).astype(BF)
    spread, spread_t = lax.optimization_barrier((spread, spread.T))

    active, hidden = {}, 0.0
    for step in steps:
        active[step] = lax.optimization_barrier(
            jnp.maximum(dot(received, w_ones[step]), 0.0).astype(BF)
        )
        part = dot(spread, active[step])
        hidden += to_mlp(part.astype(BF), step).astype(F32) if step else part
    hidden = hidden.astype(BF)
    half = width_f // 2
    own_half = jnp.where(core == 0, received[:, :half], received[:, half:])
    other_half = jnp.where(core == 0, received[:, half:], received[:, :half])
    rows_t = jnp.concatenate([own_half, other_half], axis=1).T

    part = dot(hidden, w_two)
    parts = [part] + [to_mlp(part, step) for step in steps[:-1]]

    pairs = [(i, i ^ 1) for i in range(col_n)]

    def partner(x):
        return lax.ppermute(x, "col", pairs)

    mine, other, *d_hidden = middle(
        parts, labels[:, None], hidden, [w_twos[s] for s in steps], core.reshape(1)
    )
    grad_two = mine + partner(other).astype(F32)
    grad_one = 0.0
    for step, d_slice in zip(steps, d_hidden):
        mine, other = backward(spread_t, d_slice, active[step], rows_t)
        mine += partner(other).astype(F32)
        grad_one += to_mlp(mine.astype(BF), step).astype(F32) if step else mine
    both = jnp.concatenate([grad_one, grad_two], axis=1).astype(BF)
    chips = owners // 2
    groups = [[2 * i + c for i in range(chips)] for c in (0, 1)]
    width = units + classes
    both = exchange(both.reshape(chips, half // chips, width), ("own", "col"), groups)
    both = jnp.sum(both.astype(F32), axis=0).astype(BF)
    both = jnp.broadcast_to(both[None], (chips, half // chips, width))
    both = exchange(both, ("own", "col"), groups).reshape(half, width)
    other = partner(both)
    low = jnp.where(core == 0, both, other)
    high = jnp.where(core == 0, other, both)
    both = jnp.concatenate([low, high], axis=0).astype(F32)
    return both[:, :units], both[:, units:]


def solution(mesh):
    placed = (
        P(("own", "col"), None),
        P(("own", "col"), None),
        P(("own", "col"), None),
        P(("own", "col")),
        P(None, "mlp"),
        P("mlp", None),
    )
    return jax.shard_map(
        body,
        mesh=mesh,
        in_specs=placed,
        out_specs=(P(None, "mlp"), P("mlp", None)),
        check_vma=False,
    )
```

```python
import jax
import jax.numpy as jnp
from jax import lax
from jax.experimental import pallas as pl
from jax.experimental.pallas import tpu as pltpu
from jax.sharding import PartitionSpec as P

BF = jnp.bfloat16
F32 = jnp.float32


def dot(a, b, ca=1, cb=0):
    return lax.dot_general(a, b, (((ca,), (cb,)), ((), ())), preferred_element_type=F32)


def exchange(x, axes, groups=None):
    return lax.all_to_all(
        x, axes, split_axis=0, concat_axis=0, tiled=True, axis_index_groups=groups
    )


def middle(parts, labels, hidden, w_boths, core):
    count = len(parts)
    targets, classes = parts[0].shape
    units = hidden.shape[1]
    half = units // 2

    def kernel(core_ref, *refs):
        part_refs, refs = refs[:count], refs[count:]
        labels_ref, hidden_ref = refs[:2]
        w_refs, refs = refs[2 : 2 + count], refs[2 + count :]
        own_ref, other_ref = refs[:2]
        d_hidden_refs = refs[2:]
        logits = part_refs[0][...]
        for part in part_refs[1:]:
            logits += part[...]
        exponent = jnp.exp(logits)
        probability = exponent / jnp.sum(exponent, axis=1, keepdims=True)
        ids = lax.broadcasted_iota(jnp.int32, (targets, classes), 1)
        onehot = (labels_ref[...] == ids).astype(F32)
        d_logits = (probability - onehot).astype(BF)
        for w_ref, out in zip(w_refs, d_hidden_refs):
            out[...] = dot(d_logits, w_ref[:, units:], 1, 1).astype(BF)
        both = dot(hidden_ref[...], d_logits, 0, 0)
        swap = core_ref[0] != 0
        low, high = both[:half], both[half:]
        own_ref[...] = jnp.where(swap, high, low)
        other_ref[...] = jnp.where(swap, low, high).astype(BF)

    vmem = pl.BlockSpec(memory_space=pltpu.VMEM)
    return pl.pallas_call(
        kernel,
        out_shape=[
            jax.ShapeDtypeStruct((half, classes), F32),
            jax.ShapeDtypeStruct((half, classes), BF),
        ]
        + [jax.ShapeDtypeStruct((targets, units), BF)] * count,
        in_specs=[pl.BlockSpec(memory_space=pltpu.SMEM)] + [vmem] * (2 * count + 2),
        out_specs=[vmem] * (2 + count),
        compiler_params=pltpu.CompilerParams(vmem_limit_bytes=24 * 2**20),
        cost_estimate=pl.CostEstimate(
            flops=2 * targets * classes * units * (count + 1),
            bytes_accessed=4 * 2**20,
            transcendentals=targets * classes,
        ),
    )(core, *parts, labels, hidden, *w_boths)


VMEM = pl.BlockSpec(memory_space=pltpu.VMEM)
SMEM = pl.BlockSpec(memory_space=pltpu.SMEM)


def forward(rows, w_both, spread, core, out_type, turn):
    slots, width_f = rows.shape
    targets = spread.shape[0]
    units = width_f
    half = width_f // 2
    block = 512

    def kernel(core_ref, rows_ref, w_ref, spread_ref, active_ref, hidden_ref, *turned):
        mine = pl.multiple_of(core_ref[0] * half, half)
        other = pl.multiple_of((1 - core_ref[0]) * half, half)

        @pl.loop(0, slots // block)
        def _(i):
            at = pl.ds(pl.multiple_of(i * block, block), block)
            value = rows_ref[at, :]
            active_ref[at, :] = jnp.maximum(dot(value, w_ref[:, :units]), 0.0).astype(BF)
            for ref in turned:
                flat = value.T
                ref[pl.ds(mine, half), at] = flat[:half]
                ref[pl.ds(other, half), at] = flat[half:]

        hidden_ref[...] = dot(spread_ref[...], active_ref[...]).astype(out_type)

    shapes = [
        jax.ShapeDtypeStruct((slots, units), BF),
        jax.ShapeDtypeStruct((targets, units), out_type),
    ] + [jax.ShapeDtypeStruct((width_f, slots), BF)] * turn
    return pl.pallas_call(
        kernel,
        out_shape=shapes,
        in_specs=[SMEM] + [VMEM] * 3,
        out_specs=[VMEM] * len(shapes),
        compiler_params=pltpu.CompilerParams(vmem_limit_bytes=24 * 2**20),
        cost_estimate=pl.CostEstimate(
            flops=2 * slots * units * (width_f + targets),
            bytes_accessed=2 * slots * (width_f + units + targets),
            transcendentals=0,
        ),
    )(core, rows, w_both, spread)


def backward(spread_t, d_hidden, active, rows_t):
    slots, targets = spread_t.shape
    units = d_hidden.shape[1]
    width_f = rows_t.shape[0]
    half = width_f // 2
    block = 256

    def kernel(spread_ref, d_hidden_ref, active_ref, rows_ref, own_ref, other_ref):
        @pl.loop(0, units // block)
        def _(i):
            at = pl.ds(pl.multiple_of(i * block, block), block)
            scattered = dot(spread_ref[...], d_hidden_ref[:, at]).astype(BF)
            d_pre = jnp.where(active_ref[:, at] > 0, scattered, jnp.zeros_like(scattered))
            total = dot(rows_ref[...], d_pre)
            own_ref[:, at] = total[:half]
            other_ref[:, at] = total[half:].astype(BF)

    return pl.pallas_call(
        kernel,
        out_shape=[
            jax.ShapeDtypeStruct((half, units), F32),
            jax.ShapeDtypeStruct((half, units), BF),
        ],
        in_specs=[VMEM] * 4,
        out_specs=[VMEM] * 2,
        compiler_params=pltpu.CompilerParams(vmem_limit_bytes=24 * 2**20),
        cost_estimate=pl.CostEstimate(
            flops=2 * units,
            bytes_accessed=2 * units,
            transcendentals=0,
        ),
    )(spread_t, d_hidden, active, rows_t)


def body(features, nbr_page, nbr_weight, labels, w_one, w_two):
    rows_dev, width_f = features.shape
    targets, width_k = nbr_page.shape
    own_n, col_n, mlp_n = (lax.axis_size(a) for a in ("own", "col", "mlp"))
    owners = own_n * col_n
    entries = targets * width_k
    capacity = 2 * entries // owners
    share = capacity // mlp_n
    units, classes = w_two.shape
    me = lax.axis_index("mlp")
    core = lax.axis_index("col") % 2

    def to_mlp(x, step):
        return lax.ppermute(x, "mlp", [(j, (j + step) % mlp_n) for j in range(mlp_n)])

    steps = (2, 1, 3, 0)
    w_both = jnp.concatenate([w_one, w_two], axis=1)
    w_boths = {0: w_both}
    for step in steps[:-1]:
        w_boths[step] = to_mlp(w_both, -step)

    owner_range = jnp.arange(owners, dtype=jnp.int32)
    owner_ids = nbr_page // rows_dev
    local_row = nbr_page % rows_dev
    matches = owner_ids[:, :, None] == owner_range[None, None, :]
    row_count = jnp.sum(matches.astype(F32), axis=1)
    t_range = jnp.arange(targets)
    earlier = dot((t_range[:, None] > t_range[None, :]).astype(BF), row_count.astype(BF))
    before = dot(row_count.astype(BF), (owner_range[:, None] < owner_range[None, :]).astype(BF))
    first_slot = earlier - before
    slot_ids = (
        jnp.sum(matches.astype(F32) * first_slot[:, None, :], axis=2).astype(jnp.int32)
        + jnp.arange(width_k, dtype=jnp.int32)[None, :]
    )
    by_owner = matches.astype(BF).reshape(entries, owners)
    in_slot = slot_ids[:, :, None] == jnp.arange(capacity, dtype=jnp.int32)[None, None, :]

    def place(values):
        spread_out = jnp.where(in_slot, values.astype(BF)[:, :, None], jnp.zeros((), BF))
        return dot(by_owner, spread_out.reshape(entries, capacity), 0, 0)

    requests = (place(local_row // 64) * 64.0 + place(local_row % 64)).astype(jnp.int32)
    slot_weight = place(nbr_weight)
    slot_target = place(jnp.broadcast_to(t_range[:, None], (targets, width_k)))

    asked = exchange(requests, ("own", "col"))
    asked = lax.dynamic_slice_in_dim(asked, me * share, share, 1)
    fetched = features[asked]
    received = exchange(fetched, ("own", "col")).reshape(owners * share, width_f)

    my_weight = lax.dynamic_slice_in_dim(slot_weight, me * share, share, 1).reshape(1, -1)
    my_target = lax.dynamic_slice_in_dim(slot_target, me * share, share, 1).reshape(1, -1)
    spread = jnp.where(
        my_target.astype(jnp.int32) == t_range[:, None].astype(jnp.int32), my_weight, 0.0
    ).astype(BF)
    spread, spread_t = lax.optimization_barrier((spread, spread.T))

    core_id = core.reshape(1)
    active, hidden = {}, 0.0
    for step in steps:
        out = F32 if step == 0 else BF
        active[step], part, *turned = forward(
            received, w_boths[step], spread, core_id, out, step == 0
        )
        hidden += to_mlp(part, step).astype(F32) if step else part
    hidden = hidden.astype(BF)
    half = width_f // 2
    (rows_t,) = turned

    part = dot(hidden, w_two)
    parts = [part] + [to_mlp(part, step) for step in steps[:-1]]

    pairs = [(i, i ^ 1) for i in range(col_n)]

    def partner(x):
        return lax.ppermute(x, "col", pairs)

    mine, other, *d_hidden = middle(
        parts, labels[:, None], hidden, [w_boths[s] for s in steps], core_id
    )
    own_two, other_two = mine, other
    sums = []
    for i, step in enumerate(steps):
        d_slice = d_hidden[i]
        if i >= 2:
            d_slice, sums[i - 2] = lax.optimization_barrier((d_slice, sums[i - 2]))
        mine, other = backward(spread_t, d_slice, active[step], rows_t)
        mine += partner(other).astype(F32)
        sums.append(mine.astype(BF) if step else mine)
    grad_two = own_two + partner(other_two).astype(F32)
    grad_one = sums[-1]
    for step, value in zip(steps[:-1], sums):
        grad_one += to_mlp(value, step).astype(F32)
    both = jnp.concatenate([grad_one, grad_two], axis=1).astype(BF)
    chips = owners // 2
    groups = [[2 * i + c for i in range(chips)] for c in (0, 1)]
    width = units + classes
    both = exchange(both.reshape(chips, half // chips, width), ("own", "col"), groups)
    both = jnp.sum(both.astype(F32), axis=0).astype(BF)
    both = jnp.broadcast_to(both[None], (chips, half // chips, width))
    both = exchange(both, ("own", "col"), groups).reshape(half, width)
    other = partner(both)
    low = jnp.where(core == 0, both, other)
    high = jnp.where(core == 0, other, both)
    both = jnp.concatenate([low, high], axis=0).astype(F32)
    return both[:, :units], both[:, units:]


def solution(mesh):
    placed = (
        P(("own", "col"), None),
        P(("own", "col"), None),
        P(("own", "col"), None),
        P(("own", "col")),
        P(None, "mlp"),
        P("mlp", None),
    )
    return jax.shard_map(
        body,
        mesh=mesh,
        in_specs=placed,
        out_specs=(P(None, "mlp"), P("mlp", None)),
        check_vma=False,
    )
```

```python
import jax
import jax.numpy as jnp
from jax import lax
from jax.experimental import pallas as pl
from jax.experimental.pallas import tpu as pltpu
from jax.sharding import PartitionSpec as P

BF = jnp.bfloat16
F32 = jnp.float32


def dot(a, b, ca=1, cb=0):
    return lax.dot_general(a, b, (((ca,), (cb,)), ((), ())), preferred_element_type=F32)


def exchange(x, axes, groups=None):
    return lax.all_to_all(
        x, axes, split_axis=0, concat_axis=0, tiled=True, axis_index_groups=groups
    )


VMEM = pl.BlockSpec(memory_space=pltpu.VMEM)
SMEM = pl.BlockSpec(memory_space=pltpu.SMEM)
HBM = pl.BlockSpec(memory_space=pltpu.HBM)


def middle(parts, labels, hidden, w_boths, core):
    count = len(parts)
    targets, classes = parts[0].shape
    units = hidden.shape[1]
    half = units // 2

    def kernel(core_ref, *refs):
        part_refs, refs = refs[:count], refs[count:]
        labels_ref, hidden_ref = refs[:2]
        w_refs, refs = refs[2 : 2 + count], refs[2 + count :]
        own_ref, other_ref = refs[:2]
        d_hidden_refs = refs[2 : 2 + count]
        w_all, sems = refs[2 + count :]
        copies = [
            pltpu.make_async_copy(w_refs[i].at[:, pl.ds(units, classes)], w_all.at[i], sems.at[i])
            for i in range(count)
        ]
        for copy in copies:
            copy.start()
        logits = part_refs[0][...]
        for part in part_refs[1:]:
            logits += part[...]
        exponent = jnp.exp(logits)
        probability = exponent / jnp.sum(exponent, axis=1, keepdims=True)
        ids = lax.broadcasted_iota(jnp.int32, (targets, classes), 1)
        onehot = (labels_ref[...] == ids).astype(F32)
        d_logits = (probability - onehot).astype(BF)
        both = dot(hidden_ref[...], d_logits, 0, 0)
        swap = core_ref[0] != 0
        low, high = both[:half], both[half:]
        own_ref[...] = jnp.where(swap, high, low)
        other_ref[...] = jnp.where(swap, low, high).astype(BF)
        for i in range(count):
            copies[i].wait()
            d_hidden_refs[i][...] = dot(d_logits, w_all[i], 1, 1).astype(BF)

    return pl.pallas_call(
        kernel,
        out_shape=[
            jax.ShapeDtypeStruct((half, classes), F32),
            jax.ShapeDtypeStruct((half, classes), BF),
        ]
        + [jax.ShapeDtypeStruct((targets, units), BF)] * count,
        in_specs=[SMEM] + [VMEM] * (count + 2) + [HBM] * count,
        out_specs=[VMEM] * (2 + count),
        scratch_shapes=[
            pltpu.VMEM((count, units, classes), BF),
            pltpu.SemaphoreType.DMA((count,)),
        ],
        compiler_params=pltpu.CompilerParams(vmem_limit_bytes=24 * 2**20),
        cost_estimate=pl.CostEstimate(
            flops=2 * targets * classes * units * (count + 1),
            bytes_accessed=4 * 2**20,
            transcendentals=targets * classes,
        ),
    )(core, *parts, labels, hidden, *w_boths)


def forward(rows, w_boths, spread, core, out_type, turn):
    slots, width_f = rows.shape
    targets = spread.shape[0]
    units = width_f
    half = width_f // 2
    block = 512
    count = len(w_boths)

    def kernel(core_ref, rows_ref, spread_ref, *refs):
        w_refs, refs = refs[:count], refs[count:]
        active_refs, refs = refs[:count], refs[count:]
        hidden_refs, refs = refs[:count], refs[count:]
        turned_refs, refs = refs[:turn], refs[turn:]
        w_all, active_all, spread_all, w_sems, out_sems, spread_sem = refs[:6]
        turned, turned_sems = refs[6 : 6 + turn], refs[6 + turn :]
        for i in range(count):
            pltpu.make_async_copy(
                w_refs[i].at[:, pl.ds(0, units)], w_all.at[i], w_sems.at[i]
            ).start()
        spread_copy = pltpu.make_async_copy(spread_ref, spread_all, spread_sem)
        spread_copy.start()
        mine = pl.multiple_of(core_ref[0] * half, half)
        other = pl.multiple_of((1 - core_ref[0]) * half, half)
        for i in range(count):
            pltpu.make_async_copy(
                w_refs[i].at[:, pl.ds(0, units)], w_all.at[i], w_sems.at[i]
            ).wait()

            @pl.loop(0, slots // block)
            def _(j, i=i):
                at = pl.ds(pl.multiple_of(j * block, block), block)
                value = rows_ref[at, :]
                active_all[i, at, :] = jnp.maximum(dot(value, w_all[i]), 0.0).astype(BF)
                if i == count - 1:
                    for ref in turned:
                        flat = value.T
                        ref[pl.ds(mine, half), at] = flat[:half]
                        ref[pl.ds(other, half), at] = flat[half:]

            pltpu.make_async_copy(active_all.at[i], active_refs[i], out_sems.at[i]).start()
            if i == count - 1:
                for source, target, sem in zip(turned, turned_refs, turned_sems):
                    pltpu.make_async_copy(source, target, sem).start()
            if i == 0:
                spread_copy.wait()
            hidden_refs[i][...] = dot(spread_all[...], active_all[i]).astype(out_type)
        for i in range(count):
            pltpu.make_async_copy(active_all.at[i], active_refs[i], out_sems.at[i]).wait()
        for source, target, sem in zip(turned, turned_refs, turned_sems):
            pltpu.make_async_copy(source, target, sem).wait()

    shapes = (
        [pltpu.HBM((slots, units), BF)] * count
        + [jax.ShapeDtypeStruct((targets, units), out_type)] * count
        + [pltpu.HBM((width_f, slots), BF)] * turn
    )
    return pl.pallas_call(
        kernel,
        out_shape=shapes,
        in_specs=[SMEM, VMEM, HBM] + [HBM] * count,
        out_specs=[HBM] * count + [VMEM] * count + [HBM] * turn,
        scratch_shapes=[
            pltpu.VMEM((count, width_f, units), BF),
            pltpu.VMEM((count, slots, units), BF),
            pltpu.VMEM((targets, slots), BF),
            pltpu.SemaphoreType.DMA((count,)),
            pltpu.SemaphoreType.DMA((count,)),
            pltpu.SemaphoreType.DMA,
        ]
        + [pltpu.VMEM((width_f, slots), BF)] * turn
        + [pltpu.SemaphoreType.DMA] * turn,
        compiler_params=pltpu.CompilerParams(vmem_limit_bytes=24 * 2**20),
        cost_estimate=pl.CostEstimate(
            flops=2 * count * slots * units * (width_f + targets),
            bytes_accessed=2 * slots * (width_f + units + targets),
            transcendentals=0,
        ),
    )(core, rows, *(pltpu.with_memory_space_constraint(x, pltpu.HBM) for x in (spread, *w_boths)))


def backward(spread_t, d_hidden, active, rows_t):
    slots, targets = spread_t.shape
    units = d_hidden.shape[1]
    width_f = rows_t.shape[0]
    half = width_f // 2
    block = 256

    def kernel(spread_ref, d_hidden_ref, active_ref, rows_ref, own_ref, other_ref):
        @pl.loop(0, units // block)
        def _(i):
            at = pl.ds(pl.multiple_of(i * block, block), block)
            scattered = dot(spread_ref[...], d_hidden_ref[:, at]).astype(BF)
            d_pre = jnp.where(active_ref[:, at] > 0, scattered, jnp.zeros_like(scattered))
            total = dot(rows_ref[...], d_pre)
            own_ref[:, at] = total[:half]
            other_ref[:, at] = total[half:].astype(BF)

    return pl.pallas_call(
        kernel,
        out_shape=[
            jax.ShapeDtypeStruct((half, units), F32),
            jax.ShapeDtypeStruct((half, units), BF),
        ],
        in_specs=[VMEM] * 4,
        out_specs=[VMEM] * 2,
        compiler_params=pltpu.CompilerParams(vmem_limit_bytes=24 * 2**20),
        cost_estimate=pl.CostEstimate(
            flops=2 * units,
            bytes_accessed=2 * units,
            transcendentals=0,
        ),
    )(spread_t, d_hidden, active, rows_t)


def body(features, nbr_page, nbr_weight, labels, w_one, w_two):
    rows_dev, width_f = features.shape
    targets, width_k = nbr_page.shape
    own_n, col_n, mlp_n = (lax.axis_size(a) for a in ("own", "col", "mlp"))
    owners = own_n * col_n
    entries = targets * width_k
    capacity = 2 * entries // owners
    share = capacity // mlp_n
    units, classes = w_two.shape
    me = lax.axis_index("mlp")
    core = lax.axis_index("col") % 2

    def to_mlp(x, step):
        return lax.ppermute(x, "mlp", [(j, (j + step) % mlp_n) for j in range(mlp_n)])

    steps = (2, 1, 3, 0)
    w_both = jnp.concatenate([w_one, w_two], axis=1)
    w_boths = {0: w_both}
    for step in steps[:-1]:
        w_boths[step] = to_mlp(w_both, -step)

    owner_range = jnp.arange(owners, dtype=jnp.int32)
    owner_ids = nbr_page // rows_dev
    local_row = nbr_page % rows_dev
    matches = owner_ids[:, :, None] == owner_range[None, None, :]
    row_count = jnp.sum(matches.astype(F32), axis=1)
    t_range = jnp.arange(targets)
    earlier = dot((t_range[:, None] > t_range[None, :]).astype(BF), row_count.astype(BF))
    before = dot(row_count.astype(BF), (owner_range[:, None] < owner_range[None, :]).astype(BF))
    first_slot = earlier - before
    slot_ids = (
        jnp.sum(matches.astype(F32) * first_slot[:, None, :], axis=2).astype(jnp.int32)
        + jnp.arange(width_k, dtype=jnp.int32)[None, :]
    )
    by_owner = matches.astype(BF).reshape(entries, owners)
    in_slot = slot_ids[:, :, None] == jnp.arange(capacity, dtype=jnp.int32)[None, None, :]

    def place(values):
        spread_out = jnp.where(in_slot, values.astype(BF)[:, :, None], jnp.zeros((), BF))
        return dot(by_owner, spread_out.reshape(entries, capacity), 0, 0)

    requests = (place(local_row // 64) * 64.0 + place(local_row % 64)).astype(jnp.int32)
    slot_weight = place(nbr_weight)
    slot_target = place(jnp.broadcast_to(t_range[:, None], (targets, width_k)))

    asked = exchange(requests, ("own", "col"))
    asked = lax.dynamic_slice_in_dim(asked, me * share, share, 1)
    fetched = features[asked]
    received = exchange(fetched, ("own", "col")).reshape(owners * share, width_f)

    my_weight = lax.dynamic_slice_in_dim(slot_weight, me * share, share, 1).reshape(1, -1)
    my_target = lax.dynamic_slice_in_dim(slot_target, me * share, share, 1).reshape(1, -1)
    spread = jnp.where(
        my_target.astype(jnp.int32) == t_range[:, None].astype(jnp.int32), my_weight, 0.0
    ).astype(BF)
    spread, spread_t = lax.optimization_barrier((spread, spread.T))

    core_id = core.reshape(1)
    first = steps[:-1]
    out = forward(received, [w_boths[s] for s in first], spread, core_id, BF, 0)
    active = dict(zip(first, out))
    shares = [to_mlp(part, step) for part, step in zip(out[len(first) :], first)]
    active[0], hidden, rows_t = forward(received, [w_both], spread, core_id, F32, 1)
    for share_in in shares:
        hidden += share_in.astype(F32)
    hidden = hidden.astype(BF)
    half = width_f // 2

    part = dot(hidden, w_two)
    parts = [part] + [to_mlp(part, step) for step in steps[:-1]]

    pairs = [(i, i ^ 1) for i in range(col_n)]

    def partner(x):
        return lax.ppermute(x, "col", pairs)

    mine, other, *d_hidden = middle(
        parts, labels[:, None], hidden, [w_boths[s] for s in steps], core_id
    )
    own_two, other_two = mine, other
    grad_one, arrived = [], []
    for i, step in enumerate(steps):
        d_slice = d_hidden[i]
        if i == 2:
            d_slice, grad_one[0] = lax.optimization_barrier((d_slice, grad_one[0]))
            arrived.append(to_mlp(grad_one[0], steps[0]))
        if i == 3:
            arrived += [to_mlp(g, s) for g, s in zip(grad_one[1:], steps[1:])]
            d_slice, arrived[0] = lax.optimization_barrier((d_slice, arrived[0]))
        mine, other = backward(spread_t, d_slice, active[step], rows_t)
        mine += partner(other).astype(F32)
        grad_one.append(mine.astype(BF) if step else mine)
    grad_two = own_two + partner(other_two).astype(F32)
    grad_one = grad_one[-1]
    for value in arrived:
        grad_one += value.astype(F32)
    both = jnp.concatenate([grad_one, grad_two], axis=1).astype(BF)
    chips = owners // 2
    groups = [[2 * i + c for i in range(chips)] for c in (0, 1)]
    width = units + classes
    both = exchange(both.reshape(chips, half // chips, width), ("own", "col"), groups)
    both = jnp.sum(both.astype(F32), axis=0).astype(BF)
    both = jnp.broadcast_to(both[None], (chips, half // chips, width))
    both = exchange(both, ("own", "col"), groups).reshape(half, width)
    other = partner(both)
    low = jnp.where(core == 0, both, other)
    high = jnp.where(core == 0, other, both)
    both = jnp.concatenate([low, high], axis=0).astype(F32)
    return both[:, :units], both[:, units:]


def solution(mesh):
    placed = (
        P(("own", "col"), None),
        P(("own", "col"), None),
        P(("own", "col"), None),
        P(("own", "col")),
        P(None, "mlp"),
        P("mlp", None),
    )
    return jax.shard_map(
        body,
        mesh=mesh,
        in_specs=placed,
        out_specs=(P(None, "mlp"), P("mlp", None)),
        check_vma=False,
    )
```

```python
import jax
import jax.numpy as jnp
from jax import lax
from jax.experimental import pallas as pl
from jax.experimental.pallas import tpu as pltpu
from jax.sharding import PartitionSpec as P

BF = jnp.bfloat16
F32 = jnp.float32


def dot(a, b, ca=1, cb=0):
    return lax.dot_general(a, b, (((ca,), (cb,)), ((), ())), preferred_element_type=F32)


def exchange(x, axes, groups=None):
    return lax.all_to_all(
        x, axes, split_axis=0, concat_axis=0, tiled=True, axis_index_groups=groups
    )


VMEM = pl.BlockSpec(memory_space=pltpu.VMEM)
SMEM = pl.BlockSpec(memory_space=pltpu.SMEM)
HBM = pl.BlockSpec(memory_space=pltpu.HBM)


def slots_of(page_t, rows_dev, owners, capacity):
    width_k, targets = page_t.shape
    shift = rows_dev.bit_length() - 1
    low_bits = 6
    low_mask = (1 << low_bits) - 1

    def kernel(page_ref, request_ref, slot_ref, lhs, rhs):
        page = page_ref[...]
        owner = lax.shift_right_logical(page, jnp.int32(shift))
        row = page & (rows_dev - 1)
        high = lax.shift_right_logical(row, jnp.int32(low_bits)).astype(F32)
        low = (row & low_mask).astype(F32)
        owner_id = lax.broadcasted_iota(jnp.int32, (owners, targets), 0)
        count = jnp.zeros((owners, targets), F32)
        for k in range(width_k):
            match = (owner[k : k + 1] == owner_id).astype(F32)
            count += match
            lhs[:, k * targets : (k + 1) * targets] = match.astype(BF)
        count = count.astype(BF)

        def before(size):
            first = lax.broadcasted_iota(jnp.int32, (size, size), 0)
            return first, lax.broadcasted_iota(jnp.int32, (size, size), 1)

        first, second = before(targets)
        earlier = dot(count, (first < second).astype(F32).astype(BF))
        first, second = before(owners)
        smaller = dot((second < first).astype(F32).astype(BF), count)
        start = earlier - smaller
        slot_id = lax.broadcasted_iota(jnp.int32, (capacity, targets), 0)
        for k in range(width_k):
            mine = jnp.where(owner[k : k + 1] == owner_id, start, 0.0)
            slot = jnp.sum(mine, axis=0, keepdims=True).astype(jnp.int32) + k
            slot_ref[k : k + 1] = slot
            hit = slot == slot_id
            at = slice(k * targets, (k + 1) * targets)
            rhs[:capacity, at] = jnp.where(hit, high[k : k + 1], 0.0).astype(BF)
            rhs[capacity:, at] = jnp.where(hit, low[k : k + 1], 0.0).astype(BF)
        both = dot(lhs[...], rhs[...], 1, 1)
        request = both[:, :capacity] * float(1 << low_bits) + both[:, capacity:]
        request_ref[...] = request.astype(jnp.int32)

    entries = width_k * targets
    return pl.pallas_call(
        kernel,
        out_shape=[
            jax.ShapeDtypeStruct((owners, capacity), jnp.int32),
            jax.ShapeDtypeStruct((width_k, targets), jnp.int32),
        ],
        in_specs=[VMEM],
        out_specs=[VMEM] * 2,
        scratch_shapes=[
            pltpu.VMEM((owners, entries), BF),
            pltpu.VMEM((2 * capacity, entries), BF),
        ],
        compiler_params=pltpu.CompilerParams(vmem_limit_bytes=24 * 2**20),
    )(page_t)


def gather(features, asked, first_slot, share):
    rows_dev, width_f = features.shape
    askers = asked.shape[0]
    chunk = 512
    chunks = rows_dev // chunk

    def kernel(first_ref, asked_ref, features_ref, out_ref, wide, narrow, sems):
        copies = []
        for i in range(chunks):
            at = pl.ds(i * chunk, chunk)
            copies.append(
                pltpu.make_async_copy(features_ref.at[at, :], narrow.at[at, :], sems.at[i])
            )
        for copy in copies:
            copy.start()
        for i, copy in enumerate(copies):
            copy.wait()
            at = pl.ds(i * chunk, chunk)
            wide[at, :] = narrow[at, :].astype(F32)
        first = first_ref[0]

        @pl.loop(0, askers)
        def _(i):
            rows = [wide[pl.ds(asked_ref[i, first + j], 1), :] for j in range(share)]
            at = pl.ds(pl.multiple_of(i * share, share), share)
            out_ref[at, :] = jnp.concatenate(rows, axis=0).astype(BF)

    return pl.pallas_call(
        kernel,
        out_shape=jax.ShapeDtypeStruct((askers * share, width_f), BF),
        in_specs=[SMEM, SMEM, HBM],
        out_specs=VMEM,
        scratch_shapes=[
            pltpu.VMEM((rows_dev, width_f), F32),
            pltpu.VMEM((rows_dev, width_f), BF),
            pltpu.SemaphoreType.DMA((chunks,)),
        ],
        compiler_params=pltpu.CompilerParams(vmem_limit_bytes=32 * 2**20),
    )(first_slot, asked, pltpu.with_memory_space_constraint(features, pltpu.HBM))


def middle(parts, labels, hidden, w_boths, core):
    count = len(parts)
    targets, classes = parts[0].shape
    units = hidden.shape[1]
    half = units // 2

    def kernel(core_ref, *refs):
        part_refs, refs = refs[:count], refs[count:]
        labels_ref, hidden_ref = refs[:2]
        w_refs, refs = refs[2 : 2 + count], refs[2 + count :]
        own_ref, other_ref = refs[:2]
        d_hidden_refs = refs[2 : 2 + count]
        w_all, sems = refs[2 + count :]
        copies = [
            pltpu.make_async_copy(w_refs[i].at[:, pl.ds(units, classes)], w_all.at[i], sems.at[i])
            for i in range(count)
        ]
        for copy in copies:
            copy.start()
        logits = part_refs[0][...]
        for part in part_refs[1:]:
            logits += part[...]
        exponent = jnp.exp(logits)
        probability = exponent / jnp.sum(exponent, axis=1, keepdims=True)
        ids = lax.broadcasted_iota(jnp.int32, (targets, classes), 1)
        onehot = (labels_ref[...] == ids).astype(F32)
        d_logits = (probability - onehot).astype(BF)
        both = dot(hidden_ref[...], d_logits, 0, 0)
        swap = core_ref[0] != 0
        low, high = both[:half], both[half:]
        own_ref[...] = jnp.where(swap, high, low)
        other_ref[...] = jnp.where(swap, low, high).astype(BF)
        for i in range(count):
            copies[i].wait()
            d_hidden_refs[i][...] = dot(d_logits, w_all[i], 1, 1).astype(BF)

    return pl.pallas_call(
        kernel,
        out_shape=[
            jax.ShapeDtypeStruct((half, classes), F32),
            jax.ShapeDtypeStruct((half, classes), BF),
        ]
        + [jax.ShapeDtypeStruct((targets, units), BF)] * count,
        in_specs=[SMEM] + [VMEM] * (count + 2) + [HBM] * count,
        out_specs=[VMEM] * (2 + count),
        scratch_shapes=[
            pltpu.VMEM((count, units, classes), BF),
            pltpu.SemaphoreType.DMA((count,)),
        ],
        compiler_params=pltpu.CompilerParams(vmem_limit_bytes=24 * 2**20),
        cost_estimate=pl.CostEstimate(
            flops=2 * targets * classes * units * (count + 1),
            bytes_accessed=4 * 2**20,
            transcendentals=targets * classes,
        ),
    )(core, *parts, labels, hidden, *w_boths)


def forward(rows, w_boths, spread, core, out_type, turn):
    slots, width_f = rows.shape
    targets = spread.shape[0]
    units = width_f
    half = width_f // 2
    block = 512
    count = len(w_boths)

    def kernel(core_ref, rows_ref, spread_ref, *refs):
        w_refs, refs = refs[:count], refs[count:]
        active_refs, refs = refs[:count], refs[count:]
        hidden_refs, refs = refs[:count], refs[count:]
        turned_refs, refs = refs[:turn], refs[turn:]
        w_all, active_all, spread_all, w_sems, out_sems, spread_sem = refs[:6]
        turned, turned_sems = refs[6 : 6 + turn], refs[6 + turn :]
        for i in range(count):
            pltpu.make_async_copy(
                w_refs[i].at[:, pl.ds(0, units)], w_all.at[i], w_sems.at[i]
            ).start()
        spread_copy = pltpu.make_async_copy(spread_ref, spread_all, spread_sem)
        spread_copy.start()
        mine = pl.multiple_of(core_ref[0] * half, half)
        other = pl.multiple_of((1 - core_ref[0]) * half, half)
        for source, target, sem in zip(turned, turned_refs, turned_sems):

            @pl.loop(0, slots // block)
            def _(j, source=source):
                at = pl.ds(pl.multiple_of(j * block, block), block)
                flat = rows_ref[at, :].T
                source[pl.ds(mine, half), at] = flat[:half]
                source[pl.ds(other, half), at] = flat[half:]

            pltpu.make_async_copy(source, target, sem).start()
        for i in range(count):
            pltpu.make_async_copy(
                w_refs[i].at[:, pl.ds(0, units)], w_all.at[i], w_sems.at[i]
            ).wait()

            active_all[i] = jnp.maximum(dot(rows_ref[...], w_all[i]), 0.0).astype(BF)
            pltpu.make_async_copy(active_all.at[i], active_refs[i], out_sems.at[i]).start()
            if i == 0:
                spread_copy.wait()
            hidden_refs[i][...] = dot(spread_all[...], active_all[i]).astype(out_type)
        for i in range(count):
            pltpu.make_async_copy(active_all.at[i], active_refs[i], out_sems.at[i]).wait()
        for source, target, sem in zip(turned, turned_refs, turned_sems):
            pltpu.make_async_copy(source, target, sem).wait()

    shapes = (
        [pltpu.HBM((slots, units), BF)] * count
        + [jax.ShapeDtypeStruct((targets, units), out_type)] * count
        + [pltpu.HBM((width_f, slots), BF)] * turn
    )
    return pl.pallas_call(
        kernel,
        out_shape=shapes,
        in_specs=[SMEM, VMEM, HBM] + [HBM] * count,
        out_specs=[HBM] * count + [VMEM] * count + [HBM] * turn,
        scratch_shapes=[
            pltpu.VMEM((count, width_f, units), BF),
            pltpu.VMEM((count, slots, units), BF),
            pltpu.VMEM((targets, slots), BF),
            pltpu.SemaphoreType.DMA((count,)),
            pltpu.SemaphoreType.DMA((count,)),
            pltpu.SemaphoreType.DMA,
        ]
        + [pltpu.VMEM((width_f, slots), BF)] * turn
        + [pltpu.SemaphoreType.DMA] * turn,
        compiler_params=pltpu.CompilerParams(vmem_limit_bytes=24 * 2**20),
        cost_estimate=pl.CostEstimate(
            flops=2 * count * slots * units * (width_f + targets),
            bytes_accessed=2 * slots * (width_f + units + targets),
            transcendentals=0,
        ),
    )(core, rows, *(pltpu.with_memory_space_constraint(x, pltpu.HBM) for x in (spread, *w_boths)))


def backward(spread_t, d_hidden, active, rows_t, arrived):
    slots, targets = spread_t.shape
    units = d_hidden.shape[1]
    width_f = rows_t.shape[0]
    half = width_f // 2

    def kernel(spread_ref, d_hidden_ref, active_ref, rows_ref, *refs):
        own_ref, other_ref = refs[-2:]
        scattered = dot(spread_ref[...], d_hidden_ref[...]).astype(BF)
        d_pre = jnp.where(active_ref[...] > 0, scattered, jnp.zeros_like(scattered))
        total = dot(rows_ref[...], d_pre)
        own = total[:half]
        for ref in refs[:-2]:
            own += ref[...].astype(F32)
        own_ref[...] = own
        other_ref[...] = total[half:].astype(BF)

    return pl.pallas_call(
        kernel,
        out_shape=[
            jax.ShapeDtypeStruct((half, units), F32),
            jax.ShapeDtypeStruct((half, units), BF),
        ],
        in_specs=[VMEM] * (4 + len(arrived)),
        out_specs=[VMEM] * 2,
        compiler_params=pltpu.CompilerParams(vmem_limit_bytes=24 * 2**20),
        cost_estimate=pl.CostEstimate(
            flops=2 * units,
            bytes_accessed=2 * units,
            transcendentals=0,
        ),
    )(spread_t, d_hidden, active, rows_t, *arrived)


def body(features, nbr_page, nbr_weight, labels, w_one, w_two):
    rows_dev, width_f = features.shape
    targets, width_k = nbr_page.shape
    own_n, col_n, mlp_n = (lax.axis_size(a) for a in ("own", "col", "mlp"))
    owners = own_n * col_n
    entries = targets * width_k
    capacity = 2 * entries // owners
    share = capacity // mlp_n
    units, classes = w_two.shape
    me = lax.axis_index("mlp")
    core = lax.axis_index("col") % 2

    def to_mlp(x, step):
        return lax.ppermute(x, "mlp", [(j, (j + step) % mlp_n) for j in range(mlp_n)])

    steps = (2, 1, 3, 0)
    w_both = jnp.concatenate([w_one, w_two], axis=1)
    w_boths = {0: w_both}
    for step in steps[:-1]:
        w_boths[step] = to_mlp(w_both, -step)

    requests, slot_ids = slots_of(nbr_page.T, rows_dev, owners, capacity)
    asked = exchange(requests, ("own", "col"))
    fetched = gather(features, asked, (me * share).reshape(1), share)
    fetched = fetched.reshape(owners, share, width_f)
    received = exchange(fetched, ("own", "col")).reshape(owners * share, width_f)

    slot_ids = slot_ids.T
    owner_range = jnp.arange(owners, dtype=jnp.int32)
    t_range = jnp.arange(targets)
    matches = (nbr_page // rows_dev)[:, :, None] == owner_range[None, None, :]
    by_owner = matches.astype(BF).reshape(entries, owners)
    in_slot = slot_ids[:, :, None] == jnp.arange(capacity, dtype=jnp.int32)[None, None, :]

    def place(values):
        spread_out = jnp.where(in_slot, values.astype(BF)[:, :, None], jnp.zeros((), BF))
        return dot(by_owner, spread_out.reshape(entries, capacity), 0, 0)

    slot_weight = place(nbr_weight)
    slot_target = place(jnp.broadcast_to(t_range[:, None], (targets, width_k)))

    my_weight = lax.dynamic_slice_in_dim(slot_weight, me * share, share, 1).reshape(1, -1)
    my_target = lax.dynamic_slice_in_dim(slot_target, me * share, share, 1).reshape(1, -1)
    spread = jnp.where(
        my_target.astype(jnp.int32) == t_range[:, None].astype(jnp.int32), my_weight, 0.0
    ).astype(BF)
    spread, spread_t = lax.optimization_barrier((spread, spread.T))

    core_id = core.reshape(1)
    first = steps[:-1]
    out = forward(received, [w_boths[s] for s in first], spread, core_id, BF, 0)
    active = dict(zip(first, out))
    shares = [to_mlp(part, step) for part, step in zip(out[len(first) :], first)]
    active[0], hidden, rows_t = forward(received, [w_both], spread, core_id, F32, 1)
    for share_in in shares:
        hidden += share_in.astype(F32)
    hidden = hidden.astype(BF)
    half = width_f // 2

    part = dot(hidden, w_two)
    parts = [part] + [to_mlp(part, step) for step in steps[:-1]]

    pairs = [(i, i ^ 1) for i in range(col_n)]

    def partner(x):
        return lax.ppermute(x, "col", pairs)

    mine, other, *d_hidden = middle(
        parts, labels[:, None], hidden, [w_boths[s] for s in steps], core_id
    )
    own_two, other_two = mine, other
    grad_one, arrived = [], []
    for i, step in enumerate(steps):
        d_slice = d_hidden[i]
        if i == 2:
            d_slice, grad_one[0] = lax.optimization_barrier((d_slice, grad_one[0]))
            arrived.append(to_mlp(grad_one[0], steps[0]))
        if i == 3:
            arrived += [to_mlp(g, s) for g, s in zip(grad_one[1:], steps[1:])]
        mine, other = backward(spread_t, d_slice, active[step], rows_t, arrived if i == 3 else [])
        mine += partner(other).astype(F32)
        grad_one.append(mine.astype(BF) if step else mine)
    grad_two = own_two + partner(other_two).astype(F32)
    grad_one = grad_one[-1]
    both = jnp.concatenate([grad_one, grad_two], axis=1).astype(BF)
    chips = owners // 2
    groups = [[2 * i + c for i in range(chips)] for c in (0, 1)]
    width = units + classes
    both = exchange(both.reshape(chips, half // chips, width), ("own", "col"), groups)
    both = jnp.sum(both.astype(F32), axis=0).astype(BF)
    both = jnp.broadcast_to(both[None], (chips, half // chips, width))
    both = exchange(both, ("own", "col"), groups).reshape(half, width)
    other = partner(both)
    low = jnp.where(core == 0, both, other)
    high = jnp.where(core == 0, other, both)
    both = jnp.concatenate([low, high], axis=0).astype(F32)
    return both[:, :units], both[:, units:]


def solution(mesh):
    placed = (
        P(("own", "col"), None),
        P(("own", "col"), None),
        P(("own", "col"), None),
        P(("own", "col")),
        P(None, "mlp"),
        P("mlp", None),
    )
    return jax.shard_map(
        body,
        mesh=mesh,
        in_specs=placed,
        out_specs=(P(None, "mlp"), P("mlp", None)),
        check_vma=False,
    )
```

```python
import jax
import jax.numpy as jnp
from jax import lax
from jax.experimental import pallas as pl
from jax.experimental.pallas import tpu as pltpu
from jax.sharding import PartitionSpec as P

BF = jnp.bfloat16
F32 = jnp.float32


def dot(a, b, ca=1, cb=0):
    return lax.dot_general(a, b, (((ca,), (cb,)), ((), ())), preferred_element_type=F32)


def exchange(x, axes, groups=None):
    return lax.all_to_all(
        x, axes, split_axis=0, concat_axis=0, tiled=True, axis_index_groups=groups
    )


VMEM = pl.BlockSpec(memory_space=pltpu.VMEM)
SMEM = pl.BlockSpec(memory_space=pltpu.SMEM)
HBM = pl.BlockSpec(memory_space=pltpu.HBM)


def slots_of(page_t, rows_dev, owners, capacity):
    width_k, targets = page_t.shape
    shift = rows_dev.bit_length() - 1
    low_bits = 6
    low_mask = (1 << low_bits) - 1

    def kernel(page_ref, request_ref, slot_ref, lhs, rhs):
        page = page_ref[...]
        owner = lax.shift_right_logical(page, jnp.int32(shift))
        row = page & (rows_dev - 1)
        high = lax.shift_right_logical(row, jnp.int32(low_bits)).astype(F32)
        low = (row & low_mask).astype(F32)
        owner_id = lax.broadcasted_iota(jnp.int32, (owners, targets), 0)
        count = jnp.zeros((owners, targets), F32)
        for k in range(width_k):
            match = (owner[k : k + 1] == owner_id).astype(F32)
            count += match
            lhs[:, k * targets : (k + 1) * targets] = match.astype(BF)
        count = count.astype(BF)

        def before(size):
            first = lax.broadcasted_iota(jnp.int32, (size, size), 0)
            return first, lax.broadcasted_iota(jnp.int32, (size, size), 1)

        first, second = before(targets)
        earlier = dot(count, (first < second).astype(F32).astype(BF))
        first, second = before(owners)
        smaller = dot((second < first).astype(F32).astype(BF), count)
        start = earlier - smaller
        slot_id = lax.broadcasted_iota(jnp.int32, (capacity, targets), 0)
        for k in range(width_k):
            mine = jnp.where(owner[k : k + 1] == owner_id, start, 0.0)
            slot = jnp.sum(mine, axis=0, keepdims=True).astype(jnp.int32) + k
            slot_ref[k : k + 1] = slot
            hit = slot == slot_id
            at = slice(k * targets, (k + 1) * targets)
            rhs[:capacity, at] = jnp.where(hit, high[k : k + 1], 0.0).astype(BF)
            rhs[capacity:, at] = jnp.where(hit, low[k : k + 1], 0.0).astype(BF)
        both = dot(lhs[...], rhs[...], 1, 1)
        request = both[:, :capacity] * float(1 << low_bits) + both[:, capacity:]
        request_ref[...] = request.astype(jnp.int32)

    entries = width_k * targets
    return pl.pallas_call(
        kernel,
        out_shape=[
            jax.ShapeDtypeStruct((owners, capacity), jnp.int32),
            jax.ShapeDtypeStruct((width_k, targets), jnp.int32),
        ],
        in_specs=[VMEM],
        out_specs=[VMEM] * 2,
        scratch_shapes=[
            pltpu.VMEM((owners, entries), BF),
            pltpu.VMEM((2 * capacity, entries), BF),
        ],
        compiler_params=pltpu.CompilerParams(vmem_limit_bytes=24 * 2**20),
    )(page_t)


def gather(features, asked):
    rows_dev, width_f = features.shape
    (count,) = asked.shape
    group = 32
    chunk = 512
    chunks = rows_dev // chunk

    def kernel(asked_ref, features_ref, out_ref, wide, narrow, sems):
        copies = []
        for i in range(chunks):
            at = pl.ds(i * chunk, chunk)
            copies.append(
                pltpu.make_async_copy(features_ref.at[at, :], narrow.at[at, :], sems.at[i])
            )
        for copy in copies:
            copy.start()
        for i, copy in enumerate(copies):
            copy.wait()
            at = pl.ds(i * chunk, chunk)
            wide[at, :] = narrow[at, :].astype(F32)

        @pl.loop(0, count // group)
        def _(i):
            base = pl.multiple_of(i * group, group)
            rows = [wide[pl.ds(asked_ref[base + j], 1), :] for j in range(group)]
            out_ref[pl.ds(base, group), :] = jnp.concatenate(rows, axis=0).astype(BF)

    return pl.pallas_call(
        kernel,
        out_shape=jax.ShapeDtypeStruct((count, width_f), BF),
        in_specs=[SMEM, HBM],
        out_specs=VMEM,
        scratch_shapes=[
            pltpu.VMEM((rows_dev, width_f), F32),
            pltpu.VMEM((rows_dev, width_f), BF),
            pltpu.SemaphoreType.DMA((chunks,)),
        ],
        compiler_params=pltpu.CompilerParams(vmem_limit_bytes=32 * 2**20),
    )(asked, pltpu.with_memory_space_constraint(features, pltpu.HBM))


def slice_grad(spread_ref, d_hidden, active_ref, rows_ref, own_ref, other_ref):
    half = own_ref.shape[0]
    scattered = dot(spread_ref[...], d_hidden).astype(BF)
    d_pre = jnp.where(active_ref[...] > 0, scattered, jnp.zeros_like(scattered))
    total = dot(rows_ref[...], d_pre)
    own_ref[...] = total[:half]
    other_ref[...] = total[half:].astype(BF)


def middle(parts, labels, hidden, w_twos, core, spread_t, active, rows_t):
    count = len(parts)
    targets, classes = parts[0].shape
    units = hidden.shape[1]
    half = units // 2
    half_f = rows_t.shape[0] // 2

    def kernel(core_ref, *refs):
        part_refs, refs = refs[:count], refs[count:]
        labels_ref, hidden_ref = refs[:2]
        w_refs, refs = refs[2 : 2 + count], refs[2 + count :]
        spread_ref, active_ref, rows_ref, own_ref, other_ref, own_two, other_two = refs[:7]
        d_hidden_refs = refs[7:]
        logits = part_refs[0][...]
        for part in part_refs[1:]:
            logits += part[...]
        exponent = jnp.exp(logits)
        probability = exponent / jnp.sum(exponent, axis=1, keepdims=True)
        ids = lax.broadcasted_iota(jnp.int32, (targets, classes), 1)
        label = jnp.broadcast_to(labels_ref[...], (targets, targets)).T[:, :1]
        d_logits = (probability - (label == ids).astype(F32)).astype(BF)
        d_first = dot(d_logits, w_refs[0][...], 1, 1).astype(BF)
        for w_ref, out in zip(w_refs[1:], d_hidden_refs):
            out[...] = dot(d_logits, w_ref[...], 1, 1).astype(BF)
        slice_grad(spread_ref, d_first, active_ref, rows_ref, own_ref, other_ref)
        both = dot(hidden_ref[...], d_logits, 0, 0)
        swap = core_ref[0] != 0
        low, high = both[:half], both[half:]
        own_two[...] = jnp.where(swap, high, low)
        other_two[...] = jnp.where(swap, low, high).astype(BF)

    return pl.pallas_call(
        kernel,
        out_shape=[
            jax.ShapeDtypeStruct((half_f, units), F32),
            jax.ShapeDtypeStruct((half_f, units), BF),
            jax.ShapeDtypeStruct((half, classes), F32),
            jax.ShapeDtypeStruct((half, classes), BF),
        ]
        + [jax.ShapeDtypeStruct((targets, units), BF)] * (count - 1),
        in_specs=[SMEM] + [VMEM] * (2 * count + 5),
        out_specs=[VMEM] * (3 + count),
        compiler_params=pltpu.CompilerParams(vmem_limit_bytes=24 * 2**20),
        cost_estimate=pl.CostEstimate(
            flops=2 * targets * classes * units * (count + 1),
            bytes_accessed=4 * 2**20,
            transcendentals=targets * classes,
        ),
    )(core, *parts, labels, hidden, *w_twos, spread_t, active, rows_t)


def forward(rows, w_boths, spread, core, out_type, turn):
    slots, width_f = rows.shape
    targets = spread.shape[0]
    units = width_f
    half = width_f // 2
    block = 512
    count = len(w_boths)

    def kernel(core_ref, rows_ref, spread_ref, *refs):
        w_refs, refs = refs[:count], refs[count:]
        active_refs, refs = refs[:count], refs[count:]
        hidden_refs, refs = refs[:count], refs[count:]
        turned_refs, refs = refs[:turn], refs[turn:]
        w_all, active_all, spread_all, w_sems, out_sems, spread_sem = refs[:6]
        turned, turned_sems = refs[6 : 6 + turn], refs[6 + turn :]
        for i in range(count):
            pltpu.make_async_copy(
                w_refs[i].at[:, pl.ds(0, units)], w_all.at[i], w_sems.at[i]
            ).start()
        spread_copy = pltpu.make_async_copy(spread_ref, spread_all, spread_sem)
        spread_copy.start()
        mine = pl.multiple_of(core_ref[0] * half, half)
        other = pl.multiple_of((1 - core_ref[0]) * half, half)
        for source, target, sem in zip(turned, turned_refs, turned_sems):

            @pl.loop(0, slots // block)
            def _(j, source=source):
                at = pl.ds(pl.multiple_of(j * block, block), block)
                flat = rows_ref[at, :].T
                source[pl.ds(mine, half), at] = flat[:half]
                source[pl.ds(other, half), at] = flat[half:]

            pltpu.make_async_copy(source, target, sem).start()
        for i in range(count):
            pltpu.make_async_copy(
                w_refs[i].at[:, pl.ds(0, units)], w_all.at[i], w_sems.at[i]
            ).wait()

            active_all[i] = jnp.maximum(dot(rows_ref[...], w_all[i]), 0.0).astype(BF)
            pltpu.make_async_copy(active_all.at[i], active_refs[i], out_sems.at[i]).start()
            if i == 0:
                spread_copy.wait()
            hidden_refs[i][...] = dot(spread_all[...], active_all[i]).astype(out_type)
        for i in range(count):
            pltpu.make_async_copy(active_all.at[i], active_refs[i], out_sems.at[i]).wait()
        for source, target, sem in zip(turned, turned_refs, turned_sems):
            pltpu.make_async_copy(source, target, sem).wait()

    shapes = (
        [pltpu.HBM((slots, units), BF)] * count
        + [jax.ShapeDtypeStruct((targets, units), out_type)] * count
        + [pltpu.HBM((width_f, slots), BF)] * turn
    )
    return pl.pallas_call(
        kernel,
        out_shape=shapes,
        in_specs=[SMEM, VMEM, HBM] + [HBM] * count,
        out_specs=[HBM] * count + [VMEM] * count + [HBM] * turn,
        scratch_shapes=[
            pltpu.VMEM((count, width_f, units), BF),
            pltpu.VMEM((count, slots, units), BF),
            pltpu.VMEM((targets, slots), BF),
            pltpu.SemaphoreType.DMA((count,)),
            pltpu.SemaphoreType.DMA((count,)),
            pltpu.SemaphoreType.DMA,
        ]
        + [pltpu.VMEM((width_f, slots), BF)] * turn
        + [pltpu.SemaphoreType.DMA] * turn,
        compiler_params=pltpu.CompilerParams(vmem_limit_bytes=24 * 2**20),
        cost_estimate=pl.CostEstimate(
            flops=2 * count * slots * units * (width_f + targets),
            bytes_accessed=2 * slots * (width_f + units + targets),
            transcendentals=0,
        ),
    )(core, rows, *(pltpu.with_memory_space_constraint(x, pltpu.HBM) for x in (spread, *w_boths)))


def backward(spread_t, d_hidden, active, rows_t):
    units = d_hidden.shape[1]
    half = rows_t.shape[0] // 2

    def kernel(spread_ref, d_hidden_ref, *refs):
        slice_grad(spread_ref, d_hidden_ref[...], *refs)

    return pl.pallas_call(
        kernel,
        out_shape=[
            jax.ShapeDtypeStruct((half, units), F32),
            jax.ShapeDtypeStruct((half, units), BF),
        ],
        in_specs=[VMEM] * 4,
        out_specs=[VMEM] * 2,
        compiler_params=pltpu.CompilerParams(vmem_limit_bytes=24 * 2**20),
        cost_estimate=pl.CostEstimate(
            flops=2 * units, bytes_accessed=2 * units, transcendentals=0
        ),
    )(spread_t, d_hidden, active, rows_t)


def outputs(own, other, core, units):
    half, width = own.shape

    def kernel(core_ref, own_ref, other_ref, one_ref, two_ref, wide, sems):
        copies = []
        for i, ref in enumerate((own_ref, other_ref)):
            wide[i] = ref[...].astype(F32)
            place = core_ref[0] if i == 0 else 1 - core_ref[0]
            at = pl.ds(pl.multiple_of(place * half, half), half)
            for j, (out, first) in enumerate(((one_ref, 0), (two_ref, units))):
                source = wide.at[i, :, pl.ds(first, out.shape[1])]
                copies.append(pltpu.make_async_copy(source, out.at[at, :], sems.at[2 * i + j]))
                copies[-1].start()
        for copy in copies:
            copy.wait()

    return pl.pallas_call(
        kernel,
        out_shape=[pltpu.HBM((2 * half, units), F32), pltpu.HBM((2 * half, width - units), F32)],
        in_specs=[SMEM, VMEM, VMEM],
        out_specs=[HBM, HBM],
        scratch_shapes=[pltpu.VMEM((2, half, width), F32), pltpu.SemaphoreType.DMA((4,))],
        compiler_params=pltpu.CompilerParams(vmem_limit_bytes=24 * 2**20),
    )(core, own, other)


def body(features, nbr_page, nbr_weight, labels, w_one, w_two):
    rows_dev, width_f = features.shape
    targets, width_k = nbr_page.shape
    own_n, col_n, mlp_n = (lax.axis_size(a) for a in ("own", "col", "mlp"))
    owners = own_n * col_n
    entries = targets * width_k
    capacity = 2 * entries // owners
    share = capacity // mlp_n
    units, classes = w_two.shape
    me = lax.axis_index("mlp")
    core = lax.axis_index("col") % 2

    def to_mlp(x, step):
        return lax.ppermute(x, "mlp", [(j, (j + step) % mlp_n) for j in range(mlp_n)])

    steps = (2, 1, 3, 0)
    w_both = jnp.concatenate([w_one, w_two], axis=1)
    w_boths = {0: w_both}
    for step in steps[:-1]:
        w_boths[step] = to_mlp(w_both, -step)

    requests, slot_ids = slots_of(nbr_page.T, rows_dev, owners, capacity)
    asked = exchange(requests, ("own", "col"))
    asked = lax.dynamic_slice_in_dim(asked, me * share, share, 1).reshape(-1)
    fetched = gather(features, asked)
    fetched = fetched.reshape(owners, share, width_f)
    received = exchange(fetched, ("own", "col")).reshape(owners * share, width_f)

    slot_ids = slot_ids.T
    owner_range = jnp.arange(owners, dtype=jnp.int32)
    t_range = jnp.arange(targets)
    matches = (nbr_page // rows_dev)[:, :, None] == owner_range[None, None, :]
    by_owner = matches.astype(BF).reshape(entries, owners)
    in_slot = slot_ids[:, :, None] == jnp.arange(capacity, dtype=jnp.int32)[None, None, :]

    def place(values):
        spread_out = jnp.where(in_slot, values.astype(BF)[:, :, None], jnp.zeros((), BF))
        return dot(by_owner, spread_out.reshape(entries, capacity), 0, 0)

    slot_weight = place(nbr_weight)
    slot_target = place(jnp.broadcast_to(t_range[:, None], (targets, width_k)))

    my_weight = lax.dynamic_slice_in_dim(slot_weight, me * share, share, 1).reshape(1, -1)
    my_target = lax.dynamic_slice_in_dim(slot_target, me * share, share, 1).reshape(1, -1)
    spread = jnp.where(
        my_target.astype(jnp.int32) == t_range[:, None].astype(jnp.int32), my_weight, 0.0
    ).astype(BF)
    spread, spread_t = lax.optimization_barrier((spread, spread.T))

    core_id = core.reshape(1)
    first = steps[:-1]
    out = forward(received, [w_boths[s] for s in first], spread, core_id, BF, 0)
    active = dict(zip(first, out))
    shares = [to_mlp(part, step) for part, step in zip(out[len(first) :], first)]
    active[0], hidden, rows_t = forward(received, [w_both], spread, core_id, F32, 1)
    for share_in in shares:
        hidden += share_in.astype(F32)
    hidden = hidden.astype(BF)
    half = width_f // 2

    part = dot(hidden, w_two)
    parts = [part] + [to_mlp(part, step) for step in steps[:-1]]

    pairs = [(i, i ^ 1) for i in range(col_n)]

    def partner(x):
        return lax.ppermute(x, "col", pairs)

    mine, other, own_two, other_two, *d_hidden = middle(
        parts,
        labels[None],
        hidden,
        [w_both[:, units:] for w_both in (w_boths[s] for s in steps)],
        core_id,
        spread_t,
        active[2],
        rows_t,
    )
    far = (mine + partner(other).astype(F32)).astype(BF)
    upward, downward = to_mlp(far[: half // 2], 1), to_mlp(far[half // 2 :], -1)
    near = {}
    d_hidden = dict(zip(steps[1:], d_hidden))
    for step in (1, 0, 3):
        d_slice = d_hidden[step]
        if step == 0:
            d_slice, far = lax.optimization_barrier((d_slice, far))
            upward, downward = to_mlp(far[: half // 2], 1), to_mlp(far[half // 2 :], -1)
        if step == 3:
            d_slice, near[1] = lax.optimization_barrier((d_slice, near[1]))
        mine, other = backward(spread_t, d_slice, active[step], rows_t)
        near[step] = mine + partner(other).astype(F32)
    top, bottom = near[1][: half // 2], near[1][half // 2 :]
    near[1] = jnp.concatenate([top + upward.astype(F32), bottom], axis=0).astype(BF)
    top, bottom = near[3][: half // 2], near[3][half // 2 :]
    near[3] = jnp.concatenate([top, bottom + downward.astype(F32)], axis=0).astype(BF)
    grad_one = near[0] + to_mlp(near[1], 1).astype(F32) + to_mlp(near[3], -1).astype(F32)
    grad_two = own_two + partner(other_two).astype(F32)
    both = jnp.concatenate([grad_one, grad_two], axis=1).astype(BF)
    chips = owners // 2
    groups = [[2 * i + c for i in range(chips)] for c in (0, 1)]
    width = units + classes
    both = exchange(both.reshape(chips, half // chips, width), ("own", "col"), groups)
    both = jnp.sum(both.astype(F32), axis=0).astype(BF)
    both = jnp.broadcast_to(both[None], (chips, half // chips, width))
    both = exchange(both, ("own", "col"), groups).reshape(half, width)
    other = partner(both)
    return tuple(outputs(both, other, core_id, units))


def solution(mesh):
    placed = (
        P(("own", "col"), None),
        P(("own", "col"), None),
        P(("own", "col"), None),
        P(("own", "col")),
        P(None, "mlp"),
        P("mlp", None),
    )
    return jax.shard_map(
        body,
        mesh=mesh,
        in_specs=placed,
        out_specs=(P(None, "mlp"), P("mlp", None)),
        check_vma=False,
    )
```

```python
import jax
import jax.numpy as jnp
from jax import lax
from jax.experimental import pallas as pl
from jax.experimental.pallas import tpu as pltpu
from jax.sharding import PartitionSpec as P

BF = jnp.bfloat16
F32 = jnp.float32


def dot(a, b, ca=1, cb=0):
    return lax.dot_general(a, b, (((ca,), (cb,)), ((), ())), preferred_element_type=F32)


def exchange(x, axes, groups=None):
    return lax.all_to_all(
        x, axes, split_axis=0, concat_axis=0, tiled=True, axis_index_groups=groups
    )


VMEM = pl.BlockSpec(memory_space=pltpu.VMEM)
SMEM = pl.BlockSpec(memory_space=pltpu.SMEM)
HBM = pl.BlockSpec(memory_space=pltpu.HBM)


def slots_of(page_t, rows_dev, owners, capacity):
    width_k, targets = page_t.shape
    shift = rows_dev.bit_length() - 1
    low_bits = 6
    low_mask = (1 << low_bits) - 1

    def kernel(page_ref, request_ref, slot_ref, lhs, rhs):
        page = page_ref[...]
        owner = lax.shift_right_logical(page, jnp.int32(shift))
        row = page & (rows_dev - 1)
        high = lax.shift_right_logical(row, jnp.int32(low_bits)).astype(F32)
        low = (row & low_mask).astype(F32)
        owner_id = lax.broadcasted_iota(jnp.int32, (owners, targets), 0)
        count = jnp.zeros((owners, targets), F32)
        for k in range(width_k):
            match = (owner[k : k + 1] == owner_id).astype(F32)
            count += match
            lhs[:, k * targets : (k + 1) * targets] = match.astype(BF)
        count = count.astype(BF)

        def before(size):
            first = lax.broadcasted_iota(jnp.int32, (size, size), 0)
            return first, lax.broadcasted_iota(jnp.int32, (size, size), 1)

        first, second = before(targets)
        earlier = dot(count, (first < second).astype(F32).astype(BF))
        first, second = before(owners)
        smaller = dot((second < first).astype(F32).astype(BF), count)
        start = earlier - smaller
        slot_id = lax.broadcasted_iota(jnp.int32, (capacity, targets), 0)
        for k in range(width_k):
            mine = jnp.where(owner[k : k + 1] == owner_id, start, 0.0)
            slot = jnp.sum(mine, axis=0, keepdims=True).astype(jnp.int32) + k
            slot_ref[k : k + 1] = slot
            hit = slot == slot_id
            at = slice(k * targets, (k + 1) * targets)
            rhs[:capacity, at] = jnp.where(hit, high[k : k + 1], 0.0).astype(BF)
            rhs[capacity:, at] = jnp.where(hit, low[k : k + 1], 0.0).astype(BF)
        both = dot(lhs[...], rhs[...], 1, 1)
        request = both[:, :capacity] * float(1 << low_bits) + both[:, capacity:]
        request_ref[...] = request.astype(jnp.int32)

    entries = width_k * targets
    return pl.pallas_call(
        kernel,
        out_shape=[
            jax.ShapeDtypeStruct((owners, capacity), jnp.int32),
            jax.ShapeDtypeStruct((width_k, targets), jnp.int32),
        ],
        in_specs=[VMEM],
        out_specs=[VMEM] * 2,
        scratch_shapes=[
            pltpu.VMEM((owners, entries), BF),
            pltpu.VMEM((2 * capacity, entries), BF),
        ],
        compiler_params=pltpu.CompilerParams(vmem_limit_bytes=24 * 2**20),
    )(page_t)


def gather(features, asked):
    rows_dev, width_f = features.shape
    (count,) = asked.shape
    group = 32
    parts = 4
    chunk = 512
    chunks = rows_dev // chunk

    def kernel(asked_ref, features_ref, out_ref, wide, narrow, out, sems, out_sems):
        copies = []
        for i in range(chunks):
            at = pl.ds(i * chunk, chunk)
            copies.append(
                pltpu.make_async_copy(features_ref.at[at, :], narrow.at[at, :], sems.at[i])
            )
        for copy in copies:
            copy.start()
        for i, copy in enumerate(copies):
            copy.wait()
            at = pl.ds(i * chunk, chunk)
            wide[at, :] = narrow[at, :].astype(F32)

        copies = []
        part = count // parts
        for p in range(parts):

            @pl.loop(0, part // group)
            def _(i, p=p):
                base = pl.multiple_of(p * part + i * group, group)
                rows = [wide[pl.ds(asked_ref[base + j], 1), :] for j in range(group)]
                out[pl.ds(base, group), :] = jnp.concatenate(rows, axis=0).astype(BF)

            at = pl.ds(p * part, part)
            copies.append(pltpu.make_async_copy(out.at[at, :], out_ref.at[at, :], out_sems.at[p]))
            copies[-1].start()
        for copy in copies:
            copy.wait()

    return pl.pallas_call(
        kernel,
        out_shape=pltpu.HBM((count, width_f), BF),
        in_specs=[SMEM, HBM],
        out_specs=HBM,
        scratch_shapes=[
            pltpu.VMEM((rows_dev, width_f), F32),
            pltpu.VMEM((rows_dev, width_f), BF),
            pltpu.VMEM((count, width_f), BF),
            pltpu.SemaphoreType.DMA((chunks,)),
            pltpu.SemaphoreType.DMA((parts,)),
        ],
        compiler_params=pltpu.CompilerParams(vmem_limit_bytes=32 * 2**20),
    )(asked, pltpu.with_memory_space_constraint(features, pltpu.HBM))


def slice_grad(spread_ref, d_hidden, active_ref, rows_ref, own_ref, other_ref):
    half = own_ref.shape[0]
    scattered = dot(spread_ref[...], d_hidden).astype(BF)
    d_pre = jnp.where(active_ref[...] > 0, scattered, jnp.zeros_like(scattered))
    total = dot(rows_ref[...], d_pre)
    own_ref[...] = total[:half]
    other_ref[...] = total[half:].astype(BF)


def middle(parts, labels, hidden, w_twos, core, spread_t, active, rows_t):
    count = len(parts)
    targets, classes = parts[0].shape
    units = hidden.shape[1]
    half = units // 2
    half_f = rows_t.shape[0] // 2

    def kernel(core_ref, *refs):
        part_refs, refs = refs[:count], refs[count:]
        labels_ref, hidden_ref = refs[:2]
        w_refs, refs = refs[2 : 2 + count], refs[2 + count :]
        spread_ref, active_ref, rows_ref, own_ref, other_ref, own_two, other_two = refs[:7]
        d_hidden_refs = refs[7:]
        logits = part_refs[0][...]
        for part in part_refs[1:]:
            logits += part[...].astype(F32)
        exponent = jnp.exp(logits)
        probability = exponent / jnp.sum(exponent, axis=1, keepdims=True)
        ids = lax.broadcasted_iota(jnp.int32, (targets, classes), 1)
        label = jnp.broadcast_to(labels_ref[...], (targets, targets)).T[:, :1]
        d_logits = (probability - (label == ids).astype(F32)).astype(BF)
        d_first = dot(d_logits, w_refs[0][...], 1, 1).astype(BF)
        for w_ref, out in zip(w_refs[1:], d_hidden_refs):
            out[...] = dot(d_logits, w_ref[...], 1, 1).astype(BF)
        slice_grad(spread_ref, d_first, active_ref, rows_ref, own_ref, other_ref)
        both = dot(hidden_ref[...], d_logits, 0, 0)
        swap = core_ref[0] != 0
        low, high = both[:half], both[half:]
        own_two[...] = jnp.where(swap, high, low)
        other_two[...] = jnp.where(swap, low, high).astype(BF)

    return pl.pallas_call(
        kernel,
        out_shape=[
            jax.ShapeDtypeStruct((half_f, units), F32),
            jax.ShapeDtypeStruct((half_f, units), BF),
            jax.ShapeDtypeStruct((half, classes), F32),
            jax.ShapeDtypeStruct((half, classes), BF),
        ]
        + [jax.ShapeDtypeStruct((targets, units), BF)] * (count - 1),
        in_specs=[SMEM] + [VMEM] * (2 * count + 5),
        out_specs=[VMEM] * (3 + count),
        compiler_params=pltpu.CompilerParams(vmem_limit_bytes=24 * 2**20),
        cost_estimate=pl.CostEstimate(
            flops=2 * targets * classes * units * (count + 1),
            bytes_accessed=4 * 2**20,
            transcendentals=targets * classes,
        ),
    )(core, *parts, labels, hidden, *w_twos, spread_t, active, rows_t)


def forward(rows, w_ones, spread, core, out_type, turn):
    slots, width_f = rows.shape
    targets = spread.shape[0]
    units = width_f
    half = width_f // 2
    block = 512
    count = len(w_ones)

    def kernel(core_ref, rows_ref, spread_ref, *refs):
        w_refs, refs = refs[:count], refs[count:]
        active_refs, refs = refs[:count], refs[count:]
        hidden_refs, refs = refs[:count], refs[count:]
        turned_refs, refs = refs[:turn], refs[turn:]
        w_all, active_all, spread_all, w_sems, out_sems, spread_sem = refs[:6]
        turned, turned_sems = refs[6 : 6 + turn], refs[6 + turn :]
        for i in range(count):
            pltpu.make_async_copy(
                w_refs[i], w_all.at[i], w_sems.at[i]
            ).start()
        spread_copy = pltpu.make_async_copy(spread_ref, spread_all, spread_sem)
        spread_copy.start()
        mine = pl.multiple_of(core_ref[0] * half, half)
        other = pl.multiple_of((1 - core_ref[0]) * half, half)
        for source, target, sem in zip(turned, turned_refs, turned_sems):

            @pl.loop(0, slots // block)
            def _(j, source=source):
                at = pl.ds(pl.multiple_of(j * block, block), block)
                flat = rows_ref[at, :].T
                source[pl.ds(mine, half), at] = flat[:half]
                source[pl.ds(other, half), at] = flat[half:]

            pltpu.make_async_copy(source, target, sem).start()
        for i in range(count):
            pltpu.make_async_copy(
                w_refs[i], w_all.at[i], w_sems.at[i]
            ).wait()

            active_all[i] = jnp.maximum(dot(rows_ref[...], w_all[i]), 0.0).astype(BF)
            pltpu.make_async_copy(active_all.at[i], active_refs[i], out_sems.at[i]).start()
            if i == 0:
                spread_copy.wait()
            hidden_refs[i][...] = dot(spread_all[...], active_all[i]).astype(out_type)
        for i in range(count):
            pltpu.make_async_copy(active_all.at[i], active_refs[i], out_sems.at[i]).wait()
        for source, target, sem in zip(turned, turned_refs, turned_sems):
            pltpu.make_async_copy(source, target, sem).wait()

    shapes = (
        [pltpu.HBM((slots, units), BF)] * count
        + [jax.ShapeDtypeStruct((targets, units), out_type)] * count
        + [pltpu.HBM((width_f, slots), BF)] * turn
    )
    return pl.pallas_call(
        kernel,
        out_shape=shapes,
        in_specs=[SMEM, VMEM, HBM] + [HBM] * count,
        out_specs=[HBM] * count + [VMEM] * count + [HBM] * turn,
        scratch_shapes=[
            pltpu.VMEM((count, width_f, units), BF),
            pltpu.VMEM((count, slots, units), BF),
            pltpu.VMEM((targets, slots), BF),
            pltpu.SemaphoreType.DMA((count,)),
            pltpu.SemaphoreType.DMA((count,)),
            pltpu.SemaphoreType.DMA,
        ]
        + [pltpu.VMEM((width_f, slots), BF)] * turn
        + [pltpu.SemaphoreType.DMA] * turn,
        compiler_params=pltpu.CompilerParams(vmem_limit_bytes=24 * 2**20),
        cost_estimate=pl.CostEstimate(
            flops=2 * count * slots * units * (width_f + targets),
            bytes_accessed=2 * slots * (width_f + units + targets),
            transcendentals=0,
        ),
    )(core, rows, *(pltpu.with_memory_space_constraint(x, pltpu.HBM) for x in (spread, *w_ones)))


def backward(spread_t, d_hidden, active, rows_t, earlier):
    units = d_hidden.shape[1]
    half = rows_t.shape[0] // 2

    def kernel(spread_ref, d_hidden_ref, active_ref, rows_ref, *refs):
        slice_grad(spread_ref, d_hidden_ref[...], active_ref, rows_ref, *refs[-2:])

    return pl.pallas_call(
        kernel,
        out_shape=[
            jax.ShapeDtypeStruct((half, units), F32),
            jax.ShapeDtypeStruct((half, units), BF),
        ],
        in_specs=[VMEM] * 4 + [pl.BlockSpec(memory_space=pl.ANY)] * len(earlier),
        out_specs=[VMEM] * 2,
        compiler_params=pltpu.CompilerParams(vmem_limit_bytes=24 * 2**20),
        cost_estimate=pl.CostEstimate(
            flops=2 * units, bytes_accessed=2 * units, transcendentals=0
        ),
    )(spread_t, d_hidden, active, rows_t, *earlier)


def outputs(own, other, core, units):
    half, width = own.shape

    def kernel(core_ref, own_ref, other_ref, one_ref, two_ref, wide, sems):
        copies = []
        for i, ref in enumerate((own_ref, other_ref)):
            wide[i] = ref[...].astype(F32)
            place = core_ref[0] if i == 0 else 1 - core_ref[0]
            at = pl.ds(pl.multiple_of(place * half, half), half)
            for j, (out, first) in enumerate(((one_ref, 0), (two_ref, units))):
                source = wide.at[i, :, pl.ds(first, out.shape[1])]
                copies.append(pltpu.make_async_copy(source, out.at[at, :], sems.at[2 * i + j]))
                copies[-1].start()
        for copy in copies:
            copy.wait()

    return pl.pallas_call(
        kernel,
        out_shape=[pltpu.HBM((2 * half, units), F32), pltpu.HBM((2 * half, width - units), F32)],
        in_specs=[SMEM, VMEM, VMEM],
        out_specs=[HBM, HBM],
        scratch_shapes=[pltpu.VMEM((2, half, width), F32), pltpu.SemaphoreType.DMA((4,))],
        compiler_params=pltpu.CompilerParams(vmem_limit_bytes=24 * 2**20),
    )(core, own, other)


def body(features, nbr_page, nbr_weight, labels, w_one, w_two):
    rows_dev, width_f = features.shape
    targets, width_k = nbr_page.shape
    own_n, col_n, mlp_n = (lax.axis_size(a) for a in ("own", "col", "mlp"))
    owners = own_n * col_n
    entries = targets * width_k
    capacity = 2 * entries // owners
    share = capacity // mlp_n
    units, classes = w_two.shape
    me = lax.axis_index("mlp")
    core = lax.axis_index("col") % 2

    def to_mlp(x, step):
        return lax.ppermute(x, "mlp", [(j, (j + step) % mlp_n) for j in range(mlp_n)])

    steps = (2, 1, 3, 0)
    w_ones, w_twos = {0: w_one}, {0: w_two}
    for step in steps[:-1]:
        w_ones[step] = to_mlp(w_one, -step)
        w_twos[step] = to_mlp(w_two, -step)
    w_ones, w_twos = lax.optimization_barrier((w_ones, w_twos))

    requests, slot_ids = slots_of(nbr_page.T, rows_dev, owners, capacity)
    asked = exchange(requests, ("own", "col"))
    asked = lax.dynamic_slice_in_dim(asked, me * share, share, 1).reshape(-1)
    fetched = gather(features, asked)
    fetched = fetched.reshape(owners, share, width_f)
    received = exchange(fetched, ("own", "col")).reshape(owners * share, width_f)

    slot_ids = slot_ids.T
    owner_range = jnp.arange(owners, dtype=jnp.int32)
    t_range = jnp.arange(targets)
    matches = (nbr_page // rows_dev)[:, :, None] == owner_range[None, None, :]
    by_owner = matches.astype(BF).reshape(entries, owners)
    in_slot = slot_ids[:, :, None] == jnp.arange(capacity, dtype=jnp.int32)[None, None, :]

    def place(values):
        spread_out = jnp.where(in_slot, values.astype(BF)[:, :, None], jnp.zeros((), BF))
        return dot(by_owner, spread_out.reshape(entries, capacity), 0, 0)

    slot_weight = place(nbr_weight)
    slot_target = place(jnp.broadcast_to(t_range[:, None], (targets, width_k)))

    my_weight = lax.dynamic_slice_in_dim(slot_weight, me * share, share, 1).reshape(1, -1)
    my_target = lax.dynamic_slice_in_dim(slot_target, me * share, share, 1).reshape(1, -1)
    spread = jnp.where(
        my_target.astype(jnp.int32) == t_range[:, None].astype(jnp.int32), my_weight, 0.0
    ).astype(BF)
    spread, spread_t = lax.optimization_barrier((spread, spread.T))

    core_id = core.reshape(1)
    first = steps[:-1]
    out = forward(received, [w_ones[s] for s in first], spread, core_id, BF, 0)
    active = dict(zip(first, out))
    shares = [to_mlp(part, step) for part, step in zip(out[len(first) :], first)]
    active[0], hidden, rows_t = forward(received, [w_one], spread, core_id, F32, 1)
    for share_in in shares:
        hidden += share_in.astype(F32)
    hidden = hidden.astype(BF)
    half = width_f // 2

    part = dot(hidden, w_two)
    parts = [part] + [to_mlp(part.astype(BF), step) for step in steps[:-1]]

    pairs = [(i, i ^ 1) for i in range(col_n)]

    def partner(x):
        return lax.ppermute(x, "col", pairs)

    mine, other, own_two, other_two, *d_hidden = middle(
        parts,
        labels[None],
        hidden,
        [w_twos[s] for s in steps],
        core_id,
        spread_t,
        active[2],
        rows_t,
    )
    far = (mine + partner(other).astype(F32)).astype(BF)
    far = (far[: half // 2], far[half // 2 :])
    upward, downward = to_mlp(far[0], 1), to_mlp(far[1], -1)
    near = {}
    for step in (1, 0, 3):
        i = steps.index(step) - 1
        earlier = () if step == 1 else far if step == 0 else (near[1],)
        mine, other = backward(spread_t, d_hidden[i], active[step], rows_t, earlier)
        near[step] = mine + partner(other).astype(F32)
    top, bottom = near[1][: half // 2], near[1][half // 2 :]
    near[1] = jnp.concatenate([top + upward.astype(F32), bottom], axis=0).astype(BF)
    top, bottom = near[3][: half // 2], near[3][half // 2 :]
    near[3] = jnp.concatenate([top, bottom + downward.astype(F32)], axis=0).astype(BF)
    grad_one = near[0] + to_mlp(near[1], 1).astype(F32) + to_mlp(near[3], -1).astype(F32)
    grad_two = own_two + partner(other_two).astype(F32)
    both = jnp.concatenate([grad_one, grad_two], axis=1).astype(BF)
    chips = owners // 2
    groups = [[2 * i + c for i in range(chips)] for c in (0, 1)]
    width = units + classes
    both = exchange(both.reshape(chips, half // chips, width), ("own", "col"), groups)
    both = jnp.sum(both.astype(F32), axis=0).astype(BF)
    both = jnp.broadcast_to(both[None], (chips, half // chips, width))
    both = exchange(both, ("own", "col"), groups).reshape(half, width)
    other = partner(both)
    return tuple(outputs(both, other, core_id, units))


def solution(mesh):
    placed = (
        P(("own", "col"), None),
        P(("own", "col"), None),
        P(("own", "col"), None),
        P(("own", "col")),
        P(None, "mlp"),
        P("mlp", None),
    )
    return jax.shard_map(
        body,
        mesh=mesh,
        in_specs=placed,
        out_specs=(P(None, "mlp"), P("mlp", None)),
        check_vma=False,
    )
```

```python
import jax
import jax.numpy as jnp
from jax import lax
from jax.experimental import pallas as pl
from jax.experimental.pallas import tpu as pltpu
from jax.sharding import PartitionSpec as P

BF = jnp.bfloat16
F32 = jnp.float32


def dot(a, b, ca=1, cb=0):
    return lax.dot_general(a, b, (((ca,), (cb,)), ((), ())), preferred_element_type=F32)


def exchange(x, axes, groups=None):
    return lax.all_to_all(
        x, axes, split_axis=0, concat_axis=0, tiled=True, axis_index_groups=groups
    )


VMEM = pl.BlockSpec(memory_space=pltpu.VMEM)
SMEM = pl.BlockSpec(memory_space=pltpu.SMEM)
HBM = pl.BlockSpec(memory_space=pltpu.HBM)


def slots_of(page_t, rows_dev, owners, capacity):
    width_k, targets = page_t.shape
    shift = rows_dev.bit_length() - 1
    low_bits = 6
    low_mask = (1 << low_bits) - 1

    def kernel(page_ref, request_ref, slot_ref, lhs, rhs):
        page = page_ref[...]
        owner = lax.shift_right_logical(page, jnp.int32(shift))
        row = page & (rows_dev - 1)
        high = lax.shift_right_logical(row, jnp.int32(low_bits)).astype(F32)
        low = (row & low_mask).astype(F32)
        owner_id = lax.broadcasted_iota(jnp.int32, (owners, targets), 0)
        count = jnp.zeros((owners, targets), F32)
        for k in range(width_k):
            match = (owner[k : k + 1] == owner_id).astype(F32)
            count += match
            lhs[:, k * targets : (k + 1) * targets] = match.astype(BF)
        count = count.astype(BF)

        def before(size):
            first = lax.broadcasted_iota(jnp.int32, (size, size), 0)
            return first, lax.broadcasted_iota(jnp.int32, (size, size), 1)

        first, second = before(targets)
        earlier = dot(count, (first < second).astype(F32).astype(BF))
        first, second = before(owners)
        smaller = dot((second < first).astype(F32).astype(BF), count)
        start = earlier - smaller
        slot_id = lax.broadcasted_iota(jnp.int32, (capacity, targets), 0)
        for k in range(width_k):
            mine = jnp.where(owner[k : k + 1] == owner_id, start, 0.0)
            slot = jnp.sum(mine, axis=0, keepdims=True).astype(jnp.int32) + k
            slot_ref[k : k + 1] = slot
            hit = slot == slot_id
            at = slice(k * targets, (k + 1) * targets)
            rhs[:capacity, at] = jnp.where(hit, high[k : k + 1], 0.0).astype(BF)
            rhs[capacity:, at] = jnp.where(hit, low[k : k + 1], 0.0).astype(BF)
        both = dot(lhs[...], rhs[...], 1, 1)
        request = both[:, :capacity] * float(1 << low_bits) + both[:, capacity:]
        request_ref[...] = request.astype(jnp.int32)

    entries = width_k * targets
    return pl.pallas_call(
        kernel,
        out_shape=[
            jax.ShapeDtypeStruct((owners, capacity), jnp.int32),
            jax.ShapeDtypeStruct((width_k, targets), jnp.int32),
        ],
        in_specs=[VMEM],
        out_specs=[VMEM] * 2,
        scratch_shapes=[
            pltpu.VMEM((owners, entries), BF),
            pltpu.VMEM((2 * capacity, entries), BF),
        ],
        compiler_params=pltpu.CompilerParams(vmem_limit_bytes=24 * 2**20),
    )(page_t)


def gather(features, asked):
    rows_dev, width_f = features.shape
    (count,) = asked.shape
    group = 32
    parts = 4
    chunk = 512
    chunks = rows_dev // chunk

    def kernel(asked_ref, features_ref, out_ref, wide, narrow, out, sems, out_sems):
        copies = []
        for i in range(chunks):
            at = pl.ds(i * chunk, chunk)
            copies.append(
                pltpu.make_async_copy(features_ref.at[at, :], narrow.at[at, :], sems.at[i])
            )
        for copy in copies:
            copy.start()
        for i, copy in enumerate(copies):
            copy.wait()
            at = pl.ds(i * chunk, chunk)
            wide[at, :] = narrow[at, :].astype(F32)

        copies = []
        part = count // parts
        for p in range(parts):

            @pl.loop(0, part // group)
            def _(i, p=p):
                base = pl.multiple_of(p * part + i * group, group)
                rows = [wide[pl.ds(asked_ref[base + j], 1), :] for j in range(group)]
                out[pl.ds(base, group), :] = jnp.concatenate(rows, axis=0).astype(BF)

            at = pl.ds(p * part, part)
            copies.append(pltpu.make_async_copy(out.at[at, :], out_ref.at[at, :], out_sems.at[p]))
            copies[-1].start()
        for copy in copies:
            copy.wait()

    return pl.pallas_call(
        kernel,
        out_shape=pltpu.HBM((count, width_f), BF),
        in_specs=[SMEM, HBM],
        out_specs=HBM,
        scratch_shapes=[
            pltpu.VMEM((rows_dev, width_f), F32),
            pltpu.VMEM((rows_dev, width_f), BF),
            pltpu.VMEM((count, width_f), BF),
            pltpu.SemaphoreType.DMA((chunks,)),
            pltpu.SemaphoreType.DMA((parts,)),
        ],
        compiler_params=pltpu.CompilerParams(vmem_limit_bytes=32 * 2**20),
    )(asked, pltpu.with_memory_space_constraint(features, pltpu.HBM))


def slice_grad(core, spread, d_hidden, active, rows, hidden, d_logits, own_ref, other_ref):
    half = own_ref.shape[0]
    units = d_hidden.shape[1]
    scattered = dot(spread[...], d_hidden).astype(BF)
    d_pre = jnp.where(active[...] > 0, scattered, jnp.zeros_like(scattered))
    total = dot(rows[...], d_pre)
    own_ref[:, :units] = total[:half]
    other_ref[:, :units] = total[half:].astype(BF)
    mine = hidden[:, pl.ds(pl.multiple_of(core * half, half), half)]
    other = hidden[:, pl.ds(pl.multiple_of((1 - core) * half, half), half)]
    own_ref[:, units:] = dot(mine, d_logits, 0, 0)
    other_ref[:, units:] = dot(other, d_logits, 0, 0).astype(BF)


def middle(parts, labels, hidden, w_twos, core, spread_t, active, rows_t):
    count = len(parts)
    targets, classes = parts[0].shape
    units = hidden.shape[1]
    half = units // 2

    def kernel(core_ref, *refs):
        part_refs, refs = refs[:count], refs[count:]
        labels_ref, hidden_ref = refs[:2]
        sources, refs = refs[2 : 5 + count], refs[5 + count :]
        own_ref, other_ref, d_logits_ref = refs[:3]
        d_hidden_refs, refs = refs[3 : 2 + count], refs[2 + count :]
        scratch, sems = refs[:-1], refs[-1]
        copies = [
            pltpu.make_async_copy(source, target, sems.at[i])
            for i, (source, target) in enumerate(zip(sources, scratch))
        ]
        for copy in copies:
            copy.start()
        logits = part_refs[0][...]
        for part in part_refs[1:]:
            logits += part[...].astype(F32)
        exponent = jnp.exp(logits)
        probability = exponent / jnp.sum(exponent, axis=1, keepdims=True)
        ids = lax.broadcasted_iota(jnp.int32, (targets, classes), 1)
        label = jnp.broadcast_to(labels_ref[...], (targets, targets)).T[:, :1]
        d_logits = (probability - (label == ids).astype(F32)).astype(BF)
        d_logits_ref[...] = d_logits
        copies[0].wait()
        d_first = dot(d_logits, scratch[0][...], 1, 1).astype(BF)
        for copy in copies[1:4]:
            copy.wait()
        slice_grad(
            core_ref[0],
            scratch[1],
            d_first,
            scratch[2],
            scratch[3],
            hidden_ref,
            d_logits,
            own_ref,
            other_ref,
        )
        for copy, w_two, out in zip(copies[4:], scratch[4:], d_hidden_refs):
            copy.wait()
            out[...] = dot(d_logits, w_two[...], 1, 1).astype(BF)

    moved = [w_twos[0], spread_t, active, rows_t, *w_twos[1:]]
    moved = [pltpu.with_memory_space_constraint(x, pltpu.HBM) for x in moved]
    return pl.pallas_call(
        kernel,
        out_shape=[
            jax.ShapeDtypeStruct((half, units + classes), F32),
            jax.ShapeDtypeStruct((half, units + classes), BF),
            jax.ShapeDtypeStruct((targets, classes), BF),
        ]
        + [jax.ShapeDtypeStruct((targets, units), BF)] * (count - 1),
        in_specs=[SMEM] + [VMEM] * (count + 2) + [HBM] * len(moved),
        out_specs=[VMEM] * (2 + count),
        scratch_shapes=[pltpu.VMEM(x.shape, BF) for x in moved]
        + [pltpu.SemaphoreType.DMA((len(moved),))],
        compiler_params=pltpu.CompilerParams(vmem_limit_bytes=24 * 2**20),
        cost_estimate=pl.CostEstimate(
            flops=2 * targets * classes * units * (count + 1),
            bytes_accessed=4 * 2**20,
            transcendentals=targets * classes,
        ),
    )(core, *parts, labels, hidden, *moved)


def forward(rows, w_ones, w_twos, spread, core):
    slots, width_f = rows.shape
    targets = spread.shape[0]
    units, classes = w_twos[0].shape
    half = width_f // 2
    block = 512
    count = len(w_ones)

    def kernel(core_ref, rows_ref, spread_ref, *refs):
        w_refs, refs = refs[: 2 * count], refs[2 * count :]
        active_refs, hidden_refs = refs[:count], refs[count : 2 * count]
        logits_ref, narrow_ref, turned_ref = refs[2 * count : 2 * count + 3]
        refs = refs[2 * count + 3 :]
        w_one_all, w_two_all, active_all, spread_all, turned, w_sems, out_sems, sem = refs

        def w_copy(i):
            target = w_one_all.at[i] if i < count else w_two_all.at[i - count]
            return pltpu.make_async_copy(w_refs[i], target, w_sems.at[i])

        for i in range(2 * count):
            w_copy(i).start()
        spread_copy = pltpu.make_async_copy(spread_ref, spread_all, sem)
        spread_copy.start()
        mine = pl.multiple_of(core_ref[0] * half, half)
        other = pl.multiple_of((1 - core_ref[0]) * half, half)

        @pl.loop(0, slots // block)
        def _(j):
            at = pl.ds(pl.multiple_of(j * block, block), block)
            flat = rows_ref[at, :].T
            turned[pl.ds(mine, half), at] = flat[:half]
            turned[pl.ds(other, half), at] = flat[half:]

        turned_copy = pltpu.make_async_copy(turned, turned_ref, out_sems.at[count])
        turned_copy.start()
        out_copies = [
            pltpu.make_async_copy(active_all.at[i], active_refs[i], out_sems.at[i])
            for i in range(count)
        ]
        spread_copy.wait()
        logits = jnp.zeros((targets, classes), F32)
        for i in range(count):
            w_copy(i).wait()
            active_all[i] = jnp.maximum(dot(rows_ref[...], w_one_all[i]), 0.0).astype(BF)
            out_copies[i].start()
            hidden = dot(spread_all[...], active_all[i]).astype(BF)
            hidden_refs[i][...] = hidden
            w_copy(count + i).wait()
            logits += dot(hidden, w_two_all[i])
        logits_ref[...] = logits
        narrow_ref[...] = logits.astype(BF)
        for copy in out_copies:
            copy.wait()
        turned_copy.wait()

    w_all = [pltpu.with_memory_space_constraint(x, pltpu.HBM) for x in (*w_ones, *w_twos)]
    return pl.pallas_call(
        kernel,
        out_shape=[pltpu.HBM((slots, units), BF)] * count
        + [jax.ShapeDtypeStruct((targets, units), BF)] * count
        + [
            jax.ShapeDtypeStruct((targets, classes), F32),
            jax.ShapeDtypeStruct((targets, classes), BF),
            pltpu.HBM((width_f, slots), BF),
        ],
        in_specs=[SMEM, VMEM, HBM] + [HBM] * (2 * count),
        out_specs=[HBM] * count + [VMEM] * (count + 2) + [HBM],
        scratch_shapes=[
            pltpu.VMEM((count, width_f, units), BF),
            pltpu.VMEM((count, units, classes), BF),
            pltpu.VMEM((count, slots, units), BF),
            pltpu.VMEM((targets, slots), BF),
            pltpu.VMEM((width_f, slots), BF),
            pltpu.SemaphoreType.DMA((2 * count,)),
            pltpu.SemaphoreType.DMA((count + 1,)),
            pltpu.SemaphoreType.DMA,
        ],
        compiler_params=pltpu.CompilerParams(vmem_limit_bytes=32 * 2**20),
        cost_estimate=pl.CostEstimate(
            flops=2 * count * slots * units * (width_f + targets),
            bytes_accessed=2 * slots * (width_f + units + targets),
            transcendentals=0,
        ),
    )(core, rows, pltpu.with_memory_space_constraint(spread, pltpu.HBM), *w_all)


def backward(core, spread_t, d_hidden, active, rows_t, hidden, d_logits, earlier):
    units = d_hidden.shape[1]
    half = rows_t.shape[0] // 2
    width = units + d_logits.shape[1]

    def kernel(core_ref, spread_ref, d_hidden_ref, active_ref, rows_ref, hidden_ref, logits_ref, *refs):
        slice_grad(
            core_ref[0],
            spread_ref,
            d_hidden_ref[...],
            active_ref,
            rows_ref,
            hidden_ref,
            logits_ref[...],
            *refs[-2:],
        )

    return pl.pallas_call(
        kernel,
        out_shape=[
            jax.ShapeDtypeStruct((half, width), F32),
            jax.ShapeDtypeStruct((half, width), BF),
        ],
        in_specs=[SMEM] + [VMEM] * 6 + [pl.BlockSpec(memory_space=pl.ANY)] * len(earlier),
        out_specs=[VMEM] * 2,
        compiler_params=pltpu.CompilerParams(vmem_limit_bytes=24 * 2**20),
        cost_estimate=pl.CostEstimate(
            flops=2 * units, bytes_accessed=2 * units, transcendentals=0
        ),
    )(core, spread_t, d_hidden, active, rows_t, hidden, d_logits, *earlier)


def outputs(own, other, core, units):
    half, width = own.shape

    def kernel(core_ref, own_ref, other_ref, one_ref, two_ref, wide, sems):
        copies = []
        for i, ref in enumerate((own_ref, other_ref)):
            wide[i] = ref[...].astype(F32)
            place = core_ref[0] if i == 0 else 1 - core_ref[0]
            at = pl.ds(pl.multiple_of(place * half, half), half)
            for j, (out, first) in enumerate(((one_ref, 0), (two_ref, units))):
                source = wide.at[i, :, pl.ds(first, out.shape[1])]
                copies.append(pltpu.make_async_copy(source, out.at[at, :], sems.at[2 * i + j]))
                copies[-1].start()
        for copy in copies:
            copy.wait()

    return pl.pallas_call(
        kernel,
        out_shape=[pltpu.HBM((2 * half, units), F32), pltpu.HBM((2 * half, width - units), F32)],
        in_specs=[SMEM, VMEM, VMEM],
        out_specs=[HBM, HBM],
        scratch_shapes=[pltpu.VMEM((2, half, width), F32), pltpu.SemaphoreType.DMA((4,))],
        compiler_params=pltpu.CompilerParams(vmem_limit_bytes=24 * 2**20),
    )(core, own, other)


def body(features, nbr_page, nbr_weight, labels, w_one, w_two):
    rows_dev, width_f = features.shape
    targets, width_k = nbr_page.shape
    own_n, col_n, mlp_n = (lax.axis_size(a) for a in ("own", "col", "mlp"))
    owners = own_n * col_n
    entries = targets * width_k
    capacity = 2 * entries // owners
    share = capacity // mlp_n
    units, classes = w_two.shape
    me = lax.axis_index("mlp")
    core = lax.axis_index("col") % 2

    def to_mlp(x, step):
        return lax.ppermute(x, "mlp", [(j, (j + step) % mlp_n) for j in range(mlp_n)])

    steps = (2, 1, 3, 0)
    w_ones, w_twos = {0: w_one}, {0: w_two}
    for step in steps[:-1]:
        w_ones[step] = to_mlp(w_one, -step)
        w_twos[step] = to_mlp(w_two, -step)
    w_ones, w_twos = lax.optimization_barrier((w_ones, w_twos))

    requests, slot_ids = slots_of(nbr_page.T, rows_dev, owners, capacity)
    asked = exchange(requests, ("own", "col"))
    asked = lax.dynamic_slice_in_dim(asked, me * share, share, 1).reshape(-1)
    fetched = gather(features, asked)
    fetched = fetched.reshape(owners, share, width_f)
    received = exchange(fetched, ("own", "col")).reshape(owners * share, width_f)

    slot_ids = slot_ids.T
    owner_range = jnp.arange(owners, dtype=jnp.int32)
    t_range = jnp.arange(targets)
    matches = (nbr_page // rows_dev)[:, :, None] == owner_range[None, None, :]
    by_owner = matches.astype(BF).reshape(entries, owners)
    in_slot = slot_ids[:, :, None] == jnp.arange(capacity, dtype=jnp.int32)[None, None, :]

    def place(values):
        spread_out = jnp.where(in_slot, values.astype(BF)[:, :, None], jnp.zeros((), BF))
        return dot(by_owner, spread_out.reshape(entries, capacity), 0, 0)

    slot_weight = place(nbr_weight)
    slot_target = place(jnp.broadcast_to(t_range[:, None], (targets, width_k)))

    my_weight = lax.dynamic_slice_in_dim(slot_weight, me * share, share, 1).reshape(1, -1)
    my_target = lax.dynamic_slice_in_dim(slot_target, me * share, share, 1).reshape(1, -1)
    spread = jnp.where(
        my_target.astype(jnp.int32) == t_range[:, None].astype(jnp.int32), my_weight, 0.0
    ).astype(BF)
    spread, spread_t = lax.optimization_barrier((spread, spread.T))

    core_id = core.reshape(1)
    half = width_f // 2
    out = forward(
        received, [w_ones[s] for s in steps], [w_twos[s] for s in steps], spread, core_id
    )
    active, hidden = dict(zip(steps, out)), dict(zip(steps, out[mlp_n:]))
    part, narrow, rows_t = out[2 * mlp_n :]
    parts = [part] + [to_mlp(narrow, step) for step in steps[:-1]]

    pairs = [(i, i ^ 1) for i in range(col_n)]

    def partner(x):
        return lax.ppermute(x, "col", pairs)

    mine, other, d_logits, *d_hidden = middle(
        parts,
        labels[None],
        hidden[2],
        [w_twos[s] for s in steps],
        core_id,
        spread_t,
        active[2],
        rows_t,
    )
    far = (mine + partner(other).astype(F32)).astype(BF)
    far = (far[: half // 2], far[half // 2 :])
    upward, downward = to_mlp(far[0], 1), to_mlp(far[1], -1)
    near = {}
    for step in (1, 0, 3):
        i = steps.index(step) - 1
        earlier = () if step == 1 else far if step == 0 else (near[1],)
        mine, other = backward(
            core_id, spread_t, d_hidden[i], active[step], rows_t, hidden[step], d_logits, earlier
        )
        near[step] = mine + partner(other).astype(F32)
    top, bottom = near[1][: half // 2], near[1][half // 2 :]
    near[1] = jnp.concatenate([top + upward.astype(F32), bottom], axis=0).astype(BF)
    top, bottom = near[3][: half // 2], near[3][half // 2 :]
    near[3] = jnp.concatenate([top, bottom + downward.astype(F32)], axis=0).astype(BF)
    both = near[0] + to_mlp(near[1], 1).astype(F32) + to_mlp(near[3], -1).astype(F32)
    both = both.astype(BF)
    chips = owners // 2
    groups = [[2 * i + c for i in range(chips)] for c in (0, 1)]
    width = units + classes
    both = exchange(both.reshape(chips, half // chips, width), ("own", "col"), groups)
    both = jnp.sum(both.astype(F32), axis=0).astype(BF)
    both = jnp.broadcast_to(both[None], (chips, half // chips, width))
    both = exchange(both, ("own", "col"), groups).reshape(half, width)
    other = partner(both)
    return tuple(outputs(both, other, core_id, units))


def solution(mesh):
    placed = (
        P(("own", "col"), None),
        P(("own", "col"), None),
        P(("own", "col"), None),
        P(("own", "col")),
        P(None, "mlp"),
        P("mlp", None),
    )
    return jax.shard_map(
        body,
        mesh=mesh,
        in_specs=placed,
        out_specs=(P(None, "mlp"), P("mlp", None)),
        check_vma=False,
    )
```

```python
import jax
import jax.numpy as jnp
from jax import lax
from jax.experimental import pallas as pl
from jax.experimental.pallas import tpu as pltpu
from jax.sharding import PartitionSpec as P

BF = jnp.bfloat16
F32 = jnp.float32


def dot(a, b, ca=1, cb=0):
    return lax.dot_general(a, b, (((ca,), (cb,)), ((), ())), preferred_element_type=F32)


def exchange(x, axes, groups=None):
    return lax.all_to_all(
        x, axes, split_axis=0, concat_axis=0, tiled=True, axis_index_groups=groups
    )


VMEM = pl.BlockSpec(memory_space=pltpu.VMEM)
SMEM = pl.BlockSpec(memory_space=pltpu.SMEM)
HBM = pl.BlockSpec(memory_space=pltpu.HBM)


def slots_of(page_t, rows_dev, owners, capacity):
    width_k, targets = page_t.shape
    shift = rows_dev.bit_length() - 1
    low_bits = 6
    low_mask = (1 << low_bits) - 1

    def kernel(page_ref, request_ref, slot_ref, lhs, rhs):
        page = page_ref[...]
        owner = lax.shift_right_logical(page, jnp.int32(shift))
        row = page & (rows_dev - 1)
        high = lax.shift_right_logical(row, jnp.int32(low_bits)).astype(F32)
        low = (row & low_mask).astype(F32)
        owner_id = lax.broadcasted_iota(jnp.int32, (owners, targets), 0)
        count = jnp.zeros((owners, targets), F32)
        for k in range(width_k):
            match = (owner[k : k + 1] == owner_id).astype(F32)
            count += match
            lhs[:, k * targets : (k + 1) * targets] = match.astype(BF)
        count = count.astype(BF)

        def before(size):
            first = lax.broadcasted_iota(jnp.int32, (size, size), 0)
            return first, lax.broadcasted_iota(jnp.int32, (size, size), 1)

        first, second = before(targets)
        earlier = dot(count, (first < second).astype(F32).astype(BF))
        first, second = before(owners)
        smaller = dot((second < first).astype(F32).astype(BF), count)
        start = earlier - smaller
        slot_id = lax.broadcasted_iota(jnp.int32, (capacity, targets), 0)
        for k in range(width_k):
            mine = jnp.where(owner[k : k + 1] == owner_id, start, 0.0)
            slot = jnp.sum(mine, axis=0, keepdims=True).astype(jnp.int32) + k
            slot_ref[k : k + 1] = slot
            hit = slot == slot_id
            at = slice(k * targets, (k + 1) * targets)
            rhs[:capacity, at] = jnp.where(hit, high[k : k + 1], 0.0).astype(BF)
            rhs[capacity:, at] = jnp.where(hit, low[k : k + 1], 0.0).astype(BF)
        both = dot(lhs[...], rhs[...], 1, 1)
        request = both[:, :capacity] * float(1 << low_bits) + both[:, capacity:]
        request_ref[...] = request.astype(jnp.int32)

    entries = width_k * targets
    return pl.pallas_call(
        kernel,
        out_shape=[
            jax.ShapeDtypeStruct((owners, capacity), jnp.int32),
            jax.ShapeDtypeStruct((width_k, targets), jnp.int32),
        ],
        in_specs=[VMEM],
        out_specs=[VMEM] * 2,
        scratch_shapes=[
            pltpu.VMEM((owners, entries), BF),
            pltpu.VMEM((2 * capacity, entries), BF),
        ],
        compiler_params=pltpu.CompilerParams(vmem_limit_bytes=24 * 2**20),
    )(page_t)


def gather(features, asked):
    rows_dev, width_f = features.shape
    (count,) = asked.shape
    group = 32
    parts = 4
    chunk = 512
    chunks = rows_dev // chunk

    def kernel(asked_ref, features_ref, out_ref, wide, narrow, out, sems, out_sems):
        copies = []
        for i in range(chunks):
            at = pl.ds(i * chunk, chunk)
            copies.append(
                pltpu.make_async_copy(features_ref.at[at, :], narrow.at[at, :], sems.at[i])
            )
        for copy in copies:
            copy.start()
        for i, copy in enumerate(copies):
            copy.wait()
            at = pl.ds(i * chunk, chunk)
            wide[at, :] = narrow[at, :].astype(F32)

        copies = []
        part = count // parts
        for p in range(parts):

            @pl.loop(0, part // group)
            def _(i, p=p):
                base = pl.multiple_of(p * part + i * group, group)
                rows = [wide[pl.ds(asked_ref[base + j], 1), :] for j in range(group)]
                out[pl.ds(base, group), :] = jnp.concatenate(rows, axis=0).astype(BF)

            at = pl.ds(p * part, part)
            copies.append(pltpu.make_async_copy(out.at[at, :], out_ref.at[at, :], out_sems.at[p]))
            copies[-1].start()
        for copy in copies:
            copy.wait()

    return pl.pallas_call(
        kernel,
        out_shape=pltpu.HBM((count, width_f), BF),
        in_specs=[SMEM, HBM],
        out_specs=HBM,
        scratch_shapes=[
            pltpu.VMEM((rows_dev, width_f), F32),
            pltpu.VMEM((rows_dev, width_f), BF),
            pltpu.VMEM((count, width_f), BF),
            pltpu.SemaphoreType.DMA((chunks,)),
            pltpu.SemaphoreType.DMA((parts,)),
        ],
        compiler_params=pltpu.CompilerParams(vmem_limit_bytes=32 * 2**20),
    )(asked, pltpu.with_memory_space_constraint(features, pltpu.HBM))


def slice_grad(
    core, spread, d_hidden, active, rows, hidden, d_logits, own_ref, other_ref, waits=(None,) * 3
):
    def arrived(i):
        if waits[i] is not None:
            waits[i].wait()

    half = own_ref.shape[0]
    units = d_hidden.shape[1]
    mine = hidden[:, pl.ds(pl.multiple_of(core * half, half), half)]
    other = hidden[:, pl.ds(pl.multiple_of((1 - core) * half, half), half)]
    own_ref[:, units:] = dot(mine, d_logits, 0, 0)
    other_ref[:, units:] = dot(other, d_logits, 0, 0).astype(BF)
    arrived(0)
    scattered = dot(spread[...], d_hidden).astype(BF)
    arrived(1)
    d_pre = jnp.where(active[...] > 0, scattered, jnp.zeros_like(scattered))
    arrived(2)
    total = dot(rows[...], d_pre)
    own_ref[:, :units] = total[:half]
    other_ref[:, :units] = total[half:].astype(BF)


def middle(parts, labels, hidden, w_twos, core, spread_t, active, rows_t):
    count = len(parts)
    targets, classes = parts[0].shape
    units = hidden.shape[1]
    half = units // 2

    def kernel(core_ref, *refs):
        part_refs, refs = refs[:count], refs[count:]
        labels_ref, hidden_ref = refs[:2]
        sources, refs = refs[2 : 5 + count], refs[5 + count :]
        own_ref, other_ref, d_logits_ref = refs[:3]
        d_hidden_refs, refs = refs[3 : 2 + count], refs[2 + count :]
        scratch, sems = refs[:-1], refs[-1]
        copies = [
            pltpu.make_async_copy(source, target, sems.at[i])
            for i, (source, target) in enumerate(zip(sources, scratch))
        ]
        for copy in copies:
            copy.start()
        logits = part_refs[0][...]
        for part in part_refs[1:]:
            logits += part[...].astype(F32)
        exponent = jnp.exp(logits)
        probability = exponent / jnp.sum(exponent, axis=1, keepdims=True)
        ids = lax.broadcasted_iota(jnp.int32, (targets, classes), 1)
        label = jnp.broadcast_to(labels_ref[...], (targets, targets)).T[:, :1]
        d_logits = (probability - (label == ids).astype(F32)).astype(BF)
        d_logits_ref[...] = d_logits
        copies[0].wait()
        d_first = dot(d_logits, scratch[0][...], 1, 1).astype(BF)
        slice_grad(
            core_ref[0],
            scratch[1],
            d_first,
            scratch[2],
            scratch[3],
            hidden_ref,
            d_logits,
            own_ref,
            other_ref,
            copies[1:4],
        )
        for copy, w_two, out in zip(copies[4:], scratch[4:], d_hidden_refs):
            copy.wait()
            out[...] = dot(d_logits, w_two[...], 1, 1).astype(BF)

    moved = [w_twos[0], spread_t, active, rows_t, *w_twos[1:]]
    moved = [pltpu.with_memory_space_constraint(x, pltpu.HBM) for x in moved]
    return pl.pallas_call(
        kernel,
        out_shape=[
            jax.ShapeDtypeStruct((half, units + classes), F32),
            jax.ShapeDtypeStruct((half, units + classes), BF),
            jax.ShapeDtypeStruct((targets, classes), BF),
        ]
        + [jax.ShapeDtypeStruct((targets, units), BF)] * (count - 1),
        in_specs=[SMEM] + [VMEM] * (count + 2) + [HBM] * len(moved),
        out_specs=[VMEM] * (2 + count),
        scratch_shapes=[pltpu.VMEM(x.shape, BF) for x in moved]
        + [pltpu.SemaphoreType.DMA((len(moved),))],
        compiler_params=pltpu.CompilerParams(vmem_limit_bytes=24 * 2**20),
        cost_estimate=pl.CostEstimate(
            flops=2 * targets * classes * units * (count + 1),
            bytes_accessed=4 * 2**20,
            transcendentals=targets * classes,
        ),
    )(core, *parts, labels, hidden, *moved)


def forward(rows, w_ones, w_twos, spread, core):
    slots, width_f = rows.shape
    targets = spread.shape[0]
    units, classes = w_twos[0].shape
    half = width_f // 2
    block = 512
    count = len(w_ones)

    def kernel(core_ref, rows_ref, spread_ref, *refs):
        w_refs, refs = refs[: 2 * count], refs[2 * count :]
        active_refs, hidden_refs = refs[:count], refs[count : 2 * count]
        logits_ref, narrow_ref, turned_ref = refs[2 * count : 2 * count + 3]
        refs = refs[2 * count + 3 :]
        w_one_all, w_two_all, active_all, spread_all, turned, w_sems, out_sems, sem = refs

        def w_copy(i):
            target = w_one_all.at[i] if i < count else w_two_all.at[i - count]
            return pltpu.make_async_copy(w_refs[i], target, w_sems.at[i])

        for i in range(2 * count):
            w_copy(i).start()
        spread_copy = pltpu.make_async_copy(spread_ref, spread_all, sem)
        spread_copy.start()
        mine = pl.multiple_of(core_ref[0] * half, half)
        other = pl.multiple_of((1 - core_ref[0]) * half, half)

        @pl.loop(0, slots // block)
        def _(j):
            at = pl.ds(pl.multiple_of(j * block, block), block)
            flat = rows_ref[at, :].T
            turned[pl.ds(mine, half), at] = flat[:half]
            turned[pl.ds(other, half), at] = flat[half:]

        turned_copy = pltpu.make_async_copy(turned, turned_ref, out_sems.at[count])
        turned_copy.start()
        out_copies = [
            pltpu.make_async_copy(active_all.at[i], active_refs[i], out_sems.at[i])
            for i in range(count)
        ]
        spread_copy.wait()
        logits = jnp.zeros((targets, classes), F32)
        for i in range(count):
            w_copy(i).wait()
            active_all[i] = jnp.maximum(dot(rows_ref[...], w_one_all[i]), 0.0).astype(BF)
            out_copies[i].start()
            hidden = dot(spread_all[...], active_all[i]).astype(BF)
            hidden_refs[i][...] = hidden
            w_copy(count + i).wait()
            logits += dot(hidden, w_two_all[i])
        logits_ref[...] = logits
        narrow_ref[...] = logits.astype(BF)
        for copy in out_copies:
            copy.wait()
        turned_copy.wait()

    w_all = [pltpu.with_memory_space_constraint(x, pltpu.HBM) for x in (*w_ones, *w_twos)]
    return pl.pallas_call(
        kernel,
        out_shape=[pltpu.HBM((slots, units), BF)] * count
        + [jax.ShapeDtypeStruct((targets, units), BF)] * count
        + [
            jax.ShapeDtypeStruct((targets, classes), F32),
            jax.ShapeDtypeStruct((targets, classes), BF),
            pltpu.HBM((width_f, slots), BF),
        ],
        in_specs=[SMEM, VMEM, HBM] + [HBM] * (2 * count),
        out_specs=[HBM] * count + [VMEM] * (count + 2) + [HBM],
        scratch_shapes=[
            pltpu.VMEM((count, width_f, units), BF),
            pltpu.VMEM((count, units, classes), BF),
            pltpu.VMEM((count, slots, units), BF),
            pltpu.VMEM((targets, slots), BF),
            pltpu.VMEM((width_f, slots), BF),
            pltpu.SemaphoreType.DMA((2 * count,)),
            pltpu.SemaphoreType.DMA((count + 1,)),
            pltpu.SemaphoreType.DMA,
        ],
        compiler_params=pltpu.CompilerParams(vmem_limit_bytes=32 * 2**20),
        cost_estimate=pl.CostEstimate(
            flops=2 * count * slots * units * (width_f + targets),
            bytes_accessed=2 * slots * (width_f + units + targets),
            transcendentals=0,
        ),
    )(core, rows, pltpu.with_memory_space_constraint(spread, pltpu.HBM), *w_all)


def backward(core, spread_t, d_hidden, active, rows_t, hidden, d_logits, earlier):
    units = d_hidden.shape[1]
    half = rows_t.shape[0] // 2
    width = units + d_logits.shape[1]

    def kernel(core_ref, spread_ref, d_hidden_ref, active_ref, rows_ref, hidden_ref, logits_ref, *refs):
        slice_grad(
            core_ref[0],
            spread_ref,
            d_hidden_ref[...],
            active_ref,
            rows_ref,
            hidden_ref,
            logits_ref[...],
            *refs[-2:],
        )

    return pl.pallas_call(
        kernel,
        out_shape=[
            jax.ShapeDtypeStruct((half, width), F32),
            jax.ShapeDtypeStruct((half, width), BF),
        ],
        in_specs=[SMEM] + [VMEM] * 6 + [pl.BlockSpec(memory_space=pl.ANY)] * len(earlier),
        out_specs=[VMEM] * 2,
        compiler_params=pltpu.CompilerParams(vmem_limit_bytes=24 * 2**20),
        cost_estimate=pl.CostEstimate(
            flops=2 * units, bytes_accessed=2 * units, transcendentals=0
        ),
    )(core, spread_t, d_hidden, active, rows_t, hidden, d_logits, *earlier)


def outputs(own, other, core, units):
    half, width = own.shape

    def kernel(core_ref, own_ref, other_ref, one_ref, two_ref, wide, sems):
        copies = []
        for i, ref in enumerate((own_ref, other_ref)):
            wide[i] = ref[...].astype(F32)
            place = core_ref[0] if i == 0 else 1 - core_ref[0]
            at = pl.ds(pl.multiple_of(place * half, half), half)
            for j, (out, first) in enumerate(((one_ref, 0), (two_ref, units))):
                source = wide.at[i, :, pl.ds(first, out.shape[1])]
                copies.append(pltpu.make_async_copy(source, out.at[at, :], sems.at[2 * i + j]))
                copies[-1].start()
        for copy in copies:
            copy.wait()

    return pl.pallas_call(
        kernel,
        out_shape=[pltpu.HBM((2 * half, units), F32), pltpu.HBM((2 * half, width - units), F32)],
        in_specs=[SMEM, VMEM, VMEM],
        out_specs=[HBM, HBM],
        scratch_shapes=[pltpu.VMEM((2, half, width), F32), pltpu.SemaphoreType.DMA((4,))],
        compiler_params=pltpu.CompilerParams(vmem_limit_bytes=24 * 2**20),
    )(core, own, other)


def body(features, nbr_page, nbr_weight, labels, w_one, w_two):
    rows_dev, width_f = features.shape
    targets, width_k = nbr_page.shape
    own_n, col_n, mlp_n = (lax.axis_size(a) for a in ("own", "col", "mlp"))
    owners = own_n * col_n
    entries = targets * width_k
    capacity = 2 * entries // owners
    share = capacity // mlp_n
    units, classes = w_two.shape
    me = lax.axis_index("mlp")
    core = lax.axis_index("col") % 2

    def to_mlp(x, step):
        return lax.ppermute(x, "mlp", [(j, (j + step) % mlp_n) for j in range(mlp_n)])

    steps = (2, 1, 3, 0)
    w_ones, w_twos = {0: w_one}, {0: w_two}
    for step in steps[:-1]:
        w_ones[step] = to_mlp(w_one, -step)
        w_twos[step] = to_mlp(w_two, -step)
    w_ones, w_twos = lax.optimization_barrier((w_ones, w_twos))

    requests, slot_ids = slots_of(nbr_page.T, rows_dev, owners, capacity)
    asked = exchange(requests, ("own", "col"))
    asked = lax.dynamic_slice_in_dim(asked, me * share, share, 1).reshape(-1)
    fetched = gather(features, asked)
    fetched = fetched.reshape(owners, share, width_f)
    received = exchange(fetched, ("own", "col")).reshape(owners * share, width_f)

    slot_ids = slot_ids.T
    owner_range = jnp.arange(owners, dtype=jnp.int32)
    t_range = jnp.arange(targets)
    matches = (nbr_page // rows_dev)[:, :, None] == owner_range[None, None, :]
    by_owner = matches.astype(BF).reshape(entries, owners)
    in_slot = slot_ids[:, :, None] == jnp.arange(capacity, dtype=jnp.int32)[None, None, :]

    def place(values):
        spread_out = jnp.where(in_slot, values.astype(BF)[:, :, None], jnp.zeros((), BF))
        return dot(by_owner, spread_out.reshape(entries, capacity), 0, 0)

    slot_weight = place(nbr_weight)
    slot_target = place(jnp.broadcast_to(t_range[:, None], (targets, width_k)))

    my_weight = lax.dynamic_slice_in_dim(slot_weight, me * share, share, 1).reshape(1, -1)
    my_target = lax.dynamic_slice_in_dim(slot_target, me * share, share, 1).reshape(1, -1)
    spread = jnp.where(
        my_target.astype(jnp.int32) == t_range[:, None].astype(jnp.int32), my_weight, 0.0
    ).astype(BF)
    spread, spread_t = lax.optimization_barrier((spread, spread.T))

    core_id = core.reshape(1)
    half = width_f // 2
    out = forward(
        received, [w_ones[s] for s in steps], [w_twos[s] for s in steps], spread, core_id
    )
    active, hidden = dict(zip(steps, out)), dict(zip(steps, out[mlp_n:]))
    part, narrow, rows_t = out[2 * mlp_n :]
    parts = [part] + [to_mlp(narrow, step) for step in steps[:-1]]

    pairs = [(i, i ^ 1) for i in range(col_n)]

    def partner(x):
        return lax.ppermute(x, "col", pairs)

    mine, other, d_logits, *d_hidden = middle(
        parts,
        labels[None],
        hidden[2],
        [w_twos[s] for s in steps],
        core_id,
        spread_t,
        active[2],
        rows_t,
    )
    far = (mine + partner(other).astype(F32)).astype(BF)
    far = (far[: half // 2], far[half // 2 :])
    upward, downward = to_mlp(far[0], 1), to_mlp(far[1], -1)
    near = {}
    for step in (1, 0, 3):
        i = steps.index(step) - 1
        earlier = far if step == 1 else (near[1],) if step == 0 else ()
        mine, other = backward(
            core_id, spread_t, d_hidden[i], active[step], rows_t, hidden[step], d_logits, earlier
        )
        near[step] = mine + partner(other).astype(F32)
    top, bottom = near[1][: half // 2], near[1][half // 2 :]
    near[1] = jnp.concatenate([top + upward.astype(F32), bottom], axis=0).astype(BF)
    top, bottom = near[3][: half // 2], near[3][half // 2 :]
    near[3] = jnp.concatenate([top, bottom + downward.astype(F32)], axis=0).astype(BF)
    both = near[0] + to_mlp(near[1], 1).astype(F32) + to_mlp(near[3], -1).astype(F32)
    both = both.astype(BF)
    chips = owners // 2
    groups = [[2 * i + c for i in range(chips)] for c in (0, 1)]
    width = units + classes
    both = exchange(both.reshape(chips, half // chips, width), ("own", "col"), groups)
    both = jnp.sum(both.astype(F32), axis=0).astype(BF)
    both = jnp.broadcast_to(both[None], (chips, half // chips, width))
    both = exchange(both, ("own", "col"), groups).reshape(half, width)
    other = partner(both)
    return tuple(outputs(both, other, core_id, units))


def solution(mesh):
    placed = (
        P(("own", "col"), None),
        P(("own", "col"), None),
        P(("own", "col"), None),
        P(("own", "col")),
        P(None, "mlp"),
        P("mlp", None),
    )
    return jax.shard_map(
        body,
        mesh=mesh,
        in_specs=placed,
        out_specs=(P(None, "mlp"), P("mlp", None)),
        check_vma=False,
    )
```

```python
import jax
import jax.numpy as jnp
from jax import lax
from jax.experimental import pallas as pl
from jax.experimental.pallas import tpu as pltpu
from jax.sharding import PartitionSpec as P

BF = jnp.bfloat16
F32 = jnp.float32


def dot(a, b, ca=1, cb=0):
    return lax.dot_general(a, b, (((ca,), (cb,)), ((), ())), preferred_element_type=F32)


def exchange(x, axes, groups=None):
    return lax.all_to_all(
        x, axes, split_axis=0, concat_axis=0, tiled=True, axis_index_groups=groups
    )


VMEM = pl.BlockSpec(memory_space=pltpu.VMEM)
SMEM = pl.BlockSpec(memory_space=pltpu.SMEM)
HBM = pl.BlockSpec(memory_space=pltpu.HBM)


def slots_of(page_t, rows_dev, owners, capacity):
    width_k, targets = page_t.shape
    shift = rows_dev.bit_length() - 1
    low_bits = 6
    low_mask = (1 << low_bits) - 1

    def kernel(page_ref, request_ref, slot_ref, lhs, rhs):
        page = page_ref[...]
        owner = lax.shift_right_logical(page, jnp.int32(shift))
        row = page & (rows_dev - 1)
        high = lax.shift_right_logical(row, jnp.int32(low_bits)).astype(F32)
        low = (row & low_mask).astype(F32)
        owner_id = lax.broadcasted_iota(jnp.int32, (owners, targets), 0)
        count = jnp.zeros((owners, targets), F32)
        for k in range(width_k):
            match = (owner[k : k + 1] == owner_id).astype(F32)
            count += match
            lhs[:, k * targets : (k + 1) * targets] = match.astype(BF)
        count = count.astype(BF)

        def before(size):
            first = lax.broadcasted_iota(jnp.int32, (size, size), 0)
            return first, lax.broadcasted_iota(jnp.int32, (size, size), 1)

        first, second = before(targets)
        earlier = dot(count, (first < second).astype(F32).astype(BF))
        first, second = before(owners)
        smaller = dot((second < first).astype(F32).astype(BF), count)
        start = earlier - smaller
        slot_id = lax.broadcasted_iota(jnp.int32, (capacity, targets), 0)
        for k in range(width_k):
            mine = jnp.where(owner[k : k + 1] == owner_id, start, 0.0)
            slot = jnp.sum(mine, axis=0, keepdims=True).astype(jnp.int32) + k
            slot_ref[k : k + 1] = slot
            hit = slot == slot_id
            at = slice(k * targets, (k + 1) * targets)
            rhs[:capacity, at] = jnp.where(hit, high[k : k + 1], 0.0).astype(BF)
            rhs[capacity:, at] = jnp.where(hit, low[k : k + 1], 0.0).astype(BF)
        both = dot(lhs[...], rhs[...], 1, 1)
        request = both[:, :capacity] * float(1 << low_bits) + both[:, capacity:]
        request_ref[...] = request.astype(jnp.int32)

    entries = width_k * targets
    return pl.pallas_call(
        kernel,
        out_shape=[
            jax.ShapeDtypeStruct((owners, capacity), jnp.int32),
            jax.ShapeDtypeStruct((width_k, targets), jnp.int32),
        ],
        in_specs=[VMEM],
        out_specs=[VMEM] * 2,
        scratch_shapes=[
            pltpu.VMEM((owners, entries), BF),
            pltpu.VMEM((2 * capacity, entries), BF),
        ],
        compiler_params=pltpu.CompilerParams(vmem_limit_bytes=24 * 2**20),
    )(page_t)


def gather(features, asked):
    rows_dev, width_f = features.shape
    (count,) = asked.shape
    group = 32
    parts = 4
    chunk = 512
    chunks = rows_dev // chunk

    def kernel(asked_ref, features_ref, out_ref, wide, narrow, out, sems, out_sems):
        copies = []
        for i in range(chunks):
            at = pl.ds(i * chunk, chunk)
            copies.append(
                pltpu.make_async_copy(features_ref.at[at, :], narrow.at[at, :], sems.at[i])
            )
        for copy in copies:
            copy.start()
        for i, copy in enumerate(copies):
            copy.wait()
            at = pl.ds(i * chunk, chunk)
            wide[at, :] = narrow[at, :].astype(F32)

        copies = []
        part = count // parts
        for p in range(parts):

            @pl.loop(0, part // group)
            def _(i, p=p):
                base = pl.multiple_of(p * part + i * group, group)
                rows = [wide[pl.ds(asked_ref[base + j], 1), :] for j in range(group)]
                out[pl.ds(base, group), :] = jnp.concatenate(rows, axis=0).astype(BF)

            at = pl.ds(p * part, part)
            copies.append(pltpu.make_async_copy(out.at[at, :], out_ref.at[at, :], out_sems.at[p]))
            copies[-1].start()
        for copy in copies:
            copy.wait()

    return pl.pallas_call(
        kernel,
        out_shape=pltpu.HBM((count, width_f), BF),
        in_specs=[SMEM, HBM],
        out_specs=HBM,
        scratch_shapes=[
            pltpu.VMEM((rows_dev, width_f), F32),
            pltpu.VMEM((rows_dev, width_f), BF),
            pltpu.VMEM((count, width_f), BF),
            pltpu.SemaphoreType.DMA((chunks,)),
            pltpu.SemaphoreType.DMA((parts,)),
        ],
        compiler_params=pltpu.CompilerParams(vmem_limit_bytes=32 * 2**20),
    )(asked, pltpu.with_memory_space_constraint(features, pltpu.HBM))


def slice_grad(
    core, spread, d_hidden, active, rows, hidden, d_logits, own_ref, other_ref, waits=(None,) * 3
):
    def arrived(i):
        if waits[i] is not None:
            waits[i].wait()

    half = own_ref.shape[0]
    units = d_hidden.shape[1]
    mine = hidden[:, pl.ds(pl.multiple_of(core * half, half), half)]
    other = hidden[:, pl.ds(pl.multiple_of((1 - core) * half, half), half)]
    own_ref[:, units:] = dot(mine, d_logits, 0, 0)
    other_ref[:, units:] = dot(other, d_logits, 0, 0).astype(BF)
    arrived(0)
    scattered = dot(spread[...], d_hidden).astype(BF)
    arrived(1)
    d_pre = jnp.where(active[...] > 0, scattered, jnp.zeros_like(scattered))
    arrived(2)
    total = dot(rows[...], d_pre)
    own_ref[:, :units] = total[:half]
    other_ref[:, :units] = total[half:].astype(BF)


def middle(parts, labels, hidden, w_twos, core, spread_t, active, rows_t):
    count = len(parts)
    targets, classes = parts[0].shape
    units = hidden.shape[1]
    half = units // 2

    def kernel(core_ref, *refs):
        part_refs, refs = refs[:count], refs[count:]
        labels_ref, hidden_ref = refs[:2]
        spread_ref, rows_ref = refs[2:4]
        sources, refs = refs[4 : 5 + count], refs[5 + count :]
        own_ref, other_ref, d_logits_ref = refs[:3]
        d_hidden_refs = refs[3 : 2 + count]
        logits = part_refs[0][...]
        for part in part_refs[1:]:
            logits += part[...].astype(F32)
        exponent = jnp.exp(logits)
        probability = exponent / jnp.sum(exponent, axis=1, keepdims=True)
        ids = lax.broadcasted_iota(jnp.int32, (targets, classes), 1)
        label = jnp.broadcast_to(labels_ref[...], (targets, targets)).T[:, :1]
        d_logits = (probability - (label == ids).astype(F32)).astype(BF)
        d_logits_ref[...] = d_logits
        d_first = dot(d_logits, sources[0][...], 1, 1).astype(BF)
        slice_grad(
            core_ref[0],
            spread_ref,
            d_first,
            sources[1],
            rows_ref,
            hidden_ref,
            d_logits,
            own_ref,
            other_ref,
        )
        for w_two, out in zip(sources[2:], d_hidden_refs):
            out[...] = dot(d_logits, w_two[...], 1, 1).astype(BF)

    moved = [w_twos[0], active, *w_twos[1:]]
    return pl.pallas_call(
        kernel,
        out_shape=[
            jax.ShapeDtypeStruct((half, units + classes), F32),
            jax.ShapeDtypeStruct((half, units + classes), BF),
            jax.ShapeDtypeStruct((targets, classes), BF),
        ]
        + [jax.ShapeDtypeStruct((targets, units), BF)] * (count - 1),
        in_specs=[SMEM] + [VMEM] * (count + 4 + len(moved)),
        out_specs=[VMEM] * (2 + count),
        compiler_params=pltpu.CompilerParams(vmem_limit_bytes=24 * 2**20),
        cost_estimate=pl.CostEstimate(
            flops=2 * targets * classes * units * (count + 1),
            bytes_accessed=4 * 2**20,
            transcendentals=targets * classes,
        ),
    )(core, *parts, labels, hidden, spread_t, rows_t, *moved)


def forward(rows, w_ones, w_twos, spread):
    slots, width_f = rows.shape
    targets = spread.shape[0]
    units, classes = w_twos[0].shape
    count = len(w_ones)

    def kernel(rows_ref, spread_ref, *refs):
        w_refs, refs = refs[: 2 * count], refs[2 * count :]
        active_refs, hidden_refs = refs[:count], refs[count : 2 * count]
        logits_ref, narrow_ref = refs[2 * count : 2 * count + 2]
        refs = refs[2 * count + 2 :]
        w_one_all, w_two_all, active_all, spread_all, w_sems, out_sems, sem = refs

        def w_copy(i):
            target = w_one_all.at[i] if i < count else w_two_all.at[i - count]
            return pltpu.make_async_copy(w_refs[i], target, w_sems.at[i])

        for i in range(2 * count):
            w_copy(i).start()
        spread_copy = pltpu.make_async_copy(spread_ref, spread_all, sem)
        spread_copy.start()
        out_copies = [
            pltpu.make_async_copy(active_all.at[i], active_refs[i], out_sems.at[i])
            for i in range(count)
        ]
        spread_copy.wait()
        logits = jnp.zeros((targets, classes), F32)
        for i in range(count):
            w_copy(i).wait()
            active_all[i] = jnp.maximum(dot(rows_ref[...], w_one_all[i]), 0.0).astype(BF)
            out_copies[i].start()
            hidden = dot(spread_all[...], active_all[i]).astype(BF)
            hidden_refs[i][...] = hidden
            w_copy(count + i).wait()
            logits += dot(hidden, w_two_all[i])
        logits_ref[...] = logits
        narrow_ref[...] = logits.astype(BF)
        for copy in out_copies:
            copy.wait()

    w_all = [pltpu.with_memory_space_constraint(x, pltpu.HBM) for x in (*w_ones, *w_twos)]
    return pl.pallas_call(
        kernel,
        out_shape=[pltpu.HBM((slots, units), BF)] * count
        + [jax.ShapeDtypeStruct((targets, units), BF)] * count
        + [
            jax.ShapeDtypeStruct((targets, classes), F32),
            jax.ShapeDtypeStruct((targets, classes), BF),
        ],
        in_specs=[VMEM, HBM] + [HBM] * (2 * count),
        out_specs=[HBM] * count + [VMEM] * (count + 2),
        scratch_shapes=[
            pltpu.VMEM((count, width_f, units), BF),
            pltpu.VMEM((count, units, classes), BF),
            pltpu.VMEM((count, slots, units), BF),
            pltpu.VMEM((targets, slots), BF),
            pltpu.SemaphoreType.DMA((2 * count,)),
            pltpu.SemaphoreType.DMA((count,)),
            pltpu.SemaphoreType.DMA,
        ],
        compiler_params=pltpu.CompilerParams(vmem_limit_bytes=32 * 2**20),
        cost_estimate=pl.CostEstimate(
            flops=2 * count * slots * units * (width_f + targets),
            bytes_accessed=2 * slots * (width_f + units + targets),
            transcendentals=0,
        ),
    )(rows, pltpu.with_memory_space_constraint(spread, pltpu.HBM), *w_all)


def prepare(rows, core, moved):
    slots, width_f = rows.shape
    half = width_f // 2
    block = 512
    count = len(moved)

    def kernel(core_ref, rows_ref, *refs):
        sources, turned = refs[:count], refs[count]
        targets, sems = refs[count + 1 : -1], refs[-1]
        copies = [
            pltpu.make_async_copy(source, target, sems.at[i])
            for i, (source, target) in enumerate(zip(sources, targets))
        ]
        for copy in copies:
            copy.start()
        mine = pl.multiple_of(core_ref[0] * half, half)
        other = pl.multiple_of((1 - core_ref[0]) * half, half)

        @pl.loop(0, slots // block)
        def _(j):
            at = pl.ds(pl.multiple_of(j * block, block), block)
            flat = rows_ref[at, :].T
            turned[pl.ds(mine, half), at] = flat[:half]
            turned[pl.ds(other, half), at] = flat[half:]

        for copy in copies:
            copy.wait()

    moved = [pltpu.with_memory_space_constraint(x, pltpu.HBM) for x in moved]
    return pl.pallas_call(
        kernel,
        out_shape=[jax.ShapeDtypeStruct((width_f, slots), BF)]
        + [jax.ShapeDtypeStruct(x.shape, BF) for x in moved],
        in_specs=[SMEM, VMEM] + [HBM] * count,
        out_specs=[VMEM] * (1 + count),
        scratch_shapes=[pltpu.SemaphoreType.DMA((count,))],
        compiler_params=pltpu.CompilerParams(vmem_limit_bytes=24 * 2**20),
        cost_estimate=pl.CostEstimate(
            flops=2 * slots * width_f * width_f,
            bytes_accessed=8 * slots * width_f,
            transcendentals=0,
        ),
    )(core, rows, *moved)


def backward(core, spread_t, d_hidden, active, rows_t, hidden, d_logits, earlier):
    units = d_hidden.shape[1]
    half = rows_t.shape[0] // 2
    width = units + d_logits.shape[1]

    def kernel(core_ref, spread_ref, d_hidden_ref, active_ref, rows_ref, hidden_ref, logits_ref, *refs):
        slice_grad(
            core_ref[0],
            spread_ref,
            d_hidden_ref[...],
            active_ref,
            rows_ref,
            hidden_ref,
            logits_ref[...],
            *refs[-2:],
        )

    return pl.pallas_call(
        kernel,
        out_shape=[
            jax.ShapeDtypeStruct((half, width), F32),
            jax.ShapeDtypeStruct((half, width), BF),
        ],
        in_specs=[SMEM] + [VMEM] * 6 + [pl.BlockSpec(memory_space=pl.ANY)] * len(earlier),
        out_specs=[VMEM] * 2,
        compiler_params=pltpu.CompilerParams(vmem_limit_bytes=24 * 2**20),
        cost_estimate=pl.CostEstimate(
            flops=2 * units, bytes_accessed=2 * units, transcendentals=0
        ),
    )(core, spread_t, d_hidden, active, rows_t, hidden, d_logits, *earlier)


def outputs(own, other, core, units):
    half, width = own.shape

    def kernel(core_ref, own_ref, other_ref, one_ref, two_ref, wide, sems):
        copies = []
        for i, ref in enumerate((own_ref, other_ref)):
            wide[i] = ref[...].astype(F32)
            place = core_ref[0] if i == 0 else 1 - core_ref[0]
            at = pl.ds(pl.multiple_of(place * half, half), half)
            for j, (out, first) in enumerate(((one_ref, 0), (two_ref, units))):
                source = wide.at[i, :, pl.ds(first, out.shape[1])]
                copies.append(pltpu.make_async_copy(source, out.at[at, :], sems.at[2 * i + j]))
                copies[-1].start()
        for copy in copies:
            copy.wait()

    return pl.pallas_call(
        kernel,
        out_shape=[pltpu.HBM((2 * half, units), F32), pltpu.HBM((2 * half, width - units), F32)],
        in_specs=[SMEM, VMEM, VMEM],
        out_specs=[HBM, HBM],
        scratch_shapes=[pltpu.VMEM((2, half, width), F32), pltpu.SemaphoreType.DMA((4,))],
        compiler_params=pltpu.CompilerParams(vmem_limit_bytes=24 * 2**20),
    )(core, own, other)


def body(features, nbr_page, nbr_weight, labels, w_one, w_two):
    rows_dev, width_f = features.shape
    targets, width_k = nbr_page.shape
    own_n, col_n, mlp_n = (lax.axis_size(a) for a in ("own", "col", "mlp"))
    owners = own_n * col_n
    entries = targets * width_k
    capacity = 2 * entries // owners
    share = capacity // mlp_n
    units, classes = w_two.shape
    me = lax.axis_index("mlp")
    core = lax.axis_index("col") % 2

    def to_mlp(x, step):
        return lax.ppermute(x, "mlp", [(j, (j + step) % mlp_n) for j in range(mlp_n)])

    steps = (2, 1, 3, 0)
    w_ones, w_twos = {0: w_one}, {0: w_two}
    for step in steps[:-1]:
        w_ones[step] = to_mlp(w_one, -step)
        w_twos[step] = to_mlp(w_two, -step)
    w_ones, w_twos = lax.optimization_barrier((w_ones, w_twos))

    requests, slot_ids = slots_of(nbr_page.T, rows_dev, owners, capacity)
    asked = exchange(requests, ("own", "col"))
    asked = lax.dynamic_slice_in_dim(asked, me * share, share, 1).reshape(-1)
    fetched = gather(features, asked)
    fetched = fetched.reshape(owners, share, width_f)
    received = exchange(fetched, ("own", "col")).reshape(owners * share, width_f)

    slot_ids = slot_ids.T
    owner_range = jnp.arange(owners, dtype=jnp.int32)
    t_range = jnp.arange(targets)
    matches = (nbr_page // rows_dev)[:, :, None] == owner_range[None, None, :]
    by_owner = matches.astype(BF).reshape(entries, owners)
    in_slot = slot_ids[:, :, None] == jnp.arange(capacity, dtype=jnp.int32)[None, None, :]

    def place(values):
        spread_out = jnp.where(in_slot, values.astype(BF)[:, :, None], jnp.zeros((), BF))
        return dot(by_owner, spread_out.reshape(entries, capacity), 0, 0)

    slot_weight = place(nbr_weight)
    slot_target = place(jnp.broadcast_to(t_range[:, None], (targets, width_k)))

    my_weight = lax.dynamic_slice_in_dim(slot_weight, me * share, share, 1).reshape(1, -1)
    my_target = lax.dynamic_slice_in_dim(slot_target, me * share, share, 1).reshape(1, -1)
    spread = jnp.where(
        my_target.astype(jnp.int32) == t_range[:, None].astype(jnp.int32), my_weight, 0.0
    ).astype(BF)
    spread, spread_t = lax.optimization_barrier((spread, spread.T))

    core_id = core.reshape(1)
    half = width_f // 2
    out = forward(
        received, [w_ones[s] for s in steps], [w_twos[s] for s in steps], spread
    )
    active, hidden = dict(zip(steps, out)), dict(zip(steps, out[mlp_n:]))
    part, narrow = out[2 * mlp_n :]
    parts = [part] + [to_mlp(narrow, step) for step in steps[:-1]]

    rows_t, first_active, *near_twos = prepare(
        received, core_id, [active[2]] + [w_twos[s] for s in steps]
    )

    pairs = [(i, i ^ 1) for i in range(col_n)]

    def partner(x):
        return lax.ppermute(x, "col", pairs)

    mine, other, d_logits, *d_hidden = middle(
        parts,
        labels[None],
        hidden[2],
        near_twos,
        core_id,
        spread_t,
        first_active,
        rows_t,
    )
    far = (mine + partner(other).astype(F32)).astype(BF)
    far = (far[: half // 2], far[half // 2 :])
    upward, downward = to_mlp(far[0], 1), to_mlp(far[1], -1)

    def slice_sum(step, earlier):
        mine, other = backward(
            core_id,
            spread_t,
            d_hidden[steps.index(step) - 1],
            active[step],
            rows_t,
            hidden[step],
            d_logits,
            earlier,
        )
        return mine + partner(other).astype(F32)

    below = slice_sum(3, ())
    above = slice_sum(1, far)
    top, bottom = above[: half // 2], above[half // 2 :]
    above = jnp.concatenate([top + upward.astype(F32), bottom], axis=0).astype(BF)
    top, bottom = below[: half // 2], below[half // 2 :]
    below = jnp.concatenate([top, bottom + downward.astype(F32)], axis=0).astype(BF)
    both = slice_sum(0, (above, below))
    both += to_mlp(above, 1).astype(F32) + to_mlp(below, -1).astype(F32)
    both = both.astype(BF)
    chips = owners // 2
    groups = [[2 * i + c for i in range(chips)] for c in (0, 1)]
    width = units + classes
    both = exchange(both.reshape(chips, half // chips, width), ("own", "col"), groups)
    both = jnp.sum(both.astype(F32), axis=0).astype(BF)
    both = jnp.broadcast_to(both[None], (chips, half // chips, width))
    both = exchange(both, ("own", "col"), groups).reshape(half, width)
    other = partner(both)
    return tuple(outputs(both, other, core_id, units))


def solution(mesh):
    placed = (
        P(("own", "col"), None),
        P(("own", "col"), None),
        P(("own", "col"), None),
        P(("own", "col")),
        P(None, "mlp"),
        P("mlp", None),
    )
    return jax.shard_map(
        body,
        mesh=mesh,
        in_specs=placed,
        out_specs=(P(None, "mlp"), P("mlp", None)),
        check_vma=False,
    )
```

```python
import jax
import jax.numpy as jnp
from jax import lax
from jax.experimental import pallas as pl
from jax.experimental.pallas import tpu as pltpu
from jax.sharding import PartitionSpec as P

BF = jnp.bfloat16
F32 = jnp.float32


def dot(a, b, ca=1, cb=0):
    return lax.dot_general(a, b, (((ca,), (cb,)), ((), ())), preferred_element_type=F32)


def exchange(x, axes, groups=None):
    return lax.all_to_all(
        x, axes, split_axis=0, concat_axis=0, tiled=True, axis_index_groups=groups
    )


VMEM = pl.BlockSpec(memory_space=pltpu.VMEM)
SMEM = pl.BlockSpec(memory_space=pltpu.SMEM)
HBM = pl.BlockSpec(memory_space=pltpu.HBM)


def slots_of(page_t, rows_dev, owners, capacity):
    width_k, targets = page_t.shape
    shift = rows_dev.bit_length() - 1
    low_bits = 6
    low_mask = (1 << low_bits) - 1

    def kernel(page_ref, request_ref, slot_ref, lhs, rhs):
        page = page_ref[...]
        owner = lax.shift_right_logical(page, jnp.int32(shift))
        row = page & (rows_dev - 1)
        high = lax.shift_right_logical(row, jnp.int32(low_bits)).astype(F32)
        low = (row & low_mask).astype(F32)
        owner_id = lax.broadcasted_iota(jnp.int32, (owners, targets), 0)
        count = jnp.zeros((owners, targets), F32)
        for k in range(width_k):
            match = (owner[k : k + 1] == owner_id).astype(F32)
            count += match
            lhs[:, k * targets : (k + 1) * targets] = match.astype(BF)
        count = count.astype(BF)

        def before(size):
            first = lax.broadcasted_iota(jnp.int32, (size, size), 0)
            return first, lax.broadcasted_iota(jnp.int32, (size, size), 1)

        first, second = before(targets)
        earlier = dot(count, (first < second).astype(F32).astype(BF))
        first, second = before(owners)
        smaller = dot((second < first).astype(F32).astype(BF), count)
        start = earlier - smaller
        slot_id = lax.broadcasted_iota(jnp.int32, (capacity, targets), 0)
        for k in range(width_k):
            mine = jnp.where(owner[k : k + 1] == owner_id, start, 0.0)
            slot = jnp.sum(mine, axis=0, keepdims=True).astype(jnp.int32) + k
            slot_ref[k : k + 1] = slot
            hit = slot == slot_id
            at = slice(k * targets, (k + 1) * targets)
            rhs[:capacity, at] = jnp.where(hit, high[k : k + 1], 0.0).astype(BF)
            rhs[capacity:, at] = jnp.where(hit, low[k : k + 1], 0.0).astype(BF)
        both = dot(lhs[...], rhs[...], 1, 1)
        request = both[:, :capacity] * float(1 << low_bits) + both[:, capacity:]
        request_ref[...] = request.astype(jnp.int32)

    entries = width_k * targets
    return pl.pallas_call(
        kernel,
        out_shape=[
            jax.ShapeDtypeStruct((owners, capacity), jnp.int32),
            jax.ShapeDtypeStruct((width_k, targets), jnp.int32),
        ],
        in_specs=[VMEM],
        out_specs=[VMEM] * 2,
        scratch_shapes=[
            pltpu.VMEM((owners, entries), BF),
            pltpu.VMEM((2 * capacity, entries), BF),
        ],
        compiler_params=pltpu.CompilerParams(vmem_limit_bytes=24 * 2**20),
    )(page_t)


def gather(features, asked):
    rows_dev, width_f = features.shape
    (count,) = asked.shape
    group = 32
    parts = 4
    chunk = 512
    chunks = rows_dev // chunk

    def kernel(asked_ref, features_ref, out_ref, wide, narrow, out, sems, out_sems):
        copies = []
        for i in range(chunks):
            at = pl.ds(i * chunk, chunk)
            copies.append(
                pltpu.make_async_copy(features_ref.at[at, :], narrow.at[at, :], sems.at[i])
            )
        for copy in copies:
            copy.start()
        for i, copy in enumerate(copies):
            copy.wait()
            at = pl.ds(i * chunk, chunk)
            wide[at, :] = narrow[at, :].astype(F32)

        copies = []
        part = count // parts
        for p in range(parts):

            @pl.loop(0, part // group)
            def _(i, p=p):
                base = pl.multiple_of(p * part + i * group, group)
                rows = [wide[pl.ds(asked_ref[base + j], 1), :] for j in range(group)]
                out[pl.ds(base, group), :] = jnp.concatenate(rows, axis=0).astype(BF)

            at = pl.ds(p * part, part)
            copies.append(pltpu.make_async_copy(out.at[at, :], out_ref.at[at, :], out_sems.at[p]))
            copies[-1].start()
        for copy in copies:
            copy.wait()

    return pl.pallas_call(
        kernel,
        out_shape=pltpu.HBM((count, width_f), BF),
        in_specs=[SMEM, HBM],
        out_specs=HBM,
        scratch_shapes=[
            pltpu.VMEM((rows_dev, width_f), F32),
            pltpu.VMEM((rows_dev, width_f), BF),
            pltpu.VMEM((count, width_f), BF),
            pltpu.SemaphoreType.DMA((chunks,)),
            pltpu.SemaphoreType.DMA((parts,)),
        ],
        compiler_params=pltpu.CompilerParams(vmem_limit_bytes=32 * 2**20),
    )(asked, pltpu.with_memory_space_constraint(features, pltpu.HBM))


def slice_grad(
    core, spread, d_hidden, active, rows, hidden, d_logits, own_ref, other_ref, waits=(None,) * 3
):
    def arrived(i):
        if waits[i] is not None:
            waits[i].wait()

    half = own_ref.shape[0]
    units = d_hidden.shape[1]
    mine = hidden[:, pl.ds(pl.multiple_of(core * half, half), half)]
    other = hidden[:, pl.ds(pl.multiple_of((1 - core) * half, half), half)]
    own_ref[:, units:] = dot(mine, d_logits, 0, 0)
    other_ref[:, units:] = dot(other, d_logits, 0, 0).astype(BF)
    arrived(0)
    scattered = dot(spread[...], d_hidden).astype(BF)
    arrived(1)
    d_pre = jnp.where(active[...] > 0, scattered, jnp.zeros_like(scattered))
    arrived(2)
    total = dot(rows[...], d_pre)
    own_ref[:, :units] = total[:half]
    other_ref[:, :units] = total[half:].astype(BF)


def middle(parts, labels, hidden, w_twos, core, spread_t, active, rows_t):
    count = len(parts)
    targets, classes = parts[0].shape
    units = hidden.shape[1]
    half = units // 2

    def kernel(core_ref, *refs):
        part_refs, refs = refs[:count], refs[count:]
        labels_ref, hidden_ref = refs[:2]
        spread_ref, rows_ref = refs[2:4]
        sources, refs = refs[4 : 5 + count], refs[5 + count :]
        own_ref, other_ref, d_logits_ref = refs[:3]
        d_hidden_refs = refs[3 : 2 + count]
        logits = part_refs[0][...]
        for part in part_refs[1:]:
            logits += part[...].astype(F32)
        exponent = jnp.exp(logits)
        probability = exponent / jnp.sum(exponent, axis=1, keepdims=True)
        ids = lax.broadcasted_iota(jnp.int32, (targets, classes), 1)
        label = jnp.broadcast_to(labels_ref[...], (targets, targets)).T[:, :1]
        d_logits = (probability - (label == ids).astype(F32)).astype(BF)
        d_logits_ref[...] = d_logits
        d_first = dot(d_logits, sources[0][...], 1, 1).astype(BF)
        slice_grad(
            core_ref[0],
            spread_ref,
            d_first,
            sources[1],
            rows_ref,
            hidden_ref,
            d_logits,
            own_ref,
            other_ref,
        )
        for w_two, out in zip(sources[2:], d_hidden_refs):
            out[...] = dot(d_logits, w_two[...], 1, 1).astype(BF)

    moved = [w_twos[0], active, *w_twos[1:]]
    return pl.pallas_call(
        kernel,
        out_shape=[
            jax.ShapeDtypeStruct((half, units + classes), F32),
            jax.ShapeDtypeStruct((half, units + classes), BF),
            jax.ShapeDtypeStruct((targets, classes), BF),
        ]
        + [jax.ShapeDtypeStruct((targets, units), BF)] * (count - 1),
        in_specs=[SMEM] + [VMEM] * (count + 4 + len(moved)),
        out_specs=[VMEM] * (2 + count),
        compiler_params=pltpu.CompilerParams(vmem_limit_bytes=24 * 2**20),
        cost_estimate=pl.CostEstimate(
            flops=2 * targets * classes * units * (count + 1),
            bytes_accessed=4 * 2**20,
            transcendentals=targets * classes,
        ),
    )(core, *parts, labels, hidden, spread_t, rows_t, *moved)


def forward(rows, w_ones, w_twos, spread):
    slots, width_f = rows.shape
    targets = spread.shape[0]
    units, classes = w_twos[0].shape
    count = len(w_ones)

    def kernel(rows_ref, spread_ref, *refs):
        w_refs, refs = refs[: 2 * count], refs[2 * count :]
        active_refs, hidden_refs = refs[:count], refs[count : 2 * count]
        logits_ref, narrow_ref = refs[2 * count : 2 * count + 2]
        refs = refs[2 * count + 2 :]
        w_one_all, w_two_all, active_all, spread_all, w_sems, out_sems, sem = refs

        def w_copy(i):
            target = w_one_all.at[i] if i < count else w_two_all.at[i - count]
            return pltpu.make_async_copy(w_refs[i], target, w_sems.at[i])

        for i in range(2 * count):
            w_copy(i).start()
        spread_copy = pltpu.make_async_copy(spread_ref, spread_all, sem)
        spread_copy.start()
        out_copies = [
            pltpu.make_async_copy(active_all.at[i], active_refs[i], out_sems.at[i])
            for i in range(count)
        ]
        spread_copy.wait()
        logits = jnp.zeros((targets, classes), F32)
        for i in range(count):
            w_copy(i).wait()
            active_all[i] = jnp.maximum(dot(rows_ref[...], w_one_all[i]), 0.0).astype(BF)
            out_copies[i].start()
            hidden = dot(spread_all[...], active_all[i]).astype(BF)
            hidden_refs[i][...] = hidden
            w_copy(count + i).wait()
            logits += dot(hidden, w_two_all[i])
        logits_ref[...] = logits
        narrow_ref[...] = logits.astype(BF)
        for copy in out_copies:
            copy.wait()

    w_all = [pltpu.with_memory_space_constraint(x, pltpu.HBM) for x in (*w_ones, *w_twos)]
    return pl.pallas_call(
        kernel,
        out_shape=[pltpu.HBM((slots, units), BF)] * count
        + [jax.ShapeDtypeStruct((targets, units), BF)] * count
        + [
            jax.ShapeDtypeStruct((targets, classes), F32),
            jax.ShapeDtypeStruct((targets, classes), BF),
        ],
        in_specs=[VMEM, HBM] + [HBM] * (2 * count),
        out_specs=[HBM] * count + [VMEM] * (count + 2),
        scratch_shapes=[
            pltpu.VMEM((count, width_f, units), BF),
            pltpu.VMEM((count, units, classes), BF),
            pltpu.VMEM((count, slots, units), BF),
            pltpu.VMEM((targets, slots), BF),
            pltpu.SemaphoreType.DMA((2 * count,)),
            pltpu.SemaphoreType.DMA((count,)),
            pltpu.SemaphoreType.DMA,
        ],
        compiler_params=pltpu.CompilerParams(vmem_limit_bytes=32 * 2**20),
        cost_estimate=pl.CostEstimate(
            flops=2 * count * slots * units * (width_f + targets),
            bytes_accessed=2 * slots * (width_f + units + targets),
            transcendentals=0,
        ),
    )(rows, pltpu.with_memory_space_constraint(spread, pltpu.HBM), *w_all)


def prepare(rows, core, moved):
    slots, width_f = rows.shape
    half = width_f // 2
    block = 512
    count = len(moved)

    def kernel(core_ref, rows_ref, *refs):
        sources, turned = refs[:count], refs[count]
        targets, sems = refs[count + 1 : -1], refs[-1]
        copies = [
            pltpu.make_async_copy(source, target, sems.at[i])
            for i, (source, target) in enumerate(zip(sources, targets))
        ]
        for copy in copies:
            copy.start()
        mine = pl.multiple_of(core_ref[0] * half, half)
        other = pl.multiple_of((1 - core_ref[0]) * half, half)

        @pl.loop(0, slots // block)
        def _(j):
            at = pl.ds(pl.multiple_of(j * block, block), block)
            flat = rows_ref[at, :].T
            turned[pl.ds(mine, half), at] = flat[:half]
            turned[pl.ds(other, half), at] = flat[half:]

        for copy in copies:
            copy.wait()

    moved = [pltpu.with_memory_space_constraint(x, pltpu.HBM) for x in moved]
    return pl.pallas_call(
        kernel,
        out_shape=[jax.ShapeDtypeStruct((width_f, slots), BF)]
        + [jax.ShapeDtypeStruct(x.shape, BF) for x in moved],
        in_specs=[SMEM, VMEM] + [HBM] * count,
        out_specs=[VMEM] * (1 + count),
        scratch_shapes=[pltpu.SemaphoreType.DMA((count,))],
        compiler_params=pltpu.CompilerParams(vmem_limit_bytes=24 * 2**20),
        cost_estimate=pl.CostEstimate(
            flops=2 * slots * width_f * width_f,
            bytes_accessed=8 * slots * width_f,
            transcendentals=0,
        ),
    )(core, rows, *moved)


def backward(core, spread_t, d_hidden, active, rows_t, hidden, d_logits, earlier):
    units = d_hidden.shape[1]
    half = rows_t.shape[0] // 2
    width = units + d_logits.shape[1]

    def kernel(core_ref, spread_ref, d_hidden_ref, active_ref, rows_ref, hidden_ref, logits_ref, *refs):
        slice_grad(
            core_ref[0],
            spread_ref,
            d_hidden_ref[...],
            active_ref,
            rows_ref,
            hidden_ref,
            logits_ref[...],
            *refs[-2:],
        )

    return pl.pallas_call(
        kernel,
        out_shape=[
            jax.ShapeDtypeStruct((half, width), F32),
            jax.ShapeDtypeStruct((half, width), BF),
        ],
        in_specs=[SMEM] + [VMEM] * 6 + [pl.BlockSpec(memory_space=pl.ANY)] * len(earlier),
        out_specs=[VMEM] * 2,
        compiler_params=pltpu.CompilerParams(vmem_limit_bytes=24 * 2**20),
        cost_estimate=pl.CostEstimate(
            flops=2 * units, bytes_accessed=2 * units, transcendentals=0
        ),
    )(core, spread_t, d_hidden, active, rows_t, hidden, d_logits, *earlier)


def outputs(own, other, core, units):
    half, width = own.shape

    def kernel(core_ref, own_ref, other_ref, one_ref, two_ref, wide, sems):
        copies = []
        for i, ref in enumerate((own_ref, other_ref)):
            wide[i] = ref[...].astype(F32)
            place = core_ref[0] if i == 0 else 1 - core_ref[0]
            at = pl.ds(pl.multiple_of(place * half, half), half)
            for j, (out, first) in enumerate(((one_ref, 0), (two_ref, units))):
                source = wide.at[i, :, pl.ds(first, out.shape[1])]
                copies.append(pltpu.make_async_copy(source, out.at[at, :], sems.at[2 * i + j]))
                copies[-1].start()
        for copy in copies:
            copy.wait()

    return pl.pallas_call(
        kernel,
        out_shape=[pltpu.HBM((2 * half, units), F32), pltpu.HBM((2 * half, width - units), F32)],
        in_specs=[SMEM, VMEM, VMEM],
        out_specs=[HBM, HBM],
        scratch_shapes=[pltpu.VMEM((2, half, width), F32), pltpu.SemaphoreType.DMA((4,))],
        compiler_params=pltpu.CompilerParams(vmem_limit_bytes=24 * 2**20),
    )(core, own, other)


def body(features, nbr_page, nbr_weight, labels, w_one, w_two):
    rows_dev, width_f = features.shape
    targets, width_k = nbr_page.shape
    own_n, col_n, mlp_n = (lax.axis_size(a) for a in ("own", "col", "mlp"))
    owners = own_n * col_n
    entries = targets * width_k
    capacity = 2 * entries // owners
    share = capacity // mlp_n
    units, classes = w_two.shape
    me = lax.axis_index("mlp")
    core = lax.axis_index("col") % 2

    def to_mlp(x, step):
        return lax.ppermute(x, "mlp", [(j, (j + step) % mlp_n) for j in range(mlp_n)])

    steps = (2, 1, 3, 0)
    w_ones, w_twos = {0: w_one}, {0: w_two}
    for step in steps[:-1]:
        w_ones[step] = to_mlp(w_one, -step)
        w_twos[step] = to_mlp(w_two, -step)
    w_ones, w_twos = lax.optimization_barrier((w_ones, w_twos))

    requests, slot_ids = slots_of(nbr_page.T, rows_dev, owners, capacity)
    asked = exchange(requests, ("own", "col"))
    asked = lax.dynamic_slice_in_dim(asked, me * share, share, 1).reshape(-1)
    fetched = gather(features, asked)
    fetched = fetched.reshape(owners, share, width_f)
    received = exchange(fetched, ("own", "col")).reshape(owners * share, width_f)

    slot_ids = slot_ids.T
    owner_range = jnp.arange(owners, dtype=jnp.int32)
    t_range = jnp.arange(targets)
    matches = (nbr_page // rows_dev)[:, :, None] == owner_range[None, None, :]
    by_owner = matches.astype(BF).reshape(entries, owners)
    in_slot = slot_ids[:, :, None] == jnp.arange(capacity, dtype=jnp.int32)[None, None, :]

    def place(values):
        spread_out = jnp.where(in_slot, values.astype(BF)[:, :, None], jnp.zeros((), BF))
        return dot(by_owner, spread_out.reshape(entries, capacity), 0, 0)

    slot_weight = place(nbr_weight)
    slot_target = place(jnp.broadcast_to(t_range[:, None], (targets, width_k)))

    my_weight = lax.dynamic_slice_in_dim(slot_weight, me * share, share, 1).reshape(1, -1)
    my_target = lax.dynamic_slice_in_dim(slot_target, me * share, share, 1).reshape(1, -1)
    spread = jnp.where(
        my_target.astype(jnp.int32) == t_range[:, None].astype(jnp.int32), my_weight, 0.0
    ).astype(BF)
    spread, spread_t = lax.optimization_barrier((spread, spread.T))

    core_id = core.reshape(1)
    half = width_f // 2
    out = forward(
        received, [w_ones[s] for s in steps], [w_twos[s] for s in steps], spread
    )
    active, hidden = dict(zip(steps, out)), dict(zip(steps, out[mlp_n:]))
    part, narrow = out[2 * mlp_n :]
    parts = [part] + [to_mlp(narrow, step) for step in steps[:-1]]

    rows_t, first_active, *near_twos = prepare(
        received, core_id, [active[2]] + [w_twos[s] for s in steps]
    )

    pairs = [(i, i ^ 1) for i in range(col_n)]

    def partner(x):
        return lax.ppermute(x, "col", pairs)

    mine, other, d_logits, *d_hidden = middle(
        parts,
        labels[None],
        hidden[2],
        near_twos,
        core_id,
        spread_t,
        first_active,
        rows_t,
    )
    far = (mine + partner(other).astype(F32)).astype(BF)
    far = (far[: half // 2], far[half // 2 :])
    upward, downward = to_mlp(far[0], 1), to_mlp(far[1], -1)

    def slice_sum(step, earlier):
        mine, other = backward(
            core_id,
            spread_t,
            d_hidden[steps.index(step) - 1],
            active[step],
            rows_t,
            hidden[step],
            d_logits,
            earlier,
        )
        return mine + partner(other).astype(F32)

    below = slice_sum(3, ())
    above = slice_sum(1, far)
    top, bottom = above[: half // 2], above[half // 2 :]
    above = jnp.concatenate([top + upward.astype(F32), bottom], axis=0).astype(BF)
    top, bottom = below[: half // 2], below[half // 2 :]
    below = jnp.concatenate([top, bottom + downward.astype(F32)], axis=0).astype(BF)
    both = slice_sum(0, ())
    both += to_mlp(above, 1).astype(F32) + to_mlp(below, -1).astype(F32)
    both = both.astype(BF)
    chips = owners // 2
    groups = [[2 * i + c for i in range(chips)] for c in (0, 1)]
    width = units + classes
    both = exchange(both.reshape(chips, half // chips, width), ("own", "col"), groups)
    both = jnp.sum(both.astype(F32), axis=0).astype(BF)
    both = jnp.broadcast_to(both[None], (chips, half // chips, width))
    both = exchange(both, ("own", "col"), groups).reshape(half, width)
    other = partner(both)
    return tuple(outputs(both, other, core_id, units))


def solution(mesh):
    placed = (
        P(("own", "col"), None),
        P(("own", "col"), None),
        P(("own", "col"), None),
        P(("own", "col")),
        P(None, "mlp"),
        P("mlp", None),
    )
    return jax.shard_map(
        body,
        mesh=mesh,
        in_specs=placed,
        out_specs=(P(None, "mlp"), P("mlp", None)),
        check_vma=False,
    )
```

```python
import jax
import jax.numpy as jnp
from jax import lax
from jax.experimental import pallas as pl
from jax.experimental.pallas import tpu as pltpu
from jax.sharding import PartitionSpec as P

BF = jnp.bfloat16
F32 = jnp.float32


def dot(a, b, ca=1, cb=0):
    return lax.dot_general(a, b, (((ca,), (cb,)), ((), ())), preferred_element_type=F32)


def exchange(x, axes, groups=None):
    return lax.all_to_all(
        x, axes, split_axis=0, concat_axis=0, tiled=True, axis_index_groups=groups
    )


VMEM = pl.BlockSpec(memory_space=pltpu.VMEM)
SMEM = pl.BlockSpec(memory_space=pltpu.SMEM)
HBM = pl.BlockSpec(memory_space=pltpu.HBM)


def slots_of(page_t, rows_dev, owners, capacity):
    width_k, targets = page_t.shape
    shift = rows_dev.bit_length() - 1
    low_bits = 6
    low_mask = (1 << low_bits) - 1

    def kernel(page_ref, request_ref, slot_ref, lhs, rhs):
        page = page_ref[...]
        owner = lax.shift_right_logical(page, jnp.int32(shift))
        row = page & (rows_dev - 1)
        high = lax.shift_right_logical(row, jnp.int32(low_bits)).astype(F32)
        low = (row & low_mask).astype(F32)
        owner_id = lax.broadcasted_iota(jnp.int32, (owners, targets), 0)
        count = jnp.zeros((owners, targets), F32)
        for k in range(width_k):
            match = (owner[k : k + 1] == owner_id).astype(F32)
            count += match
            lhs[:, k * targets : (k + 1) * targets] = match.astype(BF)
        count = count.astype(BF)

        def before(size):
            first = lax.broadcasted_iota(jnp.int32, (size, size), 0)
            return first, lax.broadcasted_iota(jnp.int32, (size, size), 1)

        first, second = before(targets)
        earlier = dot(count, (first < second).astype(F32).astype(BF))
        first, second = before(owners)
        smaller = dot((second < first).astype(F32).astype(BF), count)
        start = earlier - smaller
        slot_id = lax.broadcasted_iota(jnp.int32, (capacity, targets), 0)
        for k in range(width_k):
            mine = jnp.where(owner[k : k + 1] == owner_id, start, 0.0)
            slot = jnp.sum(mine, axis=0, keepdims=True).astype(jnp.int32) + k
            slot_ref[k : k + 1] = slot
            hit = slot == slot_id
            at = slice(k * targets, (k + 1) * targets)
            rhs[:capacity, at] = jnp.where(hit, high[k : k + 1], 0.0).astype(BF)
            rhs[capacity:, at] = jnp.where(hit, low[k : k + 1], 0.0).astype(BF)
        both = dot(lhs[...], rhs[...], 1, 1)
        request = both[:, :capacity] * float(1 << low_bits) + both[:, capacity:]
        request_ref[...] = request.astype(jnp.int32)

    entries = width_k * targets
    return pl.pallas_call(
        kernel,
        out_shape=[
            jax.ShapeDtypeStruct((owners, capacity), jnp.int32),
            jax.ShapeDtypeStruct((width_k, targets), jnp.int32),
        ],
        in_specs=[VMEM],
        out_specs=[VMEM] * 2,
        scratch_shapes=[
            pltpu.VMEM((owners, entries), BF),
            pltpu.VMEM((2 * capacity, entries), BF),
        ],
        compiler_params=pltpu.CompilerParams(vmem_limit_bytes=24 * 2**20),
    )(page_t)


def gather(features, asked):
    rows_dev, width_f = features.shape
    (count,) = asked.shape
    group = 32
    parts = 4
    chunk = 512
    chunks = rows_dev // chunk

    def kernel(asked_ref, features_ref, out_ref, wide, narrow, out, sems, out_sems):
        copies = []
        for i in range(chunks):
            at = pl.ds(i * chunk, chunk)
            copies.append(
                pltpu.make_async_copy(features_ref.at[at, :], narrow.at[at, :], sems.at[i])
            )
        for copy in copies:
            copy.start()
        for i, copy in enumerate(copies):
            copy.wait()
            at = pl.ds(i * chunk, chunk)
            wide[at, :] = narrow[at, :].astype(F32)

        copies = []
        part = count // parts
        for p in range(parts):

            @pl.loop(0, part // group)
            def _(i, p=p):
                base = pl.multiple_of(p * part + i * group, group)
                rows = [wide[pl.ds(asked_ref[base + j], 1), :] for j in range(group)]
                out[pl.ds(base, group), :] = jnp.concatenate(rows, axis=0).astype(BF)

            at = pl.ds(p * part, part)
            copies.append(pltpu.make_async_copy(out.at[at, :], out_ref.at[at, :], out_sems.at[p]))
            copies[-1].start()
        for copy in copies:
            copy.wait()

    return pl.pallas_call(
        kernel,
        out_shape=pltpu.HBM((count, width_f), BF),
        in_specs=[SMEM, HBM],
        out_specs=HBM,
        scratch_shapes=[
            pltpu.VMEM((rows_dev, width_f), F32),
            pltpu.VMEM((rows_dev, width_f), BF),
            pltpu.VMEM((count, width_f), BF),
            pltpu.SemaphoreType.DMA((chunks,)),
            pltpu.SemaphoreType.DMA((parts,)),
        ],
        compiler_params=pltpu.CompilerParams(vmem_limit_bytes=32 * 2**20),
    )(asked, pltpu.with_memory_space_constraint(features, pltpu.HBM))


def slice_grad(
    core, spread, d_hidden, active, rows, hidden, d_logits, own_ref, other_ref, waits=(None,) * 3
):
    def arrived(i):
        if waits[i] is not None:
            waits[i].wait()

    half = own_ref.shape[0]
    units = d_hidden.shape[1]
    mine = hidden[:, pl.ds(pl.multiple_of(core * half, half), half)]
    other = hidden[:, pl.ds(pl.multiple_of((1 - core) * half, half), half)]
    own_ref[:, units:] = dot(mine, d_logits, 0, 0)
    other_ref[:, units:] = dot(other, d_logits, 0, 0).astype(BF)
    arrived(0)
    scattered = dot(spread[...], d_hidden).astype(BF)
    arrived(1)
    d_pre = jnp.where(active[...] > 0, scattered, jnp.zeros_like(scattered))
    arrived(2)
    total = dot(rows[...], d_pre)
    own_ref[:, :units] = total[:half]
    other_ref[:, :units] = total[half:].astype(BF)


def middle(parts, labels, hidden, w_twos, core, spread_t, active, rows_t):
    count = len(parts)
    targets, classes = parts[0].shape
    units = hidden.shape[1]
    half = units // 2

    def kernel(core_ref, *refs):
        part_refs, refs = refs[:count], refs[count:]
        labels_ref, hidden_ref = refs[:2]
        spread_ref, rows_ref = refs[2:4]
        sources, refs = refs[4 : 5 + count], refs[5 + count :]
        own_ref, other_ref, d_logits_ref = refs[:3]
        d_hidden_refs = refs[3 : 2 + count]
        logits = part_refs[0][...]
        for part in part_refs[1:]:
            logits += part[...].astype(F32)
        exponent = jnp.exp(logits)
        probability = exponent / jnp.sum(exponent, axis=1, keepdims=True)
        ids = lax.broadcasted_iota(jnp.int32, (targets, classes), 1)
        label = jnp.broadcast_to(labels_ref[...], (targets, targets)).T[:, :1]
        d_logits = (probability - (label == ids).astype(F32)).astype(BF)
        d_logits_ref[...] = d_logits
        d_first = dot(d_logits, sources[0][...], 1, 1).astype(BF)
        slice_grad(
            core_ref[0],
            spread_ref,
            d_first,
            sources[1],
            rows_ref,
            hidden_ref,
            d_logits,
            own_ref,
            other_ref,
        )
        for w_two, out in zip(sources[2:], d_hidden_refs):
            out[...] = dot(d_logits, w_two[...], 1, 1).astype(BF)

    moved = [w_twos[0], active, *w_twos[1:]]
    return pl.pallas_call(
        kernel,
        out_shape=[
            jax.ShapeDtypeStruct((half, units + classes), F32),
            jax.ShapeDtypeStruct((half, units + classes), BF),
            jax.ShapeDtypeStruct((targets, classes), BF),
        ]
        + [jax.ShapeDtypeStruct((targets, units), BF)] * (count - 1),
        in_specs=[SMEM] + [VMEM] * (count + 4 + len(moved)),
        out_specs=[VMEM] * (2 + count),
        compiler_params=pltpu.CompilerParams(vmem_limit_bytes=24 * 2**20),
        cost_estimate=pl.CostEstimate(
            flops=2 * targets * classes * units * (count + 1),
            bytes_accessed=4 * 2**20,
            transcendentals=targets * classes,
        ),
    )(core, *parts, labels, hidden, spread_t, rows_t, *moved)


def forward(rows, w_ones, w_twos, spread):
    slots, width_f = rows.shape
    targets = spread.shape[0]
    units, classes = w_twos[0].shape
    count = len(w_ones)

    def kernel(rows_ref, spread_ref, *refs):
        w_refs, refs = refs[: 2 * count], refs[2 * count :]
        active_refs, hidden_refs = refs[:count], refs[count : 2 * count]
        logits_ref, narrow_ref = refs[2 * count : 2 * count + 2]
        refs = refs[2 * count + 2 :]
        w_one_all, w_two_all, active_all, spread_all, w_sems, out_sems, sem = refs

        def w_copy(i):
            target = w_one_all.at[i] if i < count else w_two_all.at[i - count]
            return pltpu.make_async_copy(w_refs[i], target, w_sems.at[i])

        for i in range(2 * count):
            w_copy(i).start()
        spread_copy = pltpu.make_async_copy(spread_ref, spread_all, sem)
        spread_copy.start()
        out_copies = [
            pltpu.make_async_copy(active_all.at[i], active_refs[i], out_sems.at[i])
            for i in range(count)
        ]
        spread_copy.wait()
        logits = jnp.zeros((targets, classes), F32)
        for i in range(count):
            w_copy(i).wait()
            active_all[i] = jnp.maximum(dot(rows_ref[...], w_one_all[i]), 0.0).astype(BF)
            out_copies[i].start()
            hidden = dot(spread_all[...], active_all[i]).astype(BF)
            hidden_refs[i][...] = hidden
            w_copy(count + i).wait()
            logits += dot(hidden, w_two_all[i])
        logits_ref[...] = logits
        narrow_ref[...] = logits.astype(BF)
        for copy in out_copies:
            copy.wait()

    w_all = [pltpu.with_memory_space_constraint(x, pltpu.HBM) for x in (*w_ones, *w_twos)]
    return pl.pallas_call(
        kernel,
        out_shape=[pltpu.HBM((slots, units), BF)] * count
        + [jax.ShapeDtypeStruct((targets, units), BF)] * count
        + [
            jax.ShapeDtypeStruct((targets, classes), F32),
            jax.ShapeDtypeStruct((targets, classes), BF),
        ],
        in_specs=[VMEM, HBM] + [HBM] * (2 * count),
        out_specs=[HBM] * count + [VMEM] * (count + 2),
        scratch_shapes=[
            pltpu.VMEM((count, width_f, units), BF),
            pltpu.VMEM((count, units, classes), BF),
            pltpu.VMEM((count, slots, units), BF),
            pltpu.VMEM((targets, slots), BF),
            pltpu.SemaphoreType.DMA((2 * count,)),
            pltpu.SemaphoreType.DMA((count,)),
            pltpu.SemaphoreType.DMA,
        ],
        compiler_params=pltpu.CompilerParams(vmem_limit_bytes=32 * 2**20),
        cost_estimate=pl.CostEstimate(
            flops=2 * count * slots * units * (width_f + targets),
            bytes_accessed=2 * slots * (width_f + units + targets),
            transcendentals=0,
        ),
    )(rows, pltpu.with_memory_space_constraint(spread, pltpu.HBM), *w_all)


def prepare(rows, core, moved):
    slots, width_f = rows.shape
    half = width_f // 2
    block = 512
    count = len(moved)

    def kernel(core_ref, rows_ref, *refs):
        sources, turned = refs[:count], refs[count]
        targets, sems = refs[count + 1 : -1], refs[-1]
        copies = [
            pltpu.make_async_copy(source, target, sems.at[i])
            for i, (source, target) in enumerate(zip(sources, targets))
        ]
        for copy in copies:
            copy.start()
        mine = pl.multiple_of(core_ref[0] * half, half)
        other = pl.multiple_of((1 - core_ref[0]) * half, half)

        @pl.loop(0, slots // block)
        def _(j):
            at = pl.ds(pl.multiple_of(j * block, block), block)
            flat = rows_ref[at, :].T
            turned[pl.ds(mine, half), at] = flat[:half]
            turned[pl.ds(other, half), at] = flat[half:]

        for copy in copies:
            copy.wait()

    moved = [pltpu.with_memory_space_constraint(x, pltpu.HBM) for x in moved]
    return pl.pallas_call(
        kernel,
        out_shape=[jax.ShapeDtypeStruct((width_f, slots), BF)]
        + [jax.ShapeDtypeStruct(x.shape, BF) for x in moved],
        in_specs=[SMEM, VMEM] + [HBM] * count,
        out_specs=[VMEM] * (1 + count),
        scratch_shapes=[pltpu.SemaphoreType.DMA((count,))],
        compiler_params=pltpu.CompilerParams(vmem_limit_bytes=24 * 2**20),
        cost_estimate=pl.CostEstimate(
            flops=2 * slots * width_f * width_f,
            bytes_accessed=8 * slots * width_f,
            transcendentals=0,
        ),
    )(core, rows, *moved)


def backward(core, spread_t, d_hidden, active, rows_t, hidden, d_logits, earlier):
    units = d_hidden.shape[1]
    half = rows_t.shape[0] // 2
    width = units + d_logits.shape[1]

    def kernel(core_ref, spread_ref, d_hidden_ref, active_ref, rows_ref, hidden_ref, logits_ref, *refs):
        slice_grad(
            core_ref[0],
            spread_ref,
            d_hidden_ref[...],
            active_ref,
            rows_ref,
            hidden_ref,
            logits_ref[...],
            *refs[-2:],
        )

    return pl.pallas_call(
        kernel,
        out_shape=[
            jax.ShapeDtypeStruct((half, width), F32),
            jax.ShapeDtypeStruct((half, width), BF),
        ],
        in_specs=[SMEM] + [VMEM] * 6 + [pl.BlockSpec(memory_space=pl.ANY)] * len(earlier),
        out_specs=[VMEM] * 2,
        compiler_params=pltpu.CompilerParams(vmem_limit_bytes=24 * 2**20),
        cost_estimate=pl.CostEstimate(
            flops=2 * units, bytes_accessed=2 * units, transcendentals=0
        ),
    )(core, spread_t, d_hidden, active, rows_t, hidden, d_logits, *earlier)


def outputs(own, other, core, units):
    half, width = own.shape

    def kernel(core_ref, own_ref, other_ref, one_ref, two_ref, wide, sems):
        copies = []
        for i, ref in enumerate((own_ref, other_ref)):
            wide[i] = ref[...].astype(F32)
            place = core_ref[0] if i == 0 else 1 - core_ref[0]
            at = pl.ds(pl.multiple_of(place * half, half), half)
            for j, (out, first) in enumerate(((one_ref, 0), (two_ref, units))):
                source = wide.at[i, :, pl.ds(first, out.shape[1])]
                copies.append(pltpu.make_async_copy(source, out.at[at, :], sems.at[2 * i + j]))
                copies[-1].start()
        for copy in copies:
            copy.wait()

    return pl.pallas_call(
        kernel,
        out_shape=[pltpu.HBM((2 * half, units), F32), pltpu.HBM((2 * half, width - units), F32)],
        in_specs=[SMEM, VMEM, VMEM],
        out_specs=[HBM, HBM],
        scratch_shapes=[pltpu.VMEM((2, half, width), F32), pltpu.SemaphoreType.DMA((4,))],
        compiler_params=pltpu.CompilerParams(vmem_limit_bytes=24 * 2**20),
    )(core, own, other)


def body(features, nbr_page, nbr_weight, labels, w_one, w_two):
    rows_dev, width_f = features.shape
    targets, width_k = nbr_page.shape
    own_n, col_n, mlp_n = (lax.axis_size(a) for a in ("own", "col", "mlp"))
    owners = own_n * col_n
    entries = targets * width_k
    capacity = 2 * entries // owners
    share = capacity // mlp_n
    units, classes = w_two.shape
    me = lax.axis_index("mlp")
    core = lax.axis_index("col") % 2

    def to_mlp(x, step):
        return lax.ppermute(x, "mlp", [(j, (j + step) % mlp_n) for j in range(mlp_n)])

    steps = (2, 1, 3, 0)
    w_ones, w_twos = {0: w_one}, {0: w_two}
    for step in steps[:-1]:
        w_ones[step] = to_mlp(w_one, -step)
        w_twos[step] = to_mlp(w_two, -step)
    w_ones, w_twos = lax.optimization_barrier((w_ones, w_twos))

    requests, slot_ids = slots_of(nbr_page.T, rows_dev, owners, capacity)
    asked = exchange(requests, ("own", "col"))
    asked = lax.dynamic_slice_in_dim(asked, me * share, share, 1).reshape(-1)
    fetched = gather(features, asked)
    fetched = fetched.reshape(owners, share, width_f)
    received = exchange(fetched, ("own", "col")).reshape(owners * share, width_f)

    slot_ids = slot_ids.T
    owner_range = jnp.arange(owners, dtype=jnp.int32)
    t_range = jnp.arange(targets)
    matches = (nbr_page // rows_dev)[:, :, None] == owner_range[None, None, :]
    by_owner = matches.astype(BF).reshape(entries, owners)
    in_slot = slot_ids[:, :, None] == jnp.arange(capacity, dtype=jnp.int32)[None, None, :]

    def place(values):
        spread_out = jnp.where(in_slot, values.astype(BF)[:, :, None], jnp.zeros((), BF))
        return dot(by_owner, spread_out.reshape(entries, capacity), 0, 0)

    slot_weight = place(nbr_weight)
    slot_target = place(jnp.broadcast_to(t_range[:, None], (targets, width_k)))

    my_weight = lax.dynamic_slice_in_dim(slot_weight, me * share, share, 1).reshape(1, -1)
    my_target = lax.dynamic_slice_in_dim(slot_target, me * share, share, 1).reshape(1, -1)
    spread = jnp.where(
        my_target.astype(jnp.int32) == t_range[:, None].astype(jnp.int32), my_weight, 0.0
    ).astype(BF)
    spread, spread_t = lax.optimization_barrier((spread, spread.T))

    core_id = core.reshape(1)
    half = width_f // 2
    out = forward(
        received, [w_ones[s] for s in steps], [w_twos[s] for s in steps], spread
    )
    active, hidden = dict(zip(steps, out)), dict(zip(steps, out[mlp_n:]))
    part, narrow = out[2 * mlp_n :]
    parts = [part] + [to_mlp(narrow, step) for step in steps[:-1]]

    rows_t, first_active, *near_twos = prepare(
        received, core_id, [active[2]] + [w_twos[s] for s in steps]
    )

    pairs = [(i, i ^ 1) for i in range(col_n)]

    def partner(x):
        return lax.ppermute(x, "col", pairs)

    mine, other, d_logits, *d_hidden = middle(
        parts,
        labels[None],
        hidden[2],
        near_twos,
        core_id,
        spread_t,
        first_active,
        rows_t,
    )
    far = (mine + partner(other).astype(F32)).astype(BF)
    far = (far[: half // 2], far[half // 2 :])
    upward, downward = to_mlp(far[0], 1), to_mlp(far[1], -1)

    def slice_sum(step, earlier):
        mine, other = backward(
            core_id,
            spread_t,
            d_hidden[steps.index(step) - 1],
            active[step],
            rows_t,
            hidden[step],
            d_logits,
            earlier,
        )
        return mine + partner(other).astype(F32)

    below = slice_sum(3, ())
    above = slice_sum(1, far)
    top, bottom = above[: half // 2], above[half // 2 :]
    above = jnp.concatenate([top + upward.astype(F32), bottom], axis=0).astype(BF)
    top, bottom = below[: half // 2], below[half // 2 :]
    below = jnp.concatenate([top, bottom + downward.astype(F32)], axis=0).astype(BF)
    from_below, from_above = to_mlp(above, 1), to_mlp(below, -1)
    both = slice_sum(0, (from_below,)) + from_below.astype(F32) + from_above.astype(F32)
    both = both.astype(BF)
    chips = owners // 2
    groups = [[2 * i + c for i in range(chips)] for c in (0, 1)]
    width = units + classes
    both = exchange(both.reshape(chips, half // chips, width), ("own", "col"), groups)
    both = jnp.sum(both.astype(F32), axis=0).astype(BF)
    both = jnp.broadcast_to(both[None], (chips, half // chips, width))
    both = exchange(both, ("own", "col"), groups).reshape(half, width)
    other = partner(both)
    return tuple(outputs(both, other, core_id, units))


def solution(mesh):
    placed = (
        P(("own", "col"), None),
        P(("own", "col"), None),
        P(("own", "col"), None),
        P(("own", "col")),
        P(None, "mlp"),
        P("mlp", None),
    )
    return jax.shard_map(
        body,
        mesh=mesh,
        in_specs=placed,
        out_specs=(P(None, "mlp"), P("mlp", None)),
        check_vma=False,
    )
```
